512 devices in a mesh: wide: 32 (over z, core), narrow: 16 (over x, y).
Axes of the slice: x: 4, y: 4, z: 16, core: 2. Of those that a mesh axis runs over, the one named last changes fastest.
Arguments:
- activations: bfloat16 [512, 16384], P(None, 'wide'), may hold values from -6 to 6
- enc_weight: bfloat16 [16384, 16384], P('wide', 'narrow'), may hold values from -0.046875 to 0.046875
- enc_bias: float32 [16384], P('narrow'), may hold values from -4 to 4
- dec_weight: bfloat16 [16384, 16384], P('narrow', 'wide'), may hold values from -0.375 to 0.375
- dec_bias: float32 [16384], P('wide'), may hold values from -4 to 4
- active_ids: int32 [512, 64], replicated, may hold values from 0 to 16383, all different within a row
Outputs:
- dec_grad: bfloat16 [16384, 16384], P('narrow', 'wide')
- latent_grad: float32 [512, 16384], P('wide', 'narrow')
The draws below stay inside these ranges and needn't reach their ends.
Inputs may be any that keep to these rules, and one draw needn't show every extreme that they name: `active_ids`: each row names 64 different latents; every latent is named by some row.
All inputs are finite; a program needn't handle non-finite values.
Results may differ from the reference program's by a relative error of at most 0.0058.
Values may be sent and summed in bfloat16 or wider, within the bound.
No kernel may reach another device: no remote copies, remote signals or barrier semaphores. Data moves between devices by JAX's collectives and lax.ppermute only.
A program may use at most 128 MiB of HBM per device.

```python
import jax
import jax.numpy as jnp
from jax import lax

LAT_DEV = 1024
K = 64
TOKENS = 512
CHANNELS = 16384
GROUPS = 16
LATENTS = 16384


def steps_of(rng, shape, shards, least, top_value):
    loudness = 1.0
    for axis_at, parts in shards:
        heights = jax.random.uniform(jax.random.fold_in(jax.random.fold_in(rng, 6), axis_at), (parts,), jnp.float32, least / len(shards), top_value / len(shards))
        loudness = loudness * jnp.repeat(jnp.exp(heights), shape[axis_at] // parts).reshape((-1,) + (1,) * (len(shape) - 1 - axis_at))
    return loudness


def picks_of(key, rows, amount, top, lift):
    sequence = jax.random.permutation(jax.random.fold_in(key, 1), amount)
    favour = sequence
    for power in range(3):
        favour = favour * favour // amount
    favour = favour * lift // amount
    tickets = jax.random.randint(jax.random.fold_in(key, 2), (rows, amount), 0, 4096) + favour
    sure = jax.random.permutation(jax.random.fold_in(key, 3), rows)[jnp.arange(amount) % rows]
    tickets = jnp.where(jnp.arange(rows)[:, None] == sure[None, :], 1 << 14, tickets)
    merit = tickets * amount + jnp.arange(amount)
    return lax.top_k(merit.astype(jnp.int32), top)[1].astype(jnp.int32)


def normal_values(rng, dims, spread, bound, split=(), kind=jnp.bfloat16):
    array = jax.random.normal(rng, dims, jnp.float32) * spread
    if len(split) > 0:
        array = steps_of(rng, dims, split, -0.22, 0.18) * array
    return jnp.clip(array, min=-bound, max=bound).astype(kind)


def setup_inputs(seed: int = 0) -> dict:
    splits = jax.random.split(jax.random.key(seed), 7)
    return {
        "activations": normal_values(splits[0], (TOKENS, CHANNELS), 1.0, 6.0, ((1, 32),)),
        "enc_weight": normal_values(splits[1], (CHANNELS, LATENTS), CHANNELS ** -0.5, 0.046875, ((0, 32), (1, 16))),
        "enc_bias": normal_values(splits[2], (LATENTS,), 0.3, 4.0, ((0, 16),), jnp.float32),
        "dec_weight": normal_values(splits[3], (LATENTS, CHANNELS), 256 ** -0.5, 0.375, ((0, 16), (1, 32))),
        "dec_bias": normal_values(splits[4], (CHANNELS,), 0.3, 4.0, ((0, 32),), jnp.float32),
        "active_ids": picks_of(splits[5], TOKENS, LATENTS, K, 64),
    }


def reference(activations, enc_weight, enc_bias, dec_weight, dec_bias, active_ids):
    token_count = activations.shape[0]
    preact = jnp.dot(activations, enc_weight, preferred_element_type=jnp.float32) + enc_bias.astype(jnp.float32)
    row_index = jnp.arange(token_count, dtype=jnp.int32)[:, None]
    active_mask = jnp.zeros(preact.shape, jnp.float32).at[row_index, active_ids].set(1.0)
    latents = (active_mask * preact).astype(jnp.bfloat16)
    target = activations.astype(jnp.float32)
    dec_shift = dec_bias.astype(jnp.float32)
    group_list = jnp.arange(GROUPS, dtype=jnp.int32)

    def pieces(group_index):
        first_latent = (group_index * LAT_DEV).astype(jnp.int32)
        latent_cols = lax.dynamic_slice_in_dim(latents, first_latent, LAT_DEV, 1)
        dec_rows = lax.dynamic_slice_in_dim(dec_weight, first_latent, LAT_DEV, 0)
        mask_cols = lax.dynamic_slice_in_dim(active_mask, first_latent, LAT_DEV, 1)
        recon_part = jnp.dot(latent_cols, dec_rows, preferred_element_type=jnp.float32)
        return latent_cols, dec_rows, mask_cols, recon_part

    nothing = jnp.zeros(target.shape, jnp.float32)

    def first_pass(carry, group_index):
        running, summed = carry
        running = running + pieces(group_index)[3]
        return (running, summed + running), None

    (unused_run, summed), unused_out = lax.scan(first_pass, (nothing, nothing), group_list)
    total_recon = summed + GROUPS * dec_shift

    def second_pass(carry, group_index):
        running, before = carry
        latent_cols, dec_rows, mask_cols, recon_part = pieces(group_index)
        running = running + recon_part
        recon_here = dec_shift + running
        remaining = (GROUPS - group_index).astype(jnp.float32)
        suffix = total_recon - before - remaining * target
        errors = (suffix / GROUPS).astype(jnp.bfloat16)
        grad_rows = lax.dot_general(latent_cols, errors, (((0,), (0,)), ((), ())), preferred_element_type=jnp.float32).astype(jnp.bfloat16)
        grad_cols = mask_cols * lax.dot_general(errors, dec_rows, (((1,), (1,)), ((), ())), preferred_element_type=jnp.float32)
        return (running, before + recon_here), (grad_rows, grad_cols)

    unused_carry, (grad_stack, latent_stack) = lax.scan(second_pass, (nothing, nothing), group_list)
    dec_grad = grad_stack.reshape(GROUPS * LAT_DEV, target.shape[1])
    latent_grad = jnp.transpose(latent_stack, (1, 0, 2)).reshape(token_count, GROUPS * LAT_DEV)
    return dec_grad, latent_grad
```

```python
import jax
import jax.numpy as jnp
from jax import lax
from jax.experimental import pallas as pl
from jax.experimental.pallas import tpu as pltpu
from jax.sharding import Mesh
from jax.sharding import PartitionSpec as P

NARROW = ("narrow_0", "narrow_1")
WIDE = ("wide_0", "wide_1")
LANES = 128
HALF = 64
F32 = jnp.float32
BF16 = jnp.bfloat16
LIMIT = 48 * 1024 * 1024


def lookup(rows, lanes):
    return jnp.take_along_axis(rows, lanes, axis=1, mode="promise_in_bounds")


def spread_slots(ids):
    token = lax.broadcasted_iota(jnp.int32, (ids.shape[0], LANES), 0)
    lane = lax.broadcasted_iota(jnp.int32, (ids.shape[0], LANES), 1)
    both = jnp.concatenate([ids, ids], axis=1)
    return jnp.where((token >> 3) & 1 == lane >> 6, both, -1)


def pick_slots(rows, slots):
    low, high = slots & (LANES - 1), slots >> 7
    picked = jnp.zeros(slots.shape, F32)
    for c in range(rows.shape[1] // LANES):
        picked = jnp.where(high == c, lookup(rows[:, c * LANES : (c + 1) * LANES], low), picked)
    picked = picked.reshape(-1, 2, 8, LANES)
    return (picked[:, 0] + picked[:, 1]).reshape(-1, LANES)


def unpack_rows(packed):
    rows = packed.reshape(-1, 1, 8, LANES)
    return jnp.concatenate([rows, rows], axis=1).reshape(-1, LANES)


def slot_lanes(maps, c):
    return (maps[c // 4] >> (8 * (c % 4))) & 255


def place(values, maps, c, shift=None):
    lanes = slot_lanes(maps, c)
    placed = lookup(values, (lanes - 1) & (LANES - 1))
    if shift is not None:
        placed = placed + shift
    return jnp.where(lanes > 0, placed, 0.0)


def encode_kernel(act, weight, slots, out):
    step = 128
    for i in range(act.shape[0] // step):
        rows = pl.ds(i * step, step)
        part = jnp.dot(act[rows, :], weight[...], preferred_element_type=F32)
        out[pl.ds(i * step // 2, step // 2), :] = pick_slots(part, slots[rows, :]).astype(out.dtype)


def maps_kernel(ids_by_slot, out):
    count, tokens = ids_by_slot.shape
    line = lax.broadcasted_iota(jnp.int32, (LANES, LANES), 0)
    token = lax.broadcasted_iota(jnp.int32, (1, LANES), 1)
    half = HALF * ((token >> 3) & 1)
    for i in range(tokens // LANES):
        cols = pl.ds(i * LANES, LANES)

        def body(block_of_eight, maps):
            first = pl.multiple_of(8 * block_of_eight, 8)
            eight = ids_by_slot[pl.ds(first, 8), cols]
            block = eight >> 7
            code = (half + first + 1 + lax.broadcasted_iota(jnp.int32, eight.shape, 0)) << (8 * (block & 3))
            low = eight & (LANES - 1)
            codes = [
                jnp.where((block >= 0) & (block < 4), code, 0),
                jnp.where((block >= 4) & (block < 8), code, 0),
            ]
            for k in range(8):
                hit = line == low[k : k + 1]
                maps = [m | jnp.where(hit, f[k : k + 1], 0) for m, f in zip(maps, codes)]
            return tuple(maps)

        zero = jnp.zeros((LANES, LANES), jnp.int32)
        maps = lax.fori_loop(0, count // 8, body, (zero, zero))
        for m in range(2):
            out[m, cols, :] = maps[m].T


def decode_kernel(packed, maps, bias, weight, latents, rec):
    step = 128
    for i in range(latents.shape[0] // step):
        rows = pl.ds(i * step, step)
        values = unpack_rows(packed[pl.ds(i * step // 2, step // 2), :].astype(F32))
        mine = [maps[0, rows, :], maps[1, rows, :]]
        for c in range(latents.shape[1] // LANES):
            cols = pl.ds(c * LANES, LANES)
            latents[rows, cols] = place(values, mine, c, bias[:, cols]).astype(BF16)
        rec[rows, :] = jnp.dot(latents[rows, :], weight[...], preferred_element_type=F32).astype(rec.dtype)


def mix_kernel(recs, act, bias, out):
    groups = recs.shape[0]
    for r in range(0, recs.shape[1], 8):
        for c in range(0, recs.shape[2], LANES):
            at = (pl.ds(r, 8), pl.ds(c, LANES))
            err = bias[:, pl.ds(c, LANES)] - act[at].astype(F32)
            errs = []
            for g in range(groups):
                err = err + recs[(g, *at)].astype(F32)
                errs.append(err)
            suffix = jnp.zeros_like(err)
            for g in reversed(range(groups)):
                suffix = suffix + errs[g]
                out[(g, *at)] = (suffix * (1.0 / groups)).astype(out.dtype)


def grad_kernel(back, weight, slots, out):
    step = 128
    for i in range(back.shape[0] // step):
        rows = pl.ds(i * step, step)
        part = lax.dot_general(back[rows, :], weight[...], (((1,), (1,)), ((), ())), preferred_element_type=F32)
        out[pl.ds(i * step // 2, step // 2), :] = pick_slots(part, slots[rows, :]).astype(out.dtype)


def own_kernel(pieces, maps, out):
    values = unpack_rows(jnp.sum(pieces[...].astype(F32), axis=0))
    mine = [maps[0], maps[1]]
    for c in range(out.shape[1] // LANES):
        out[:, pl.ds(c * LANES, LANES)] = place(values, mine, c)


def call(kernel, shapes, flops, *args):
    moved = sum(a.size * a.dtype.itemsize for a in (*args, *jax.tree.leaves(shapes)))
    return pl.pallas_call(
        kernel,
        out_shape=shapes,
        compiler_params=pltpu.CompilerParams(vmem_limit_bytes=LIMIT),
        cost_estimate=pl.CostEstimate(flops=flops, bytes_accessed=moved, transcendentals=0),
    )(*args)


def array(shape, dtype):
    return jax.ShapeDtypeStruct(shape, dtype)


def swap(pieces, axes):
    return lax.all_to_all(pieces, axes, 0, 0)


def local(activations, enc_weight, enc_bias, dec_weight, dec_bias, active_ids):
    tokens, channels = activations.shape
    width = enc_weight.shape[1]
    groups, wide = lax.axis_size(NARROW), lax.axis_size(WIDE)
    group = lax.axis_index(NARROW)
    work = 2 * tokens * channels * width
    ids = active_ids - group * width
    slots = spread_slots(ids)
    packed = (tokens // 2, LANES)
    share = (wide, tokens // 2 // wide, LANES)

    partial = call(encode_kernel, array(packed, BF16), work, activations, enc_weight, slots)
    pieces = swap(partial.reshape(share), WIDE)
    maps = call(maps_kernel, array((2, tokens, LANES), jnp.int32), work // 8, ids.T)
    owned = jnp.sum(pieces.astype(F32), axis=0).astype(BF16)
    preact = swap(jnp.broadcast_to(owned[None], share), WIDE).reshape(packed)
    latents, rec = call(
        decode_kernel,
        (array((tokens, width), BF16), array((tokens, channels), BF16)),
        work,
        preact,
        maps,
        enc_bias[None],
        dec_weight,
    )
    rows = tokens // groups
    recs = swap(rec.reshape(groups, rows, channels), NARROW)
    act_rows = lax.dynamic_slice_in_dim(activations, group * rows, rows, 0)
    mixed = call(mix_kernel, array(recs.shape, BF16), 8 * recs.size, recs, act_rows, dec_bias[None])
    back = swap(mixed, NARROW).reshape(tokens, channels)
    grads = call(grad_kernel, array(packed, BF16), work, back, dec_weight, slots)
    parts = swap(grads.reshape(share), WIDE)
    dec_grad = lax.dot_general(
        latents, back, (((0,), (0,)), ((), ())), preferred_element_type=F32
    ).astype(BF16)
    own_rows = tokens // wide
    own_maps = lax.dynamic_slice_in_dim(maps, lax.axis_index(WIDE) * own_rows, own_rows, 1)
    latent_grad = call(own_kernel, array((own_rows, width), F32), 1 << 20, parts, own_maps)
    return dec_grad, latent_grad


def solution(mesh):
    split = Mesh(mesh.devices.reshape(16, 2, 4, 4), ("wide_0", "wide_1", "narrow_0", "narrow_1"))
    return jax.shard_map(
        local,
        mesh=split,
        in_specs=(P(None, WIDE), P(WIDE, NARROW), P(NARROW), P(NARROW, WIDE), P(WIDE), P()),
        out_specs=(P(NARROW, WIDE), P(WIDE, NARROW)),
        check_vma=False,
    )
```

```python
import functools

import jax
import jax.numpy as jnp
from jax import lax
from jax.experimental import pallas as pl
from jax.experimental.pallas import tpu as pltpu
from jax.sharding import Mesh
from jax.sharding import PartitionSpec as P

NARROW = ("narrow_0", "narrow_1")
WIDE = ("wide_0", "wide_1")
LANES = 128
F32 = jnp.float32
BF16 = jnp.bfloat16
LIMIT = 16 * 1024 * 1024


def lookup(rows, lanes):
    return jnp.take_along_axis(rows, lanes, axis=1, mode="promise_in_bounds")


def pick_slots(rows, slots, per):
    low, high = slots & (LANES - 1), slots >> 7
    picked = jnp.zeros(slots.shape, F32)
    for c in range(rows.shape[1] // LANES):
        picked = jnp.where(high == c, lookup(rows[:, c * LANES : (c + 1) * LANES], low), picked)
    picked = picked.reshape(-1, per, 8, LANES)
    total = picked[:, 0]
    for j in range(1, per):
        total = total + picked[:, j]
    return total.reshape(-1, LANES)


def unpack_rows(packed, per):
    rows = packed.reshape(-1, 1, 8, LANES)
    return jnp.concatenate([rows] * per, axis=1).reshape(-1, LANES)


def place(values, maps, c, shift=None):
    lanes = (maps[c // 4] >> (8 * (c % 4))) & 255
    placed = lookup(values, (lanes - 1) & (LANES - 1))
    if shift is not None:
        placed = placed + shift
    return jnp.where(lanes > 0, placed, 0.0)


def fill_kernel(per, width, group, ids, named, slots, most):
    count = LANES // per
    token = lax.broadcasted_iota(jnp.int32, (1, LANES), 1)
    line = lax.broadcasted_iota(jnp.int32, (LANES, LANES), 0)
    place_of = lax.broadcasted_iota(jnp.int32, (count, LANES), 0)
    groups = lax.broadcasted_iota(jnp.int32, (16, LANES), 0)
    shift = width.bit_length() - 1
    needed = jnp.zeros((16, LANES), jnp.int32)
    for i in range(ids.shape[1] // LANES):
        cols = pl.ds(i * LANES, LANES)
        theirs = ids[:, cols]
        within = theirs - group[0] * width
        mine = (within >= 0) & (within < width)
        if count == ids.shape[0]:
            held = jnp.where(mine, within, -1)
        else:
            which = theirs >> shift
            held = jnp.full((count, LANES), -1, jnp.int32)
            taken = jnp.zeros((1, LANES), jnp.int32)
            tally = jnp.zeros((16, LANES), jnp.int32)
            for k in range(ids.shape[0]):
                here = mine[k : k + 1]
                at = jnp.where(here, taken, count)
                held = jnp.where(place_of == at, within[k : k + 1], held)
                taken = taken + jnp.where(here, 1, 0)
                tally = tally + jnp.where(groups == which[k : k + 1], 1, 0)
            needed = jnp.maximum(needed, tally)
        named[:, cols] = held
        spread = jnp.concatenate([held] * per, axis=0)
        spread = jnp.where(line // count == (token >> 3) & (per - 1), spread, -1)
        slots[cols, :] = spread.T
    most[...] = needed


def maps_kernel(per, named, out):
    count, tokens = named.shape
    line = lax.broadcasted_iota(jnp.int32, (LANES, LANES), 0)
    token = lax.broadcasted_iota(jnp.int32, (1, LANES), 1)
    base = count * ((token >> 3) & (per - 1)) + 1
    for i in range(tokens // LANES):
        cols = pl.ds(i * LANES, LANES)

        def body(n, maps):
            first = pl.multiple_of(8 * n, 8)
            eight = named[pl.ds(first, 8), cols]
            block = eight >> 7
            code = (base + first + lax.broadcasted_iota(jnp.int32, eight.shape, 0)) << (8 * (block & 3))
            low = eight & (LANES - 1)
            codes = [
                jnp.where((block >= 0) & (block < 4), code, 0),
                jnp.where((block >= 4) & (block < 8), code, 0),
            ]
            for k in range(8):
                hit = line == low[k : k + 1]
                maps = [m | jnp.where(hit, f[k : k + 1], 0) for m, f in zip(maps, codes)]
            return tuple(maps)

        zero = jnp.zeros((LANES, LANES), jnp.int32)
        maps = lax.fori_loop(0, count // 8, body, (zero, zero))
        for m in range(2):
            out[m, cols, :] = maps[m].T


def encode_kernel(per, act, weight, slots, out):
    step = 128
    for i in range(act.shape[0] // step):
        rows = pl.ds(i * step, step)
        part = jnp.dot(act[rows, :], weight[...], preferred_element_type=F32)
        out[pl.ds(i * step // per, step // per), :] = pick_slots(part, slots[rows, :], per)


def decode_kernel(per, packed, maps, bias, weight, latents, rec):
    step = 128
    for i in range(latents.shape[0] // step):
        rows = pl.ds(i * step, step)
        values = unpack_rows(packed[pl.ds(i * step // per, step // per), :], per)
        mine = [maps[0, rows, :], maps[1, rows, :]]
        for c in range(latents.shape[1] // LANES):
            cols = pl.ds(c * LANES, LANES)
            latents[rows, cols] = place(values, mine, c, bias[:, cols]).astype(BF16)
        rec[rows, :] = jnp.dot(latents[rows, :], weight[...], preferred_element_type=F32).astype(rec.dtype)


def mix_kernel(recs, act, bias, out):
    groups = recs.shape[0]
    for r in range(0, recs.shape[1], 8):
        for c in range(0, recs.shape[2], LANES):
            at = (pl.ds(r, 8), pl.ds(c, LANES))
            err = bias[:, pl.ds(c, LANES)] - act[at].astype(F32)
            errs = []
            for g in range(groups):
                err = err + recs[(g, *at)].astype(F32)
                errs.append(err)
            suffix = jnp.zeros_like(err)
            for g in reversed(range(groups)):
                suffix = suffix + errs[g]
                out[(g, *at)] = (suffix * (1.0 / groups)).astype(out.dtype)


def grad_kernel(per, back, weight, slots, out):
    step = 128
    for i in range(back.shape[0] // step):
        rows = pl.ds(i * step, step)
        part = lax.dot_general(back[rows, :], weight[...], (((1,), (1,)), ((), ())), preferred_element_type=F32)
        packed = pick_slots(part, slots[rows, :], per)
        for owner in range(step // 16):
            block = 2 * owner // per
            out[i * step // 16 + owner] = packed[8 * block : 8 * block + 8]


def own_kernel(pieces, maps, out):
    values = unpack_rows(jnp.sum(pieces[...], axis=0), 2)
    mine = [maps[0], maps[1]]
    for c in range(out.shape[1] // LANES):
        out[:, pl.ds(c * LANES, LANES)] = place(values, mine, c)


def call(kernel, shapes, flops, *args, **params):
    moved = sum(a.size * a.dtype.itemsize for a in (*args, *jax.tree.leaves(shapes)))
    return pl.pallas_call(
        kernel,
        out_shape=shapes,
        compiler_params=pltpu.CompilerParams(vmem_limit_bytes=LIMIT),
        cost_estimate=pl.CostEstimate(flops=flops, bytes_accessed=moved, transcendentals=0),
        **params,
    )(*args)


def array(shape, dtype):
    return jax.ShapeDtypeStruct(shape, dtype)


def swap(pieces, axes):
    return lax.all_to_all(pieces, axes, 0, 0)


def summed_over_wide(partial):
    ring, core = WIDE
    rows = partial.shape[0] // 2
    both = lax.all_gather(partial, core)
    half = lax.dynamic_slice_in_dim(both, lax.axis_index(core) * rows, rows, 1)
    half = (half[0] + half[1]).astype(BF16)
    pieces = swap(jnp.broadcast_to(half[None], (lax.axis_size(ring), *half.shape)), ring)
    return lax.all_gather(jnp.sum(pieces.astype(F32), axis=0), core, tiled=True)


def fill(per, group, ids, width):
    tokens = ids.shape[1]
    in_vmem = pl.BlockSpec(memory_space=pltpu.VMEM)
    return call(
        functools.partial(fill_kernel, per, width),
        (
            array((LANES // per, tokens), jnp.int32),
            array((tokens, LANES), jnp.int32),
            array((16, LANES), jnp.int32),
        ),
        1 << 20,
        group,
        ids,
        in_specs=[pl.BlockSpec(memory_space=pltpu.SMEM), in_vmem],
    )


def step_with(per, activations, enc_weight, enc_bias, dec_weight, dec_bias, named, slots):
    tokens, channels = activations.shape
    width = enc_weight.shape[1]
    groups, wide = lax.axis_size(NARROW), lax.axis_size(WIDE)
    group = lax.axis_index(NARROW)
    work = 2 * tokens * channels * width

    partial = call(
        functools.partial(encode_kernel, per),
        array((tokens // per, LANES), F32),
        work,
        activations,
        enc_weight,
        slots,
    )
    maps = call(functools.partial(maps_kernel, per), array((2, tokens, LANES), jnp.int32), work // 8, named)
    preact = summed_over_wide(partial)
    latents, rec = call(
        functools.partial(decode_kernel, per),
        (array((tokens, width), BF16), array((tokens, channels), BF16)),
        work,
        preact,
        maps,
        enc_bias[None],
        dec_weight,
    )
    rows = tokens // groups
    recs = swap(rec.reshape(groups, rows, channels), NARROW)
    act_rows = lax.dynamic_slice_in_dim(activations, group * rows, rows, 0)
    mixed = call(mix_kernel, array(recs.shape, BF16), 8 * recs.size, recs, act_rows, dec_bias[None])
    back = swap(mixed, NARROW).reshape(tokens, channels)
    grads = call(
        functools.partial(grad_kernel, per), array((wide, 8, LANES), F32), work, back, dec_weight, slots
    )
    parts = swap(grads, WIDE)
    dec_grad = lax.dot_general(
        latents, back, (((0,), (0,)), ((), ())), preferred_element_type=F32
    ).astype(BF16)
    own_rows = tokens // wide
    own_maps = lax.dynamic_slice_in_dim(maps, lax.axis_index(WIDE) * own_rows, own_rows, 1)
    latent_grad = call(own_kernel, array((own_rows, width), F32), 1 << 20, parts, own_maps)
    return dec_grad, latent_grad


def local(activations, enc_weight, enc_bias, dec_weight, dec_bias, active_ids):
    width = enc_weight.shape[1]
    group = lax.axis_index(NARROW)[None]
    ids = active_ids.T
    named, slots, most = fill(8, group, ids, width)
    arrays = (activations, enc_weight, enc_bias, dec_weight, dec_bias)

    def few():
        return step_with(8, *arrays, named, slots)

    def many():
        named, slots, _ = fill(2, group, ids, width)
        return step_with(2, *arrays, named, slots)

    return lax.cond(jnp.max(most) <= LANES // 8, few, many)


def solution(mesh):
    split = Mesh(mesh.devices.reshape(16, 2, 4, 4), ("wide_0", "wide_1", "narrow_0", "narrow_1"))
    return jax.shard_map(
        local,
        mesh=split,
        in_specs=(P(None, WIDE), P(WIDE, NARROW), P(NARROW), P(NARROW, WIDE), P(WIDE), P()),
        out_specs=(P(NARROW, WIDE), P(WIDE, NARROW)),
        check_vma=False,
    )
```

```python
import functools

import jax
import jax.numpy as jnp
from jax import lax
from jax.experimental import pallas as pl
from jax.experimental.pallas import tpu as pltpu
from jax.sharding import Mesh
from jax.sharding import PartitionSpec as P

NARROW = ("narrow_0", "narrow_1")
WIDE = ("wide_0", "wide_1")
LANES = 128
F32 = jnp.float32
BF16 = jnp.bfloat16
LIMIT = 16 * 1024 * 1024

CHUNK = 16
FEW = 16


def lookup(rows, lanes):
    return jnp.take_along_axis(rows, lanes, axis=1, mode="promise_in_bounds")


def pick_slots(rows, slots, few):
    low, high = slots & (LANES - 1), slots >> 7
    picked = jnp.zeros(slots.shape, F32)
    for c in range(rows.shape[1] // LANES):
        picked = jnp.where(high == c, lookup(rows[:, c * LANES : (c + 1) * LANES], low), picked)
    picked = picked.reshape(-1, 2, 8, LANES)
    picked = picked[:, 0] + picked[:, 1]
    return jnp.sum(picked, axis=1, keepdims=True) if few else picked


def unpack_rows(packed, few):
    if few:
        return jnp.broadcast_to(packed, (CHUNK, LANES))
    return jnp.concatenate([packed, packed], axis=0)


def place(values, maps, c, shift=None):
    lanes = (maps[c // 4] >> (8 * (c % 4))) & 255
    placed = lookup(values, (lanes - 1) & (LANES - 1))
    if shift is not None:
        placed = placed + shift
    return jnp.where(lanes > 0, placed, 0.0)


def fill_slots(few, group, width, ids, named, slots, base, most):
    lane = lax.broadcasted_iota(jnp.int32, (1, LANES), 1)
    line = lax.broadcasted_iota(jnp.int32, (LANES, LANES), 0)
    entry = lax.broadcasted_iota(jnp.int32, (FEW, LANES), 0)
    every = lax.broadcasted_iota(jnp.int32, (16, LANES), 0)
    shift = width.bit_length() - 1
    needed = jnp.zeros((16, LANES), jnp.int32)

    def up_to(counts):
        at = lax.broadcasted_iota(jnp.int32, counts.shape, 1) & (CHUNK - 1)
        for s in (1, 2, 4, 8):
            counts = counts + jnp.where(at >= s, pltpu.roll(counts, s, axis=1), 0)
        return counts

    for i in range(ids.shape[1] // LANES):
        cols = pl.ds(i * LANES, LANES)
        theirs = ids[:, cols]
        within = theirs - group * width
        mine = (within >= 0) & (within < width)
        if few:
            owner = theirs >> shift
            held = jnp.full((FEW, LANES), -1, jnp.int32)
            taken = jnp.zeros((1, LANES), jnp.int32)
            tally = jnp.zeros((16, LANES), jnp.int32)
            for k in range(ids.shape[0]):
                here = mine[k : k + 1]
                held = jnp.where(entry == jnp.where(here, taken, FEW), within[k : k + 1], held)
                taken = taken + jnp.where(here, 1, 0)
                tally = tally + jnp.where(every == owner[k : k + 1], 1, 0)
            needed = jnp.maximum(needed, jnp.maximum(tally * (LANES // FEW), up_to(tally)))
            counts = jnp.broadcast_to(taken, (8, LANES))
            first = up_to(counts) - counts
            spread = jnp.full((LANES, LANES), -1, jnp.int32)
            for k in range(FEW):
                at = jnp.where(held[k : k + 1] >= 0, first[:1] + k, -1)
                spread = jnp.where(line == at, held[k : k + 1], spread)
        else:
            held = jnp.where(mine, within, -1)
            first = jnp.broadcast_to(64 * ((lane >> 3) & 1), (8, LANES))
            spread = jnp.concatenate([held, held], axis=0)
            spread = jnp.where(line >> 6 == (lane >> 3) & 1, spread, -1)
        named[:, cols] = held
        base[:, cols] = first
        slots[cols, :] = spread.T
    most[0] = jnp.max(needed)


def maps_kernel(named, base, out):
    count, tokens = named.shape
    line = lax.broadcasted_iota(jnp.int32, (LANES, LANES), 0)
    for i in range(tokens // LANES):
        cols = pl.ds(i * LANES, LANES)
        start = base[:, cols] + lax.broadcasted_iota(jnp.int32, (8, LANES), 0) + 1

        def body(n, maps):
            first = pl.multiple_of(8 * n, 8)
            eight = named[pl.ds(first, 8), cols]
            block = eight >> 7
            code = (start + first) << (8 * (block & 3))
            low = eight & (LANES - 1)
            codes = [
                jnp.where((block >= 0) & (block < 4), code, 0),
                jnp.where((block >= 4) & (block < 8), code, 0),
            ]
            for k in range(8):
                hit = line == low[k : k + 1]
                maps = [m | jnp.where(hit, f[k : k + 1], 0) for m, f in zip(maps, codes)]
            return tuple(maps)

        zero = jnp.zeros((LANES, LANES), jnp.int32)
        maps = lax.fori_loop(0, count // 8, body, (zero, zero))
        for m in range(2):
            out[m, cols, :] = maps[m].T


def encode_kernel(few, group, ids, act, weight, packed, named, slots, base, most, act_here, weight_here, arrived):
    copies = [
        pltpu.make_async_copy(act, act_here, arrived.at[0]),
        pltpu.make_async_copy(weight, weight_here, arrived.at[1]),
    ]
    for copy in copies:
        copy.start()
    fill_slots(few, group[0], weight.shape[1], ids, named, slots, base, most)
    for copy in copies:
        copy.wait()
    step = 8 * CHUNK
    for i in range(act.shape[0] // step):
        rows = pl.ds(i * step, step)
        part = jnp.dot(act_here[rows, :], weight_here[...], preferred_element_type=F32)
        picked = pick_slots(part, slots[rows, :], few)
        depth = 8 * picked.shape[1]
        packed[pl.ds(i * depth, depth), :] = picked.reshape(depth, LANES)


def decode_kernel(few, packed, maps, bias, weight, latents, rec):
    step = 8 * CHUNK
    depth = 1 if few else 8
    for i in range(latents.shape[0] // step):
        rows = pl.ds(i * step, step)
        chunks = [unpack_rows(packed[pl.ds((8 * i + q) * depth, depth), :], few) for q in range(8)]
        values = jnp.concatenate(chunks, axis=0)
        mine = [maps[0, rows, :], maps[1, rows, :]]
        for c in range(latents.shape[1] // LANES):
            cols = pl.ds(c * LANES, LANES)
            latents[rows, cols] = place(values, mine, c, bias[:, cols]).astype(BF16)
        rec[rows, :] = jnp.dot(latents[rows, :], weight[...], preferred_element_type=F32).astype(rec.dtype)


def mix_kernel(recs, act, bias, out):
    groups = recs.shape[0]
    for r in range(0, recs.shape[1], 16):
        for c in range(0, recs.shape[2], LANES):
            at = (pl.ds(r, 16), pl.ds(c, LANES))
            err = bias[:, pl.ds(c, LANES)] - act[at].astype(F32)
            errs = []
            for g in range(groups):
                err = err + recs[(g, *at)].astype(F32)
                errs.append(err)
            suffix = jnp.zeros_like(err)
            for g in reversed(range(groups)):
                suffix = suffix + errs[g]
                out[(g, *at)] = (suffix * (1.0 / groups)).astype(out.dtype)


def grad_kernel(few, back, weight, slots, out):
    step = 8 * CHUNK
    for i in range(back.shape[0] // step):
        rows = pl.ds(i * step, step)
        part = lax.dot_general(back[rows, :], weight[...], (((1,), (1,)), ((), ())), preferred_element_type=F32)
        out[pl.ds(8 * i, 8)] = pick_slots(part, slots[rows, :], few)


def own_kernel(few, pieces, maps, out):
    values = unpack_rows(jnp.sum(pieces[...], axis=0), few)
    mine = [maps[0], maps[1]]
    for c in range(out.shape[1] // LANES):
        out[:, pl.ds(c * LANES, LANES)] = place(values, mine, c)


def call(kernel, shapes, flops, *args, **params):
    moved = sum(a.size * a.dtype.itemsize for a in (*args, *jax.tree.leaves(shapes)))
    return pl.pallas_call(
        kernel,
        out_shape=shapes,
        compiler_params=pltpu.CompilerParams(vmem_limit_bytes=LIMIT),
        cost_estimate=pl.CostEstimate(flops=flops, bytes_accessed=moved, transcendentals=0),
        **params,
    )(*args)


def array(shape, dtype):
    return jax.ShapeDtypeStruct(shape, dtype)


def swap(pieces, axes):
    return lax.all_to_all(pieces, axes, 0, 0)


def summed_over_wide(partial):
    ring, core = WIDE
    rows = partial.shape[0] // 2
    both = lax.all_gather(partial, core)
    half = lax.dynamic_slice_in_dim(both, lax.axis_index(core) * rows, rows, 1)
    half = (half[0] + half[1]).astype(BF16)
    pieces = swap(jnp.broadcast_to(half[None], (lax.axis_size(ring), *half.shape)), ring)
    return lax.all_gather(jnp.sum(pieces.astype(F32), axis=0), core, tiled=True)


def encode(few, group, ids, activations, enc_weight):
    tokens, channels = activations.shape
    width = enc_weight.shape[1]
    depth = tokens // CHUNK * (1 if few else 8)
    vmem, smem = (pl.BlockSpec(memory_space=m) for m in (pltpu.VMEM, pltpu.SMEM))
    partial, named, slots, base, most = call(
        functools.partial(encode_kernel, few),
        (
            array((depth, LANES), F32),
            array((FEW if few else ids.shape[0], tokens), jnp.int32),
            array((tokens, LANES), jnp.int32),
            array((8, tokens), jnp.int32),
            array((1,), jnp.int32),
        ),
        2 * tokens * channels * width,
        group,
        ids,
        activations,
        enc_weight,
        in_specs=[smem, vmem, pl.BlockSpec(memory_space=pl.ANY), pl.BlockSpec(memory_space=pl.ANY)],
        out_specs=(vmem, vmem, vmem, vmem, smem),
        scratch_shapes=[
            pltpu.VMEM(activations.shape, BF16),
            pltpu.VMEM(enc_weight.shape, BF16),
            pltpu.SemaphoreType.DMA((2,)),
        ],
    )
    maps = call(maps_kernel, array((2, tokens, LANES), jnp.int32), 1 << 26, named, base)
    return summed_over_wide(partial), slots, maps, most[0]


def decode(few, preact, slots, maps, activations, enc_bias, dec_weight, dec_bias):
    tokens, channels = activations.shape
    width = dec_weight.shape[0]
    groups, wide = lax.axis_size(NARROW), lax.axis_size(WIDE)
    group = lax.axis_index(NARROW)
    work = 2 * tokens * channels * width
    latents, rec = call(
        functools.partial(decode_kernel, few),
        (array((tokens, width), BF16), array((tokens, channels), BF16)),
        work,
        preact,
        maps,
        enc_bias[None],
        dec_weight,
    )
    rows = tokens // groups
    recs = swap(rec.reshape(groups, rows, channels), NARROW)
    act_rows = lax.dynamic_slice_in_dim(activations, group * rows, rows, 0)
    mixed = call(mix_kernel, array(recs.shape, BF16), 8 * recs.size, recs, act_rows, dec_bias[None])
    back = swap(mixed, NARROW).reshape(tokens, channels)
    grads = call(
        functools.partial(grad_kernel, few),
        array((wide, 1 if few else 8, LANES), F32),
        work,
        back,
        dec_weight,
        slots,
    )
    parts = swap(grads, WIDE)
    dec_grad = lax.dot_general(
        latents, back, (((0,), (0,)), ((), ())), preferred_element_type=F32
    ).astype(BF16)
    own_rows = tokens // wide
    own_maps = lax.dynamic_slice_in_dim(maps, lax.axis_index(WIDE) * own_rows, own_rows, 1)
    latent_grad = call(
        functools.partial(own_kernel, few), array((own_rows, width), F32), 1 << 20, parts, own_maps
    )
    return dec_grad, latent_grad


def local(activations, enc_weight, enc_bias, dec_weight, dec_bias, active_ids):
    group = lax.axis_index(NARROW)[None]
    ids = active_ids.T
    rest = (activations, enc_bias, dec_weight, dec_bias)
    preact, slots, maps, needed = encode(True, group, ids, activations, enc_weight)

    def few():
        return decode(True, preact, slots, maps, *rest)

    def many():
        preact, slots, maps, _ = encode(False, group, ids, activations, enc_weight)
        return decode(False, preact, slots, maps, *rest)

    return lax.cond(needed <= LANES, few, many)


def solution(mesh):
    split = Mesh(mesh.devices.reshape(16, 2, 4, 4), ("wide_0", "wide_1", "narrow_0", "narrow_1"))
    return jax.shard_map(
        local,
        mesh=split,
        in_specs=(P(None, WIDE), P(WIDE, NARROW), P(NARROW), P(NARROW, WIDE), P(WIDE), P()),
        out_specs=(P(NARROW, WIDE), P(WIDE, NARROW)),
        check_vma=False,
    )
```

```python
import functools

import jax
import jax.numpy as jnp
from jax import lax
from jax.experimental import pallas as pl
from jax.experimental.pallas import tpu as pltpu
from jax.sharding import Mesh
from jax.sharding import PartitionSpec as P

NARROW = ("narrow_0", "narrow_1")
WIDE = ("wide_0", "wide_1")
LANES = 128
F32 = jnp.float32
BF16 = jnp.bfloat16
LIMIT = 16 * 1024 * 1024

CHUNK = 16
FEW = 16


def lookup(rows, lanes):
    return jnp.take_along_axis(rows, lanes, axis=1, mode="promise_in_bounds")


def pick_slots(rows, slots, few):
    low, high = slots & (LANES - 1), slots >> 7
    picked = jnp.zeros(slots.shape, F32)
    for c in range(rows.shape[1] // LANES):
        picked = jnp.where(high == c, lookup(rows[:, c * LANES : (c + 1) * LANES], low), picked)
    picked = picked.reshape(-1, 2, 8, LANES)
    picked = picked[:, 0] + picked[:, 1]
    return jnp.sum(picked, axis=1, keepdims=True) if few else picked


def unpack_rows(packed, few):
    if few:
        return jnp.broadcast_to(packed, (CHUNK, LANES))
    return jnp.concatenate([packed, packed], axis=0)


def place(values, maps, c, shift=None):
    lanes = (maps[c // 4] >> (8 * (c % 4))) & 255
    placed = lookup(values, (lanes - 1) & (LANES - 1))
    if shift is not None:
        placed = placed + shift
    return jnp.where(lanes > 0, placed, 0.0)


def fill_slots(few, group, width, ids, named, slots, base, most):
    lane = lax.broadcasted_iota(jnp.int32, (1, LANES), 1)
    line = lax.broadcasted_iota(jnp.int32, (LANES, LANES), 0)
    entry = lax.broadcasted_iota(jnp.int32, (FEW, LANES), 0)
    every = lax.broadcasted_iota(jnp.int32, (16, LANES), 0)
    shift = width.bit_length() - 1
    needed = jnp.zeros((16, LANES), jnp.int32)

    def up_to(counts):
        at = lax.broadcasted_iota(jnp.int32, counts.shape, 1) & (CHUNK - 1)
        for s in (1, 2, 4, 8):
            counts = counts + jnp.where(at >= s, pltpu.roll(counts, s, axis=1), 0)
        return counts

    for i in range(ids.shape[1] // LANES):
        cols = pl.ds(i * LANES, LANES)
        theirs = ids[:, cols]
        within = theirs - group * width
        mine = (within >= 0) & (within < width)
        if few:
            owner = theirs >> shift
            held = jnp.full((FEW, LANES), -1, jnp.int32)
            taken = jnp.zeros((1, LANES), jnp.int32)
            tally = jnp.zeros((16, LANES), jnp.int32)
            for k in range(ids.shape[0]):
                here = mine[k : k + 1]
                held = jnp.where(entry == jnp.where(here, taken, FEW), within[k : k + 1], held)
                taken = taken + jnp.where(here, 1, 0)
                tally = tally + jnp.where(every == owner[k : k + 1], 1, 0)
            needed = jnp.maximum(needed, jnp.maximum(tally * (LANES // FEW), up_to(tally)))
            counts = jnp.broadcast_to(taken, (8, LANES))
            first = up_to(counts) - counts
            spread = jnp.full((LANES, LANES), -1, jnp.int32)
            for k in range(FEW):
                at = jnp.where(held[k : k + 1] >= 0, first[:1] + k, -1)
                spread = jnp.where(line == at, held[k : k + 1], spread)
        else:
            held = jnp.where(mine, within, -1)
            first = jnp.broadcast_to(64 * ((lane >> 3) & 1), (8, LANES))
            spread = jnp.concatenate([held, held], axis=0)
            spread = jnp.where(line >> 6 == (lane >> 3) & 1, spread, -1)
        named[:, cols] = held
        base[:, cols] = first
        slots[cols, :] = spread.T
    most[0] = jnp.max(needed)


def maps_kernel(named, base, out):
    count, tokens = named.shape
    line = lax.broadcasted_iota(jnp.int32, (LANES, LANES), 0)
    for i in range(tokens // LANES):
        cols = pl.ds(i * LANES, LANES)
        start = base[:, cols] + lax.broadcasted_iota(jnp.int32, (8, LANES), 0) + 1

        def body(n, maps):
            first = pl.multiple_of(8 * n, 8)
            eight = named[pl.ds(first, 8), cols]
            block = eight >> 7
            code = (start + first) << (8 * (block & 3))
            low = eight & (LANES - 1)
            codes = [
                jnp.where((block >= 0) & (block < 4), code, 0),
                jnp.where((block >= 4) & (block < 8), code, 0),
            ]
            for k in range(8):
                hit = line == low[k : k + 1]
                maps = [m | jnp.where(hit, f[k : k + 1], 0) for m, f in zip(maps, codes)]
            return tuple(maps)

        zero = jnp.zeros((LANES, LANES), jnp.int32)
        maps = lax.fori_loop(0, count // 8, body, (zero, zero))
        for m in range(2):
            out[m, cols, :] = maps[m].T


def encode_kernel(few, group, ids, act, weight, packed, named, slots, base, most, act_here, weight_here, arrived):
    copies = [
        pltpu.make_async_copy(act, act_here, arrived.at[0]),
        pltpu.make_async_copy(weight, weight_here, arrived.at[1]),
    ]
    for copy in copies:
        copy.start()
    fill_slots(few, group[0], weight.shape[1], ids, named, slots, base, most)
    for copy in copies:
        copy.wait()
    step = 8 * CHUNK
    for i in range(act.shape[0] // step):
        rows = pl.ds(i * step, step)
        part = jnp.dot(act_here[rows, :], weight_here[...], preferred_element_type=F32)
        picked = pick_slots(part, slots[rows, :], few)
        depth = 8 * picked.shape[1]
        packed[pl.ds(i * depth, depth), :] = picked.reshape(depth, LANES)


def decode_kernel(few, packed, maps, bias, weight, latents, rec):
    step = 8 * CHUNK
    depth = 1 if few else 8
    for i in range(latents.shape[0] // step):
        rows = pl.ds(i * step, step)
        chunks = [unpack_rows(packed[pl.ds((8 * i + q) * depth, depth), :], few) for q in range(8)]
        values = jnp.concatenate(chunks, axis=0)
        mine = [maps[0, rows, :], maps[1, rows, :]]
        for c in range(latents.shape[1] // LANES):
            cols = pl.ds(c * LANES, LANES)
            latents[rows, cols] = place(values, mine, c, bias[:, cols]).astype(BF16)
        rec[rows, :] = jnp.dot(latents[rows, :], weight[...], preferred_element_type=F32).astype(rec.dtype)


def mix_kernel(recs, act, bias, out):
    groups = recs.shape[0]
    for r in range(0, recs.shape[1], 16):
        for c in range(0, recs.shape[2], LANES):
            at = (pl.ds(r, 16), pl.ds(c, LANES))
            err = bias[:, pl.ds(c, LANES)] - act[at].astype(F32)
            errs = []
            for g in range(groups):
                err = err + recs[(g, *at)].astype(F32)
                errs.append(err)
            suffix = jnp.zeros_like(err)
            for g in reversed(range(groups)):
                suffix = suffix + errs[g]
                out[(g, *at)] = (suffix * (1.0 / groups)).astype(out.dtype)


def grad_kernel(few, back, weight, slots, out):
    step = 8 * CHUNK
    for i in range(back.shape[0] // step):
        rows = pl.ds(i * step, step)
        part = lax.dot_general(back[rows, :], weight[...], (((1,), (1,)), ((), ())), preferred_element_type=F32)
        first = (8 * i + out.shape[0] // 2) % out.shape[0]
        out[pl.ds(first, 8)] = pick_slots(part, slots[rows, :], few)


def own_kernel(few, pieces, maps, out):
    values = unpack_rows(jnp.sum(pieces[...], axis=0), few)
    mine = [maps[0], maps[1]]
    for c in range(out.shape[1] // LANES):
        out[:, pl.ds(c * LANES, LANES)] = place(values, mine, c)


def call(kernel, shapes, flops, *args, **params):
    moved = sum(a.size * a.dtype.itemsize for a in (*args, *jax.tree.leaves(shapes)))
    return pl.pallas_call(
        kernel,
        out_shape=shapes,
        compiler_params=pltpu.CompilerParams(vmem_limit_bytes=LIMIT),
        cost_estimate=pl.CostEstimate(flops=flops, bytes_accessed=moved, transcendentals=0),
        **params,
    )(*args)


def array(shape, dtype):
    return jax.ShapeDtypeStruct(shape, dtype)


def swap(pieces, axes):
    return lax.all_to_all(pieces, axes, 0, 0)


def swap_from_half(pieces, axes):
    size = lax.axis_size(axes)
    order = [[(i + size // 2) % size for i in range(size)]]
    return lax.all_to_all(pieces, axes, 0, 0, axis_index_groups=order)


def summed_over_wide(partial):
    ring, core = WIDE
    rows = partial.shape[0] // 2
    both = lax.all_gather(partial, core)
    half = lax.dynamic_slice_in_dim(both, lax.axis_index(core) * rows, rows, 1)
    half = (half[0] + half[1]).astype(BF16)
    pieces = swap_from_half(jnp.broadcast_to(half[None], (lax.axis_size(ring), *half.shape)), ring)
    return lax.all_gather(jnp.sum(pieces.astype(F32), axis=0), core, tiled=True)


def encode(few, group, ids, activations, enc_weight):
    tokens, channels = activations.shape
    width = enc_weight.shape[1]
    depth = tokens // CHUNK * (1 if few else 8)
    vmem, smem = (pl.BlockSpec(memory_space=m) for m in (pltpu.VMEM, pltpu.SMEM))
    partial, named, slots, base, most = call(
        functools.partial(encode_kernel, few),
        (
            array((depth, LANES), F32),
            array((FEW if few else ids.shape[0], tokens), jnp.int32),
            array((tokens, LANES), jnp.int32),
            array((8, tokens), jnp.int32),
            array((1,), jnp.int32),
        ),
        2 * tokens * channels * width,
        group,
        ids,
        activations,
        enc_weight,
        in_specs=[smem, vmem, pl.BlockSpec(memory_space=pl.ANY), pl.BlockSpec(memory_space=pl.ANY)],
        out_specs=(vmem, vmem, vmem, vmem, smem),
        scratch_shapes=[
            pltpu.VMEM(activations.shape, BF16),
            pltpu.VMEM(enc_weight.shape, BF16),
            pltpu.SemaphoreType.DMA((2,)),
        ],
    )
    maps = call(maps_kernel, array((2, tokens, LANES), jnp.int32), 1 << 26, named, base)
    return summed_over_wide(partial), slots, maps, most[0]


def decode(few, preact, slots, maps, activations, enc_bias, dec_weight, dec_bias):
    tokens, channels = activations.shape
    width = dec_weight.shape[0]
    groups, wide = lax.axis_size(NARROW), lax.axis_size(WIDE)
    group = lax.axis_index(NARROW)
    work = 2 * tokens * channels * width
    latents, rec = call(
        functools.partial(decode_kernel, few),
        (array((tokens, width), BF16), array((tokens, channels), BF16)),
        work,
        preact,
        maps,
        enc_bias[None],
        dec_weight,
    )
    rows = tokens // groups
    recs = swap(rec.reshape(groups, rows, channels), NARROW)
    act_rows = lax.dynamic_slice_in_dim(activations, group * rows, rows, 0)
    mixed = call(mix_kernel, array(recs.shape, BF16), 8 * recs.size, recs, act_rows, dec_bias[None])
    back = swap(mixed, NARROW).reshape(tokens, channels)
    grads = call(
        functools.partial(grad_kernel, few),
        array((wide, 1 if few else 8, LANES), F32),
        work,
        back,
        dec_weight,
        slots,
    )
    parts = swap_from_half(grads, WIDE)
    dec_grad = lax.dot_general(
        latents, back, (((0,), (0,)), ((), ())), preferred_element_type=F32
    ).astype(BF16)
    own_rows = tokens // wide
    own_maps = lax.dynamic_slice_in_dim(maps, lax.axis_index(WIDE) * own_rows, own_rows, 1)
    latent_grad = call(
        functools.partial(own_kernel, few), array((own_rows, width), F32), 1 << 20, parts, own_maps
    )
    return dec_grad, latent_grad


def local(activations, enc_weight, enc_bias, dec_weight, dec_bias, active_ids):
    group = lax.axis_index(NARROW)[None]
    ids = active_ids.T
    rest = (activations, enc_bias, dec_weight, dec_bias)
    preact, slots, maps, needed = encode(True, group, ids, activations, enc_weight)

    def few():
        return decode(True, preact, slots, maps, *rest)

    def many():
        preact, slots, maps, _ = encode(False, group, ids, activations, enc_weight)
        return decode(False, preact, slots, maps, *rest)

    return lax.cond(needed <= LANES, few, many)


def solution(mesh):
    split = Mesh(mesh.devices.reshape(16, 2, 4, 4), ("wide_0", "wide_1", "narrow_0", "narrow_1"))
    return jax.shard_map(
        local,
        mesh=split,
        in_specs=(P(None, WIDE), P(WIDE, NARROW), P(NARROW), P(NARROW, WIDE), P(WIDE), P()),
        out_specs=(P(NARROW, WIDE), P(WIDE, NARROW)),
        check_vma=False,
    )
```

```python
import functools

import jax
import jax.numpy as jnp
from jax import lax
from jax.experimental import pallas as pl
from jax.experimental.pallas import tpu as pltpu
from jax.sharding import Mesh
from jax.sharding import PartitionSpec as P

NARROW = ("narrow_0", "narrow_1")
WIDE = ("wide_0", "wide_1")
LANES = 128
F32 = jnp.float32
BF16 = jnp.bfloat16
LIMIT = 16 * 1024 * 1024

CHUNK = 16
FEW = 16


def lookup(rows, lanes):
    return jnp.take_along_axis(rows, lanes, axis=1, mode="promise_in_bounds")


def pick_slots(rows, slots, few):
    low, high = slots & (LANES - 1), slots >> 7
    picked = jnp.zeros(slots.shape, F32)
    for c in range(rows.shape[1] // LANES):
        picked = jnp.where(high == c, lookup(rows[:, c * LANES : (c + 1) * LANES], low), picked)
    picked = picked.reshape(-1, 2, 8, LANES)
    picked = picked[:, 0] + picked[:, 1]
    return jnp.sum(picked, axis=1, keepdims=True) if few else picked


def unpack_rows(packed, few):
    if few:
        return jnp.broadcast_to(packed, (CHUNK, LANES))
    return jnp.concatenate([packed, packed], axis=0)


def place(values, maps, c, shift=None):
    lanes = (maps[c // 4] >> (8 * (c % 4))) & 255
    placed = lookup(values, (lanes - 1) & (LANES - 1))
    if shift is not None:
        placed = placed + shift
    return jnp.where(lanes > 0, placed, 0.0)


def fill_slots(few, group, width, ids, named, slots, base, most):
    lane = lax.broadcasted_iota(jnp.int32, (1, LANES), 1)
    line = lax.broadcasted_iota(jnp.int32, (LANES, LANES), 0)
    entry = lax.broadcasted_iota(jnp.int32, (FEW, LANES), 0)
    every = lax.broadcasted_iota(jnp.int32, (16, LANES), 0)
    shift = width.bit_length() - 1
    needed = jnp.zeros((16, LANES), jnp.int32)

    def up_to(counts):
        at = lax.broadcasted_iota(jnp.int32, counts.shape, 1) & (CHUNK - 1)
        for s in (1, 2, 4, 8):
            counts = counts + jnp.where(at >= s, pltpu.roll(counts, s, axis=1), 0)
        return counts

    for i in range(ids.shape[1] // LANES):
        cols = pl.ds(i * LANES, LANES)
        theirs = ids[:, cols]
        within = theirs - group * width
        mine = (within >= 0) & (within < width)
        if few:
            owner = theirs >> shift
            held = jnp.full((FEW, LANES), -1, jnp.int32)
            taken = jnp.zeros((1, LANES), jnp.int32)
            tally = jnp.zeros((16, LANES), jnp.int32)
            for k in range(ids.shape[0]):
                here = mine[k : k + 1]
                held = jnp.where(entry == jnp.where(here, taken, FEW), within[k : k + 1], held)
                taken = taken + jnp.where(here, 1, 0)
                tally = tally + jnp.where(every == owner[k : k + 1], 1, 0)
            needed = jnp.maximum(needed, jnp.maximum(tally * (LANES // FEW), up_to(tally)))
            counts = jnp.broadcast_to(taken, (8, LANES))
            first = up_to(counts) - counts
            spread = jnp.full((LANES, LANES), -1, jnp.int32)
            for k in range(FEW):
                at = jnp.where(held[k : k + 1] >= 0, first[:1] + k, -1)
                spread = jnp.where(line == at, held[k : k + 1], spread)
        else:
            held = jnp.where(mine, within, -1)
            first = jnp.broadcast_to(64 * ((lane >> 3) & 1), (8, LANES))
            spread = jnp.concatenate([held, held], axis=0)
            spread = jnp.where(line >> 6 == (lane >> 3) & 1, spread, -1)
        named[:, cols] = held
        base[:, cols] = first
        slots[cols, :] = spread.T
    most[0] = jnp.max(needed)


def maps_kernel(named, base, out):
    count, tokens = named.shape
    line = lax.broadcasted_iota(jnp.int32, (LANES, LANES), 0)
    for i in range(tokens // LANES):
        cols = pl.ds(i * LANES, LANES)
        start = base[:, cols] + lax.broadcasted_iota(jnp.int32, (8, LANES), 0) + 1

        def body(n, maps):
            first = pl.multiple_of(8 * n, 8)
            eight = named[pl.ds(first, 8), cols]
            block = eight >> 7
            code = (start + first) << (8 * (block & 3))
            low = eight & (LANES - 1)
            codes = [
                jnp.where((block >= 0) & (block < 4), code, 0),
                jnp.where((block >= 4) & (block < 8), code, 0),
            ]
            for k in range(8):
                hit = line == low[k : k + 1]
                maps = [m | jnp.where(hit, f[k : k + 1], 0) for m, f in zip(maps, codes)]
            return tuple(maps)

        zero = jnp.zeros((LANES, LANES), jnp.int32)
        maps = lax.fori_loop(0, count // 8, body, (zero, zero))
        for m in range(2):
            out[m, cols, :] = maps[m].T


def encode_kernel(few, group, ids, act, weight, packed, named, slots, base, most, act_here, weight_here, arrived):
    copies = [
        pltpu.make_async_copy(act, act_here, arrived.at[0]),
        pltpu.make_async_copy(weight, weight_here, arrived.at[1]),
    ]
    for copy in copies:
        copy.start()
    fill_slots(few, group[0], weight.shape[1], ids, named, slots, base, most)
    for copy in copies:
        copy.wait()
    step = 8 * CHUNK
    for i in range(act.shape[0] // step):
        rows = pl.ds(i * step, step)
        part = jnp.dot(act_here[rows, :], weight_here[...], preferred_element_type=F32)
        picked = pick_slots(part, slots[rows, :], few)
        depth = 8 * picked.shape[1]
        packed[pl.ds(i * depth, depth), :] = picked.reshape(depth, LANES)


def decode_kernel(few, packed, maps, bias, weight, latents, rec):
    step = 8 * CHUNK
    depth = 1 if few else 8
    for i in range(latents.shape[0] // step):
        rows = pl.ds(i * step, step)
        chunks = [unpack_rows(packed[pl.ds((8 * i + q) * depth, depth), :], few) for q in range(8)]
        values = jnp.concatenate(chunks, axis=0)
        mine = [maps[0, rows, :], maps[1, rows, :]]
        for c in range(latents.shape[1] // LANES):
            cols = pl.ds(c * LANES, LANES)
            latents[rows, cols] = place(values, mine, c, bias[:, cols]).astype(BF16)
        rec[rows, :] = jnp.dot(latents[rows, :], weight[...], preferred_element_type=F32).astype(rec.dtype)


def mix_kernel(sizes, recs, act, bias, out):
    groups = recs.shape[0]
    at_group = [turned(g, sizes) for g in range(groups)]
    for r in range(0, recs.shape[1], 16):
        for c in range(0, recs.shape[2], LANES):
            at = (pl.ds(r, 16), pl.ds(c, LANES))
            err = bias[:, pl.ds(c, LANES)] - act[at].astype(F32)
            errs = []
            for g in range(groups):
                err = err + recs[(at_group[g], *at)].astype(F32)
                errs.append(err)
            suffix = jnp.zeros_like(err)
            for g in reversed(range(groups)):
                suffix = suffix + errs[g]
                out[(at_group[g], *at)] = (suffix * (1.0 / groups)).astype(out.dtype)


def grad_kernel(few, back, weight, slots, out):
    step = 8 * CHUNK
    for i in range(back.shape[0] // step):
        rows = pl.ds(i * step, step)
        part = lax.dot_general(back[rows, :], weight[...], (((1,), (1,)), ((), ())), preferred_element_type=F32)
        first = (8 * i + out.shape[0] // 2) % out.shape[0]
        out[pl.ds(first, 8)] = pick_slots(part, slots[rows, :], few)


def own_kernel(few, pieces, maps, out):
    values = unpack_rows(jnp.sum(pieces[...], axis=0), few)
    mine = [maps[0], maps[1]]
    for c in range(out.shape[1] // LANES):
        out[:, pl.ds(c * LANES, LANES)] = place(values, mine, c)


def call(kernel, shapes, flops, *args, **params):
    moved = sum(a.size * a.dtype.itemsize for a in (*args, *jax.tree.leaves(shapes)))
    return pl.pallas_call(
        kernel,
        out_shape=shapes,
        compiler_params=pltpu.CompilerParams(vmem_limit_bytes=LIMIT),
        cost_estimate=pl.CostEstimate(flops=flops, bytes_accessed=moved, transcendentals=0),
        **params,
    )(*args)


def array(shape, dtype):
    return jax.ShapeDtypeStruct(shape, dtype)


def turned(place, sizes):
    out, step = 0, 1
    for size in reversed(sizes):
        out = out + (place // step % size + size // 2) % size * step
        step = step * size
    return out


def sizes_of(axes):
    return [lax.axis_size(a) for a in axes]


def swap_from_far(pieces, axes, sizes):
    order = [[turned(i, sizes) for i in range(pieces.shape[0])]]
    return lax.all_to_all(pieces, axes, 0, 0, axis_index_groups=order)


def summed_over_wide(partial):
    ring, core = WIDE
    rows = partial.shape[0] // 2
    both = lax.all_gather(partial, core)
    half = lax.dynamic_slice_in_dim(both, lax.axis_index(core) * rows, rows, 1)
    half = (half[0] + half[1]).astype(BF16)
    size = lax.axis_size(ring)
    pieces = swap_from_far(jnp.broadcast_to(half[None], (size, *half.shape)), ring, [size])
    return lax.all_gather(jnp.sum(pieces.astype(F32), axis=0), core, tiled=True)


def encode(few, group, ids, activations, enc_weight):
    tokens, channels = activations.shape
    width = enc_weight.shape[1]
    depth = tokens // CHUNK * (1 if few else 8)
    vmem, smem = (pl.BlockSpec(memory_space=m) for m in (pltpu.VMEM, pltpu.SMEM))
    partial, named, slots, base, most = call(
        functools.partial(encode_kernel, few),
        (
            array((depth, LANES), F32),
            array((FEW if few else ids.shape[0], tokens), jnp.int32),
            array((tokens, LANES), jnp.int32),
            array((8, tokens), jnp.int32),
            array((1,), jnp.int32),
        ),
        2 * tokens * channels * width,
        group,
        ids,
        activations,
        enc_weight,
        in_specs=[smem, vmem, pl.BlockSpec(memory_space=pl.ANY), pl.BlockSpec(memory_space=pl.ANY)],
        out_specs=(vmem, vmem, vmem, vmem, smem),
        scratch_shapes=[
            pltpu.VMEM(activations.shape, BF16),
            pltpu.VMEM(enc_weight.shape, BF16),
            pltpu.SemaphoreType.DMA((2,)),
        ],
    )
    maps = call(maps_kernel, array((2, tokens, LANES), jnp.int32), 1 << 26, named, base)
    return summed_over_wide(partial), slots, maps, most[0]


def decode(few, preact, slots, maps, activations, enc_bias, dec_weight, dec_bias):
    tokens, channels = activations.shape
    width = dec_weight.shape[0]
    groups, wide = lax.axis_size(NARROW), lax.axis_size(WIDE)
    group = lax.axis_index(NARROW)
    work = 2 * tokens * channels * width
    latents, rec = call(
        functools.partial(decode_kernel, few),
        (array((tokens, width), BF16), array((tokens, channels), BF16)),
        work,
        preact,
        maps,
        enc_bias[None],
        dec_weight,
    )
    rows = tokens // groups
    sizes = sizes_of(NARROW)
    recs = swap_from_far(rec.reshape(groups, rows, channels), NARROW, sizes)
    act_rows = lax.dynamic_slice_in_dim(activations, turned(group, sizes) * rows, rows, 0)
    mixed = call(
        functools.partial(mix_kernel, sizes),
        array(recs.shape, BF16),
        8 * recs.size,
        recs,
        act_rows,
        dec_bias[None],
    )
    back = swap_from_far(mixed, NARROW, sizes).reshape(tokens, channels)
    grads = call(
        functools.partial(grad_kernel, few),
        array((wide, 1 if few else 8, LANES), F32),
        work,
        back,
        dec_weight,
        slots,
    )
    parts = swap_from_far(grads, WIDE, [wide])
    dec_grad = lax.dot_general(
        latents, back, (((0,), (0,)), ((), ())), preferred_element_type=F32
    ).astype(BF16)
    own_rows = tokens // wide
    own_maps = lax.dynamic_slice_in_dim(maps, lax.axis_index(WIDE) * own_rows, own_rows, 1)
    latent_grad = call(
        functools.partial(own_kernel, few), array((own_rows, width), F32), 1 << 20, parts, own_maps
    )
    return dec_grad, latent_grad


def local(activations, enc_weight, enc_bias, dec_weight, dec_bias, active_ids):
    group = lax.axis_index(NARROW)[None]
    ids = active_ids.T
    rest = (activations, enc_bias, dec_weight, dec_bias)
    preact, slots, maps, needed = encode(True, group, ids, activations, enc_weight)

    def few():
        return decode(True, preact, slots, maps, *rest)

    def many():
        preact, slots, maps, _ = encode(False, group, ids, activations, enc_weight)
        return decode(False, preact, slots, maps, *rest)

    return lax.cond(needed <= LANES, few, many)


def solution(mesh):
    split = Mesh(mesh.devices.reshape(16, 2, 4, 4), ("wide_0", "wide_1", "narrow_0", "narrow_1"))
    return jax.shard_map(
        local,
        mesh=split,
        in_specs=(P(None, WIDE), P(WIDE, NARROW), P(NARROW), P(NARROW, WIDE), P(WIDE), P()),
        out_specs=(P(NARROW, WIDE), P(WIDE, NARROW)),
        check_vma=False,
    )
```

```python
import functools

import jax
import jax.numpy as jnp
from jax import lax
from jax.experimental import pallas as pl
from jax.experimental.pallas import tpu as pltpu
from jax.sharding import Mesh
from jax.sharding import PartitionSpec as P

NARROW = ("narrow_0", "narrow_1")
WIDE = ("wide_0", "wide_1")
LANES = 128
F32 = jnp.float32
BF16 = jnp.bfloat16
LIMIT = 16 * 1024 * 1024

CHUNK = 16
FEW = 16


def lookup(rows, lanes):
    return jnp.take_along_axis(rows, lanes, axis=1, mode="promise_in_bounds")


def pick_slots(rows, slots, few):
    low, high = slots & (LANES - 1), slots >> 7
    picked = jnp.zeros(slots.shape, F32)
    for c in range(rows.shape[1] // LANES):
        picked = jnp.where(high == c, lookup(rows[:, c * LANES : (c + 1) * LANES], low), picked)
    picked = picked.reshape(-1, 2, 8, LANES)
    picked = picked[:, 0] + picked[:, 1]
    return jnp.sum(picked, axis=1, keepdims=True) if few else picked


def unpack_rows(packed, few):
    if few:
        return jnp.broadcast_to(packed, (CHUNK, LANES))
    return jnp.concatenate([packed, packed], axis=0)


def place(values, maps, c, shift=None):
    lanes = (maps[c // 4] >> (8 * (c % 4))) & 255
    placed = lookup(values, (lanes - 1) & (LANES - 1))
    if shift is not None:
        placed = placed + shift
    return jnp.where(lanes > 0, placed, 0.0)


def up_to(counts):
    at = lax.broadcasted_iota(jnp.int32, counts.shape, 1) & (CHUNK - 1)
    for s in (1, 2, 4, 8):
        counts = counts + jnp.where(at >= s, pltpu.roll(counts, s, axis=1), 0)
    return counts


def fill_slots(few, group, width, ids, named, slots, base):
    count, tokens = ids.shape
    lane = lax.broadcasted_iota(jnp.int32, (1, LANES), 1)
    line = lax.broadcasted_iota(jnp.int32, (LANES, LANES), 0)
    within = ids[...] - group * width
    mine = (within >= 0) & (within < width)
    if few:
        entry = lax.broadcasted_iota(jnp.int32, (FEW, tokens), 0)
        earlier = lax.broadcasted_iota(jnp.int32, (count, count), 0) > lax.broadcasted_iota(jnp.int32, (count, count), 1)
        ones = jnp.where(mine, 1.0, 0.0)
        rank = jnp.dot(
            jnp.where(earlier, 1.0, 0.0).astype(BF16), ones.astype(BF16), preferred_element_type=F32
        )
        taken = (rank[count - 1 :] + ones[count - 1 :]).astype(jnp.int32)
        place_of = jnp.where(mine, rank.astype(jnp.int32), FEW)
        held = jnp.full((FEW, tokens), -1, jnp.int32)
        for k in range(count):
            held = jnp.where(entry == place_of[k : k + 1], within[k : k + 1], held)
    else:
        held = jnp.where(mine, within, -1)
    named[...] = held
    for i in range(tokens // LANES):
        cols = pl.ds(i * LANES, LANES)
        block = held[:, i * LANES : (i + 1) * LANES]
        if few:
            counts = jnp.broadcast_to(taken[:, i * LANES : (i + 1) * LANES], (8, LANES))
            first = up_to(counts) - counts
            spread = jnp.full((LANES, LANES), -1, jnp.int32)
            for k in range(FEW):
                at = jnp.where(block[k : k + 1] >= 0, first[:1] + k, -1)
                spread = jnp.where(line == at, block[k : k + 1], spread)
        else:
            first = jnp.broadcast_to(64 * ((lane >> 3) & 1), (8, LANES))
            spread = jnp.concatenate([block, block], axis=0)
            spread = jnp.where(line >> 6 == (lane >> 3) & 1, spread, -1)
        base[:, cols] = first
        slots[cols, :] = spread.T


def count_kernel(width, ids, most):
    every = lax.broadcasted_iota(jnp.int32, (16, LANES), 0)
    needed = jnp.zeros((16, LANES), jnp.int32)
    for i in range(ids.shape[1] // LANES):
        owner = ids[:, pl.ds(i * LANES, LANES)] >> (width.bit_length() - 1)
        tally = jnp.zeros((16, LANES), jnp.int32)
        for k in range(ids.shape[0]):
            tally = tally + jnp.where(every == owner[k : k + 1], 1, 0)
        needed = jnp.maximum(needed, jnp.maximum(tally * (LANES // FEW), up_to(tally)))
    most[0] = jnp.max(needed)


def target_kernel(place_of, act, bias, out):
    rows = out.shape[0]
    first = pl.multiple_of(place_of[0] * rows, rows)
    out[...] = bias[...] - act[pl.ds(first, rows), :].astype(F32)


def turn_kernel(weight, out):
    for r in range(0, weight.shape[0], 256):
        out[:, pl.ds(r, 256)] = weight[pl.ds(r, 256), :].T


def maps_kernel(named, base, out):
    count, tokens = named.shape
    line = lax.broadcasted_iota(jnp.int32, (LANES, LANES), 0)
    for i in range(tokens // LANES):
        cols = pl.ds(i * LANES, LANES)
        start = base[:, cols] + lax.broadcasted_iota(jnp.int32, (8, LANES), 0) + 1

        def body(n, maps):
            first = pl.multiple_of(8 * n, 8)
            eight = named[pl.ds(first, 8), cols]
            block = eight >> 7
            code = (start + first) << (8 * (block & 3))
            low = eight & (LANES - 1)
            codes = [
                jnp.where((block >= 0) & (block < 4), code, 0),
                jnp.where((block >= 4) & (block < 8), code, 0),
            ]
            for k in range(8):
                hit = line == low[k : k + 1]
                maps = [m | jnp.where(hit, f[k : k + 1], 0) for m, f in zip(maps, codes)]
            return tuple(maps)

        zero = jnp.zeros((LANES, LANES), jnp.int32)
        maps = lax.fori_loop(0, count // 8, body, (zero, zero))
        for m in range(2):
            out[m, cols, :] = maps[m].T


def encode_kernel(few, group, ids, act, weight, packed, named, slots, base, act_here, weight_here, arrived):
    copies = [
        pltpu.make_async_copy(act, act_here, arrived.at[0]),
        pltpu.make_async_copy(weight, weight_here, arrived.at[1]),
    ]
    for copy in copies:
        copy.start()
    fill_slots(few, group[0], weight.shape[1], ids, named, slots, base)
    for copy in copies:
        copy.wait()
    step = 8 * CHUNK
    for i in range(act.shape[0] // step):
        rows = pl.ds(i * step, step)
        part = jnp.dot(act_here[rows, :], weight_here[...], preferred_element_type=F32)
        picked = pick_slots(part, slots[rows, :], few)
        depth = 8 * picked.shape[1]
        packed[pl.ds(i * depth, depth), :] = picked.reshape(depth, LANES)


def decode_kernel(few, packed, maps, bias, weight, latents, rec):
    step = 8 * CHUNK
    depth = 1 if few else 8
    for i in range(latents.shape[0] // step):
        rows = pl.ds(i * step, step)
        chunks = [unpack_rows(packed[pl.ds((8 * i + q) * depth, depth), :], few) for q in range(8)]
        values = jnp.concatenate(chunks, axis=0)
        mine = [maps[0, rows, :], maps[1, rows, :]]
        blocks = [
            place(values, mine, c, bias[:, pl.ds(c * LANES, LANES)]) for c in range(latents.shape[1] // LANES)
        ]
        here = jnp.concatenate(blocks, axis=1).astype(BF16)
        latents[rows, :] = here
        rec[rows, :] = jnp.dot(here, weight[...], preferred_element_type=F32).astype(rec.dtype)


def mix_kernel(sizes, recs, target, out):
    groups = recs.shape[0]
    at_group = [turned(g, sizes) for g in range(groups)]
    for r in range(0, recs.shape[1], 16):
        for c in range(0, recs.shape[2], LANES):
            at = (pl.ds(r, 16), pl.ds(c, LANES))
            err = target[at]
            errs = []
            for g in range(groups):
                err = err + recs[(at_group[g], *at)].astype(F32)
                errs.append(err)
            suffix = jnp.zeros_like(err)
            for g in reversed(range(groups)):
                suffix = suffix + errs[g]
                out[(at_group[g], *at)] = (suffix * (1.0 / groups)).astype(out.dtype)


def grad_kernel(few, back, turned_weight, slots, out):
    step = 8 * CHUNK
    for i in range(back.shape[0] // step):
        rows = pl.ds(i * step, step)
        part = jnp.dot(back[rows, :], turned_weight[...], preferred_element_type=F32)
        first = (8 * i + out.shape[0] // 2) % out.shape[0]
        out[pl.ds(first, 8)] = pick_slots(part, slots[rows, :], few)


def own_kernel(few, pieces, maps, out):
    values = unpack_rows(jnp.sum(pieces[...], axis=0), few)
    mine = [maps[0], maps[1]]
    for c in range(out.shape[1] // LANES):
        out[:, pl.ds(c * LANES, LANES)] = place(values, mine, c)


def call(kernel, shapes, flops, *args, **params):
    moved = sum(a.size * a.dtype.itemsize for a in (*args, *jax.tree.leaves(shapes)))
    return pl.pallas_call(
        kernel,
        out_shape=shapes,
        compiler_params=pltpu.CompilerParams(vmem_limit_bytes=LIMIT),
        cost_estimate=pl.CostEstimate(flops=flops, bytes_accessed=moved, transcendentals=0),
        **params,
    )(*args)


def array(shape, dtype):
    return jax.ShapeDtypeStruct(shape, dtype)


def turned(place, sizes):
    out, step = 0, 1
    for size in reversed(sizes):
        out = out + (place // step % size + size // 2) % size * step
        step = step * size
    return out


def sizes_of(axes):
    return [lax.axis_size(a) for a in axes]


def swap_from_far(pieces, axes, sizes):
    order = [[turned(i, sizes) for i in range(pieces.shape[0])]]
    return lax.all_to_all(pieces, axes, 0, 0, axis_index_groups=order)


def summed_over_wide(partial):
    ring, core = WIDE
    rows = partial.shape[0] // 2
    both = lax.all_gather(partial, core)
    half = lax.dynamic_slice_in_dim(both, lax.axis_index(core) * rows, rows, 1)
    half = (half[0] + half[1]).astype(BF16)
    size = lax.axis_size(ring)
    pieces = swap_from_far(jnp.broadcast_to(half[None], (size, *half.shape)), ring, [size])
    return lax.all_gather(jnp.sum(pieces.astype(F32), axis=0), core, tiled=True)


def specs(*spaces):
    return [pl.BlockSpec(memory_space=m) for m in spaces]


def encode(few, group, ids, activations, enc_weight):
    tokens, channels = activations.shape
    width = enc_weight.shape[1]
    depth = tokens // CHUNK * (1 if few else 8)
    partial, named, slots, base = call(
        functools.partial(encode_kernel, few),
        (
            array((depth, LANES), F32),
            array((FEW if few else ids.shape[0], tokens), jnp.int32),
            array((tokens, LANES), jnp.int32),
            array((8, tokens), jnp.int32),
        ),
        2 * tokens * channels * width,
        group,
        ids,
        activations,
        enc_weight,
        in_specs=specs(pltpu.SMEM, pltpu.VMEM, pl.ANY, pl.ANY),
        scratch_shapes=[
            pltpu.VMEM(activations.shape, BF16),
            pltpu.VMEM(enc_weight.shape, BF16),
            pltpu.SemaphoreType.DMA((2,)),
        ],
    )
    maps = call(maps_kernel, array((2, tokens, LANES), jnp.int32), 1 << 26, named, base)
    return summed_over_wide(partial), slots, maps


def decode(few, preact, maps, target, enc_bias, dec_weight):
    width, channels = dec_weight.shape
    tokens = maps.shape[1]
    latents, rec = call(
        functools.partial(decode_kernel, few),
        (array((tokens, width), BF16), array((tokens, channels), BF16)),
        2 * tokens * channels * width,
        preact,
        maps,
        enc_bias[None],
        dec_weight,
    )
    sizes = sizes_of(NARROW)
    recs = swap_from_far(rec.reshape(-1, *target.shape), NARROW, sizes)
    mixed = call(functools.partial(mix_kernel, sizes), array(recs.shape, BF16), 8 * recs.size, recs, target)
    return latents, swap_from_far(mixed, NARROW, sizes).reshape(tokens, channels)


def latent_parts(few, back, turned_weight, slots):
    return call(
        functools.partial(grad_kernel, few),
        array((lax.axis_size(WIDE), 1 if few else 8, LANES), F32),
        2 * back.size * turned_weight.shape[1],
        back,
        turned_weight,
        slots,
    )


def finish(few, grads, back, latents, maps):
    wide = lax.axis_size(WIDE)
    parts = swap_from_far(grads, WIDE, [wide])
    dec_grad = lax.dot_general(
        latents, back, (((0,), (0,)), ((), ())), preferred_element_type=F32
    ).astype(BF16)
    own_rows = maps.shape[1] // wide
    own_maps = lax.dynamic_slice_in_dim(maps, lax.axis_index(WIDE) * own_rows, own_rows, 1)
    latent_grad = call(
        functools.partial(own_kernel, few),
        array((own_rows, latents.shape[1]), F32),
        1 << 20,
        parts,
        own_maps,
    )
    return dec_grad, latent_grad


def local(activations, enc_weight, enc_bias, dec_weight, dec_bias, active_ids):
    tokens, channels = activations.shape
    width = enc_weight.shape[1]
    group = lax.axis_index(NARROW)
    ids = active_ids.T
    preact, slots, maps = encode(True, group[None], ids, activations, enc_weight)
    needed = call(
        functools.partial(count_kernel, width),
        array((1,), jnp.int32),
        1 << 24,
        ids,
        out_specs=specs(pltpu.SMEM)[0],
    )
    target = call(
        target_kernel,
        array((tokens // lax.axis_size(NARROW), channels), F32),
        1 << 20,
        turned(group, sizes_of(NARROW))[None],
        activations,
        dec_bias[None],
        in_specs=specs(pltpu.SMEM, pltpu.VMEM, pltpu.VMEM),
    )
    turned_weight = call(turn_kernel, array((channels, width), BF16), 1 << 26, dec_weight)
    latents, back = decode(True, preact, maps, target, enc_bias, dec_weight)

    grads = latent_parts(True, back, turned_weight, slots)

    def few():
        return finish(True, grads, back, latents, maps)

    def many():
        preact, slots, maps = encode(False, group[None], ids, activations, enc_weight)
        latents, back = decode(False, preact, maps, target, enc_bias, dec_weight)
        return finish(False, latent_parts(False, back, turned_weight, slots), back, latents, maps)

    return lax.cond(needed[0] <= LANES, few, many)


def solution(mesh):
    split = Mesh(mesh.devices.reshape(16, 2, 4, 4), ("wide_0", "wide_1", "narrow_0", "narrow_1"))
    return jax.shard_map(
        local,
        mesh=split,
        in_specs=(P(None, WIDE), P(WIDE, NARROW), P(NARROW), P(NARROW, WIDE), P(WIDE), P()),
        out_specs=(P(NARROW, WIDE), P(WIDE, NARROW)),
        check_vma=False,
    )
```

```python
import functools

import jax
import jax.numpy as jnp
from jax import lax
from jax.experimental import pallas as pl
from jax.experimental.pallas import tpu as pltpu
from jax.sharding import Mesh
from jax.sharding import PartitionSpec as P

NARROW = ("narrow_0", "narrow_1")
WIDE = ("wide_0", "wide_1")
LANES = 128
F32 = jnp.float32
BF16 = jnp.bfloat16
LIMIT = 16 * 1024 * 1024

CHUNK = 16
FEW = 16


def lookup(rows, lanes):
    return jnp.take_along_axis(rows, lanes, axis=1, mode="promise_in_bounds")


def pick_slots(rows, slots, few):
    low, high = slots & (LANES - 1), slots >> 7
    picked = jnp.zeros(slots.shape, F32)
    for c in range(rows.shape[1] // LANES):
        picked = jnp.where(high == c, lookup(rows[:, c * LANES : (c + 1) * LANES], low), picked)
    picked = picked.reshape(-1, 2, 8, LANES)
    picked = picked[:, 0] + picked[:, 1]
    return jnp.sum(picked, axis=1, keepdims=True) if few else picked


def unpack_rows(packed, few):
    if few:
        return jnp.broadcast_to(packed, (CHUNK, LANES))
    return jnp.concatenate([packed, packed], axis=0)


def place(values, maps, c, shift=None):
    lanes = (maps[c // 4] >> (8 * (c % 4))) & 255
    placed = lookup(values, (lanes - 1) & (LANES - 1))
    if shift is not None:
        placed = placed + shift
    return jnp.where(lanes > 0, placed, 0.0)


def up_to(counts):
    at = lax.broadcasted_iota(jnp.int32, counts.shape, 1) & (CHUNK - 1)
    for s in (1, 2, 4, 8):
        counts = counts + jnp.where(at >= s, pltpu.roll(counts, s, axis=1), 0)
    return counts


def fill_slots(few, group, width, ids, named, slots, base):
    count, tokens = ids.shape
    lane = lax.broadcasted_iota(jnp.int32, (1, LANES), 1)
    line = lax.broadcasted_iota(jnp.int32, (LANES, LANES), 0)
    within = ids[...] - group * width
    mine = (within >= 0) & (within < width)
    if few:
        entry = lax.broadcasted_iota(jnp.int32, (FEW, tokens), 0)
        earlier = lax.broadcasted_iota(jnp.int32, (count, count), 0) > lax.broadcasted_iota(jnp.int32, (count, count), 1)
        ones = jnp.where(mine, 1.0, 0.0)
        rank = jnp.dot(
            jnp.where(earlier, 1.0, 0.0).astype(BF16), ones.astype(BF16), preferred_element_type=F32
        )
        taken = (rank[count - 1 :] + ones[count - 1 :]).astype(jnp.int32)
        place_of = jnp.where(mine, rank.astype(jnp.int32), FEW)
        held = jnp.full((FEW, tokens), -1, jnp.int32)
        for k in range(count):
            held = jnp.where(entry == place_of[k : k + 1], within[k : k + 1], held)
    else:
        held = jnp.where(mine, within, -1)
    named[...] = held
    for i in range(tokens // LANES):
        cols = pl.ds(i * LANES, LANES)
        block = held[:, i * LANES : (i + 1) * LANES]
        if few:
            counts = jnp.broadcast_to(taken[:, i * LANES : (i + 1) * LANES], (8, LANES))
            first = up_to(counts) - counts
            spread = jnp.full((LANES, LANES), -1, jnp.int32)
            for k in range(FEW):
                at = jnp.where(block[k : k + 1] >= 0, first[:1] + k, -1)
                spread = jnp.where(line == at, block[k : k + 1], spread)
        else:
            first = jnp.broadcast_to(64 * ((lane >> 3) & 1), (8, LANES))
            spread = jnp.concatenate([block, block], axis=0)
            spread = jnp.where(line >> 6 == (lane >> 3) & 1, spread, -1)
        base[:, cols] = first
        slots[cols, :] = spread.T


def target_kernel(width, place_of, act, bias, ids, out, most, here, arrived):
    rows = out.shape[0]
    first = pl.multiple_of(place_of[0] * rows, rows)
    copy = pltpu.make_async_copy(act.at[pl.ds(first, rows)], here, arrived)
    copy.start()
    every = lax.broadcasted_iota(jnp.int32, (16, LANES), 0)
    needed = jnp.zeros((16, LANES), jnp.int32)
    for i in range(ids.shape[1] // LANES):
        owner = ids[:, pl.ds(i * LANES, LANES)] >> (width.bit_length() - 1)
        tally = jnp.zeros((16, LANES), jnp.int32)
        for k in range(ids.shape[0]):
            tally = tally + jnp.where(every == owner[k : k + 1], 1, 0)
        needed = jnp.maximum(needed, jnp.maximum(tally * (LANES // FEW), up_to(tally)))
    most[0] = jnp.max(needed)
    copy.wait()
    out[...] = bias[...] - here[...].astype(F32)


def maps_kernel(owner, named, base, weight, out, own, turned_weight):
    count, tokens = named.shape
    line = lax.broadcasted_iota(jnp.int32, (LANES, LANES), 0)
    for i in range(tokens // LANES):
        cols = pl.ds(i * LANES, LANES)
        start = base[:, cols] + lax.broadcasted_iota(jnp.int32, (8, LANES), 0) + 1

        def body(n, maps):
            first = pl.multiple_of(8 * n, 8)
            eight = named[pl.ds(first, 8), cols]
            block = eight >> 7
            code = (start + first) << (8 * (block & 3))
            low = eight & (LANES - 1)
            codes = [
                jnp.where((block >= 0) & (block < 4), code, 0),
                jnp.where((block >= 4) & (block < 8), code, 0),
            ]
            for k in range(8):
                hit = line == low[k : k + 1]
                maps = [m | jnp.where(hit, f[k : k + 1], 0) for m, f in zip(maps, codes)]
            return tuple(maps)

        zero = jnp.zeros((LANES, LANES), jnp.int32)
        maps = lax.fori_loop(0, count // 8, body, (zero, zero))
        for m in range(2):
            out[m, cols, :] = maps[m].T
    own[...] = out[:, pl.ds(pl.multiple_of(owner[0] * CHUNK, CHUNK), CHUNK), :]
    for r in range(0, weight.shape[0], 256):
        turned_weight[:, pl.ds(r, 256)] = weight[pl.ds(r, 256), :].T


def encode_kernel(few, group, ids, act, weight, packed, named, slots, base, act_here, weight_here, arrived):
    copies = []
    for n, (array, here) in enumerate(((act, act_here), (weight, weight_here))):
        step = array.shape[0] // 4
        for i in range(4):
            rows = pl.ds(i * step, step)
            copies.append(pltpu.make_async_copy(array.at[rows], here.at[rows], arrived.at[4 * n + i]))
            copies[-1].start()
    fill_slots(few, group[0], weight.shape[1], ids, named, slots, base)
    for copy in copies:
        copy.wait()
    step = 8 * CHUNK
    for i in range(act.shape[0] // step):
        rows = pl.ds(i * step, step)
        part = jnp.dot(act_here[rows, :], weight_here[...], preferred_element_type=F32)
        picked = pick_slots(part, slots[rows, :], few)
        depth = 8 * picked.shape[1]
        packed[pl.ds(i * depth, depth), :] = picked.reshape(depth, LANES)


def decode_kernel(few, packed, maps, bias, weight, latents, rec, weight_here, rec_here, arrived, sent):
    step = 8 * CHUNK
    depth = 1 if few else 8
    steps = latents.shape[0] // step
    part = weight.shape[0] // 4
    coming = [
        pltpu.make_async_copy(weight.at[pl.ds(i * part, part)], weight_here.at[pl.ds(i * part, part)], arrived.at[i])
        for i in range(4)
    ]
    for copy in coming:
        copy.start()

    def fill(i):
        rows = pl.ds(i * step, step)
        chunks = [unpack_rows(packed[pl.ds((8 * i + q) * depth, depth), :], few) for q in range(8)]
        values = jnp.concatenate(chunks, axis=0)
        mine = [maps[0, rows, :], maps[1, rows, :]]
        blocks = [
            place(values, mine, c, bias[:, pl.ds(c * LANES, LANES)]) for c in range(latents.shape[1] // LANES)
        ]
        latents[rows, :] = jnp.concatenate(blocks, axis=1).astype(BF16)

    ahead = 2
    for i in range(ahead):
        fill(i)
    for copy in coming:
        copy.wait()
    going = []
    for i in range(steps):
        rows = pl.ds(i * step, step)
        rec_here[rows, :] = jnp.dot(latents[rows, :], weight_here[...], preferred_element_type=F32).astype(rec.dtype)
        going.append(pltpu.make_async_copy(rec_here.at[rows], rec.at[rows], sent.at[i]))
        going[-1].start()
        if i + ahead < steps:
            fill(i + ahead)
    for copy in going:
        copy.wait()


def mix_kernel(sizes, recs, target, out):
    groups = recs.shape[0]
    at_group = [turned(g, sizes) for g in range(groups)]
    for r in range(0, recs.shape[1], 16):
        for c in range(0, recs.shape[2], LANES):
            at = (pl.ds(r, 16), pl.ds(c, LANES))
            err = target[at]
            errs = []
            for g in range(groups):
                err = err + recs[(at_group[g], *at)].astype(F32)
                errs.append(err)
            suffix = jnp.zeros_like(err)
            for g in reversed(range(groups)):
                suffix = suffix + errs[g]
                out[(at_group[g], *at)] = (suffix * (1.0 / groups)).astype(out.dtype)


def grad_kernel(few, back, turned_weight, slots, out):
    step = 8 * CHUNK
    for i in range(back.shape[0] // step):
        rows = pl.ds(i * step, step)
        part = jnp.dot(back[rows, :], turned_weight[...], preferred_element_type=F32)
        first = (8 * i + out.shape[0] // 2) % out.shape[0]
        out[pl.ds(first, 8)] = pick_slots(part, slots[rows, :], few)


def outer_kernel(latents, back, out, here, sent):
    step = 256
    copies = []
    for i in range(out.shape[0] // step):
        rows = pl.ds(i * step, step)
        part = lax.dot_general(
            latents[:, i * step : (i + 1) * step],
            back[...],
            (((0,), (0,)), ((), ())),
            preferred_element_type=F32,
        )
        here[rows, :] = part.astype(out.dtype)
        copies.append(pltpu.make_async_copy(here.at[rows], out.at[rows], sent.at[i]))
        copies[-1].start()
    for copy in copies:
        copy.wait()


def own_kernel(few, pieces, maps, out):
    values = unpack_rows(jnp.sum(pieces[...], axis=0), few)
    mine = [maps[0], maps[1]]
    for c in range(out.shape[1] // LANES):
        out[:, pl.ds(c * LANES, LANES)] = place(values, mine, c)


def call(kernel, shapes, flops, *args, **params):
    moved = sum(a.size * a.dtype.itemsize for a in (*args, *jax.tree.leaves(shapes)))
    return pl.pallas_call(
        kernel,
        out_shape=shapes,
        compiler_params=pltpu.CompilerParams(vmem_limit_bytes=LIMIT),
        cost_estimate=pl.CostEstimate(flops=flops, bytes_accessed=moved, transcendentals=0),
        **params,
    )(*args)


def array(shape, dtype):
    return jax.ShapeDtypeStruct(shape, dtype)


def turned(place, sizes):
    out, step = 0, 1
    for size in reversed(sizes):
        out = out + (place // step % size + size // 2) % size * step
        step = step * size
    return out


def sizes_of(axes):
    return [lax.axis_size(a) for a in axes]


def swap_from_far(pieces, axes, sizes):
    order = [[turned(i, sizes) for i in range(pieces.shape[0])]]
    return lax.all_to_all(pieces, axes, 0, 0, axis_index_groups=order)


def summed_over_wide(partial):
    ring, core = WIDE
    rows = partial.shape[0] // 2
    both = lax.all_gather(partial, core)
    half = lax.dynamic_slice_in_dim(both, lax.axis_index(core) * rows, rows, 1)
    half = (half[0] + half[1]).astype(BF16)
    size = lax.axis_size(ring)
    pieces = swap_from_far(jnp.broadcast_to(half[None], (size, *half.shape)), ring, [size])
    return lax.all_gather(jnp.sum(pieces.astype(F32), axis=0), core, tiled=True)


def specs(*spaces):
    return [pl.BlockSpec(memory_space=m) for m in spaces]


def encode(few, group, ids, activations, enc_weight):
    tokens, channels = activations.shape
    width = enc_weight.shape[1]
    depth = tokens // CHUNK * (1 if few else 8)
    partial, named, slots, base = call(
        functools.partial(encode_kernel, few),
        (
            array((depth, LANES), F32),
            array((FEW if few else ids.shape[0], tokens), jnp.int32),
            array((tokens, LANES), jnp.int32),
            array((8, tokens), jnp.int32),
        ),
        2 * tokens * channels * width,
        group,
        ids,
        activations,
        enc_weight,
        in_specs=specs(pltpu.SMEM, pltpu.VMEM, pl.ANY, pl.ANY),
        scratch_shapes=[
            pltpu.VMEM(activations.shape, BF16),
            pltpu.VMEM(enc_weight.shape, BF16),
            pltpu.SemaphoreType.DMA((8,)),
        ],
    )
    return partial, named, slots, base


def find(named, base, dec_weight):
    tokens = named.shape[1]
    return call(
        maps_kernel,
        (
            array((2, tokens, LANES), jnp.int32),
            array((2, CHUNK, LANES), jnp.int32),
            array(dec_weight.shape[::-1], BF16),
        ),
        1 << 26,
        lax.axis_index(WIDE)[None],
        named,
        base,
        dec_weight,
        in_specs=specs(pltpu.SMEM, pltpu.VMEM, pltpu.VMEM, pltpu.VMEM),
    )


def decode(few, preact, maps, target, enc_bias, dec_weight):
    width, channels = dec_weight.shape
    tokens = maps.shape[1]
    latents, rec = call(
        functools.partial(decode_kernel, few),
        (array((tokens, width), BF16), array((tokens, channels), BF16)),
        2 * tokens * channels * width,
        preact,
        maps,
        enc_bias[None],
        dec_weight,
        in_specs=specs(pltpu.VMEM, pltpu.VMEM, pltpu.VMEM, pl.ANY),
        out_specs=specs(pltpu.VMEM, pl.ANY),
        scratch_shapes=[
            pltpu.VMEM(dec_weight.shape, BF16),
            pltpu.VMEM((tokens, channels), BF16),
            pltpu.SemaphoreType.DMA((4,)),
            pltpu.SemaphoreType.DMA((4,)),
        ],
    )
    sizes = sizes_of(NARROW)
    recs = swap_from_far(rec.reshape(-1, *target.shape), NARROW, sizes)
    mixed = call(
        functools.partial(mix_kernel, sizes),
        array(recs.shape, BF16),
        8 * recs.size,
        recs,
        target,
    )
    return latents, swap_from_far(mixed, NARROW, sizes).reshape(tokens, channels)


def latent_parts(few, back, turned_weight, slots):
    return call(
        functools.partial(grad_kernel, few),
        array((lax.axis_size(WIDE), 1 if few else 8, LANES), F32),
        2 * back.size * turned_weight.shape[1],
        back,
        turned_weight,
        slots,
    )


def outer(latents, back):
    shape = (latents.shape[1], back.shape[1])
    return call(
        outer_kernel,
        array(shape, BF16),
        2 * latents.size * back.shape[1],
        latents,
        back,
        out_specs=specs(pl.ANY)[0],
        scratch_shapes=[pltpu.VMEM(shape, BF16), pltpu.SemaphoreType.DMA((4,))],
    )


def own_gradient(few, parts, own, width):
    return call(functools.partial(own_kernel, few), array((CHUNK, width), F32), 1 << 20, parts, own)


def local(activations, enc_weight, enc_bias, dec_weight, dec_bias, active_ids):
    tokens, channels = activations.shape
    width = enc_weight.shape[1]
    group = lax.axis_index(NARROW)
    ids = active_ids.T
    partial, named, slots, base = encode(True, group[None], ids, activations, enc_weight)
    preact = summed_over_wide(partial)
    maps, own, turned_weight = find(named, base, dec_weight)
    rows = tokens // lax.axis_size(NARROW)
    target, needed = call(
        functools.partial(target_kernel, width),
        (array((rows, channels), F32), array((1,), jnp.int32)),
        1 << 24,
        turned(group, sizes_of(NARROW))[None],
        activations,
        dec_bias[None],
        ids,
        in_specs=specs(pltpu.SMEM, pl.ANY, pltpu.VMEM, pltpu.VMEM),
        out_specs=specs(pltpu.VMEM, pltpu.SMEM),
        scratch_shapes=[pltpu.VMEM((rows, channels), BF16), pltpu.SemaphoreType.DMA],
    )
    wide = [lax.axis_size(WIDE)]
    latents, back = decode(True, preact, maps, target, enc_bias, dec_weight)
    parts = swap_from_far(latent_parts(True, back, turned_weight, slots), WIDE, wide)
    dec_grad = outer(latents, back)

    def few():
        return dec_grad, own_gradient(True, parts, own, width)

    def many():
        partial, named, slots, base = encode(False, group[None], ids, activations, enc_weight)
        preact = summed_over_wide(partial)
        maps, own, turned_weight = find(named, base, dec_weight)
        latents, back = decode(False, preact, maps, target, enc_bias, dec_weight)
        parts = swap_from_far(latent_parts(False, back, turned_weight, slots), WIDE, wide)
        return outer(latents, back), own_gradient(False, parts, own, width)

    return lax.cond(needed[0] <= LANES, few, many)


def solution(mesh):
    split = Mesh(mesh.devices.reshape(16, 2, 4, 4), ("wide_0", "wide_1", "narrow_0", "narrow_1"))
    return jax.shard_map(
        local,
        mesh=split,
        in_specs=(P(None, WIDE), P(WIDE, NARROW), P(NARROW), P(NARROW, WIDE), P(WIDE), P()),
        out_specs=(P(NARROW, WIDE), P(WIDE, NARROW)),
        check_vma=False,
    )
```

```python
import functools

import jax
import jax.numpy as jnp
from jax import lax
from jax.experimental import pallas as pl
from jax.experimental.pallas import tpu as pltpu
from jax.sharding import Mesh
from jax.sharding import PartitionSpec as P

NARROW = ("narrow_0", "narrow_1")
WIDE = ("wide_0", "wide_1")
LANES = 128
F32 = jnp.float32
BF16 = jnp.bfloat16
LIMIT = 16 * 1024 * 1024

CHUNK = 16
FEW = 16


def lookup(rows, lanes):
    return jnp.take_along_axis(rows, lanes, axis=1, mode="promise_in_bounds")


def pick_more(picked, rows, first, slots):
    low, high = slots & (LANES - 1), slots >> 7
    for c in range(rows.shape[1] // LANES):
        found = lookup(rows[:, c * LANES : (c + 1) * LANES], low)
        picked = jnp.where(high == first // LANES + c, found, picked)
    return picked


def pack(picked, few):
    picked = picked.reshape(-1, 2, 8, LANES)
    picked = picked[:, 0] + picked[:, 1]
    return jnp.sum(picked, axis=1, keepdims=True) if few else picked


def pick_slots(rows, slots, few):
    return pack(pick_more(jnp.zeros(slots.shape, F32), rows, 0, slots), few)


def unpack_rows(packed, few):
    if few:
        return jnp.broadcast_to(packed, (CHUNK, LANES))
    return jnp.concatenate([packed, packed], axis=0)


def place(values, maps, c, shift=None):
    lanes = (maps[c // 4] >> (8 * (c % 4))) & 255
    placed = lookup(values, (lanes - 1) & (LANES - 1))
    if shift is not None:
        placed = placed + shift
    return jnp.where(lanes > 0, placed, 0.0)


def up_to(counts):
    at = lax.broadcasted_iota(jnp.int32, counts.shape, 1) & (CHUNK - 1)
    for s in (1, 2, 4, 8):
        counts = counts + jnp.where(at >= s, pltpu.roll(counts, s, axis=1), 0)
    return counts


def fill_slots(few, group, width, ids, named, slots, base):
    count, tokens = ids.shape
    lane = lax.broadcasted_iota(jnp.int32, (1, LANES), 1)
    line = lax.broadcasted_iota(jnp.int32, (LANES, LANES), 0)
    within = ids[...] - group * width
    mine = (within >= 0) & (within < width)
    if few:
        entry = lax.broadcasted_iota(jnp.int32, (FEW, tokens), 0)
        earlier = lax.broadcasted_iota(jnp.int32, (count, count), 0) > lax.broadcasted_iota(jnp.int32, (count, count), 1)
        ones = jnp.where(mine, 1.0, 0.0)
        rank = jnp.dot(
            jnp.where(earlier, 1.0, 0.0).astype(BF16), ones.astype(BF16), preferred_element_type=F32
        )
        taken = (rank[count - 1 :] + ones[count - 1 :]).astype(jnp.int32)
        place_of = jnp.where(mine, rank.astype(jnp.int32), FEW)
        held = jnp.full((FEW, tokens), -1, jnp.int32)
        for k in range(count):
            held = jnp.where(entry == place_of[k : k + 1], within[k : k + 1], held)
    else:
        held = jnp.where(mine, within, -1)
    named[...] = held
    for i in range(tokens // LANES):
        cols = pl.ds(i * LANES, LANES)
        block = held[:, i * LANES : (i + 1) * LANES]
        if few:
            counts = jnp.broadcast_to(taken[:, i * LANES : (i + 1) * LANES], (8, LANES))
            first = up_to(counts) - counts
            spread = jnp.full((LANES, LANES), -1, jnp.int32)
            for k in range(FEW):
                at = jnp.where(block[k : k + 1] >= 0, first[:1] + k, -1)
                spread = jnp.where(line == at, block[k : k + 1], spread)
        else:
            first = jnp.broadcast_to(64 * ((lane >> 3) & 1), (8, LANES))
            spread = jnp.concatenate([block, block], axis=0)
            spread = jnp.where(line >> 6 == (lane >> 3) & 1, spread, -1)
        base[:, cols] = first
        slots[cols, :] = spread.T


def target_kernel(width, place_of, act, bias, ids, out, most, here, arrived):
    rows = out.shape[0]
    first = pl.multiple_of(place_of[0] * rows, rows)
    copy = pltpu.make_async_copy(act.at[pl.ds(first, rows)], here, arrived)
    copy.start()
    every = lax.broadcasted_iota(jnp.int32, (16, LANES), 0)
    needed = jnp.zeros((16, LANES), jnp.int32)
    for i in range(ids.shape[1] // LANES):
        owner = ids[:, pl.ds(i * LANES, LANES)] >> (width.bit_length() - 1)
        tally = jnp.zeros((16, LANES), jnp.int32)
        for k in range(ids.shape[0]):
            tally = tally + jnp.where(every == owner[k : k + 1], 1, 0)
        needed = jnp.maximum(needed, jnp.maximum(tally * (LANES // FEW), up_to(tally)))
    most[0] = jnp.max(needed)
    copy.wait()
    out[...] = bias[...] - here[...].astype(F32)


def maps_kernel(owner, named, base, weight, out, own, turned_weight):
    count, tokens = named.shape
    line = lax.broadcasted_iota(jnp.int32, (LANES, LANES), 0)
    for i in range(tokens // LANES):
        cols = pl.ds(i * LANES, LANES)
        start = base[:, cols] + lax.broadcasted_iota(jnp.int32, (8, LANES), 0) + 1

        def body(n, maps):
            first = pl.multiple_of(8 * n, 8)
            eight = named[pl.ds(first, 8), cols]
            block = eight >> 7
            code = (start + first) << (8 * (block & 3))
            low = eight & (LANES - 1)
            codes = [
                jnp.where((block >= 0) & (block < 4), code, 0),
                jnp.where((block >= 4) & (block < 8), code, 0),
            ]
            for k in range(8):
                hit = line == low[k : k + 1]
                maps = [m | jnp.where(hit, f[k : k + 1], 0) for m, f in zip(maps, codes)]
            return tuple(maps)

        zero = jnp.zeros((LANES, LANES), jnp.int32)
        maps = lax.fori_loop(0, count // 8, body, (zero, zero))
        for m in range(2):
            out[m, cols, :] = maps[m].T
    own[...] = out[:, pl.ds(pl.multiple_of(owner[0] * CHUNK, CHUNK), CHUNK), :]
    for r in range(0, weight.shape[0], 256):
        turned_weight[:, pl.ds(r, 256)] = weight[pl.ds(r, 256), :].T


def window_kernel(
    width, owner, named, base, weight, place_of, act, bias, ids, out, own, turned_weight, target, most, *scratch
):
    maps_kernel(owner, named, base, weight, out, own, turned_weight)
    target_kernel(width, place_of, act, bias, ids, target, most, *scratch)


def encode_kernel(
    few, group, ids, act, weight, packed, named, slots, base, act_here, weight_here, picked, arrived
):
    width = weight.shape[1]
    block = width // 4
    copies = [pltpu.make_async_copy(act, act_here, arrived.at[4])]
    for n in range(4):
        cols = pl.ds(n * block, block)
        copies.append(pltpu.make_async_copy(weight.at[:, cols], weight_here.at[:, cols], arrived.at[n]))
    for copy in copies:
        copy.start()
    fill_slots(few, group[0], width, ids, named, slots, base)
    copies[0].wait()
    step = 8 * CHUNK
    for n in range(4):
        copies[n + 1].wait()
        for i in range(act.shape[0] // step):
            rows = pl.ds(i * step, step)
            part = jnp.dot(
                act_here[rows, :], weight_here[:, pl.ds(n * block, block)], preferred_element_type=F32
            )
            sofar = picked[rows, :] if n else jnp.zeros((step, LANES), F32)
            sofar = pick_more(sofar, part, n * block, slots[rows, :])
            if n < 3:
                picked[rows, :] = sofar
            else:
                done = pack(sofar, few)
                depth = 8 * done.shape[1]
                packed[pl.ds(i * depth, depth), :] = done.reshape(depth, LANES)


def decode_kernel(few, packed, maps, bias, weight, latents, rec, weight_here, rec_here, arrived, sent):
    step = 8 * CHUNK
    depth = 1 if few else 8
    steps = latents.shape[0] // step
    part = weight.shape[0] // 4
    coming = [
        pltpu.make_async_copy(weight.at[pl.ds(i * part, part)], weight_here.at[pl.ds(i * part, part)], arrived.at[i])
        for i in range(4)
    ]
    for copy in coming:
        copy.start()

    def fill(i):
        rows = pl.ds(i * step, step)
        chunks = [unpack_rows(packed[pl.ds((8 * i + q) * depth, depth), :], few) for q in range(8)]
        values = jnp.concatenate(chunks, axis=0)
        mine = [maps[0, rows, :], maps[1, rows, :]]
        blocks = [
            place(values, mine, c, bias[:, pl.ds(c * LANES, LANES)]) for c in range(latents.shape[1] // LANES)
        ]
        latents[rows, :] = jnp.concatenate(blocks, axis=1).astype(BF16)

    ahead = 2
    for i in range(ahead):
        fill(i)
    for copy in coming:
        copy.wait()
    going = []
    for i in range(steps):
        rows = pl.ds(i * step, step)
        rec_here[rows, :] = jnp.dot(latents[rows, :], weight_here[...], preferred_element_type=F32).astype(rec.dtype)
        going.append(pltpu.make_async_copy(rec_here.at[rows], rec.at[rows], sent.at[i]))
        going[-1].start()
        if i + ahead < steps:
            fill(i + ahead)
    for copy in going:
        copy.wait()


def mix_kernel(sizes, recs, target, out):
    groups = recs.shape[0]
    at_group = [turned(g, sizes) for g in range(groups)]
    for r in range(0, recs.shape[1], 16):
        for c in range(0, recs.shape[2], LANES):
            at = (pl.ds(r, 16), pl.ds(c, LANES))
            err = target[at]
            errs = []
            for g in range(groups):
                err = err + recs[(at_group[g], *at)].astype(F32)
                errs.append(err)
            suffix = jnp.zeros_like(err)
            for g in reversed(range(groups)):
                suffix = suffix + errs[g]
                out[(at_group[g], *at)] = (suffix * (1.0 / groups)).astype(out.dtype)


def grad_kernel(few, back, turned_weight, slots, out):
    step = 8 * CHUNK
    for i in range(back.shape[0] // step):
        rows = pl.ds(i * step, step)
        part = jnp.dot(back[rows, :], turned_weight[...], preferred_element_type=F32)
        first = (8 * i + out.shape[0] // 2) % out.shape[0]
        out[pl.ds(first, 8)] = pick_slots(part, slots[rows, :], few)


def outer_kernel(latents, back, out, here, sent):
    step = 256
    copies = []
    for i in range(out.shape[0] // step):
        rows = pl.ds(i * step, step)
        part = lax.dot_general(
            latents[:, i * step : (i + 1) * step],
            back[...],
            (((0,), (0,)), ((), ())),
            preferred_element_type=F32,
        )
        here[rows, :] = part.astype(out.dtype)
        copies.append(pltpu.make_async_copy(here.at[rows], out.at[rows], sent.at[i]))
        copies[-1].start()
    for copy in copies:
        copy.wait()


def own_kernel(few, pieces, maps, out):
    values = unpack_rows(jnp.sum(pieces[...], axis=0), few)
    mine = [maps[0], maps[1]]
    for c in range(out.shape[1] // LANES):
        out[:, pl.ds(c * LANES, LANES)] = place(values, mine, c)


def call(kernel, shapes, flops, *args, **params):
    moved = sum(a.size * a.dtype.itemsize for a in (*args, *jax.tree.leaves(shapes)))
    return pl.pallas_call(
        kernel,
        out_shape=shapes,
        compiler_params=pltpu.CompilerParams(vmem_limit_bytes=LIMIT),
        cost_estimate=pl.CostEstimate(flops=flops, bytes_accessed=moved, transcendentals=0),
        **params,
    )(*args)


def array(shape, dtype):
    return jax.ShapeDtypeStruct(shape, dtype)


def turned(place, sizes):
    out, step = 0, 1
    for size in reversed(sizes):
        out = out + (place // step % size + size // 2) % size * step
        step = step * size
    return out


def sizes_of(axes):
    return [lax.axis_size(a) for a in axes]


def swap_from_far(pieces, axes, sizes):
    order = [[turned(i, sizes) for i in range(pieces.shape[0])]]
    return lax.all_to_all(pieces, axes, 0, 0, axis_index_groups=order)


def summed_over_wide(partial):
    ring, core = WIDE
    rows = partial.shape[0] // 2
    both = lax.all_gather(partial, core)
    half = lax.dynamic_slice_in_dim(both, lax.axis_index(core) * rows, rows, 1)
    half = (half[0] + half[1]).astype(BF16)
    size = lax.axis_size(ring)
    pieces = swap_from_far(jnp.broadcast_to(half[None], (size, *half.shape)), ring, [size])
    return lax.all_gather(jnp.sum(pieces.astype(F32), axis=0), core, tiled=True)


def specs(*spaces):
    return [pl.BlockSpec(memory_space=m) for m in spaces]


def encode(few, group, ids, activations, enc_weight):
    tokens, channels = activations.shape
    width = enc_weight.shape[1]
    depth = tokens // CHUNK * (1 if few else 8)
    partial, named, slots, base = call(
        functools.partial(encode_kernel, few),
        (
            array((depth, LANES), F32),
            array((FEW if few else ids.shape[0], tokens), jnp.int32),
            array((tokens, LANES), jnp.int32),
            array((8, tokens), jnp.int32),
        ),
        2 * tokens * channels * width,
        group,
        ids,
        activations,
        enc_weight,
        in_specs=specs(pltpu.SMEM, pltpu.VMEM, pltpu.HBM, pltpu.HBM),
        scratch_shapes=[
            pltpu.VMEM(activations.shape, BF16),
            pltpu.VMEM(enc_weight.shape, BF16),
            pltpu.VMEM((tokens, LANES), F32),
            pltpu.SemaphoreType.DMA((5,)),
        ],
    )
    return partial, named, slots, base


def find(named, base, dec_weight, *rest):
    tokens = named.shape[1]
    width, channels = dec_weight.shape
    shapes = (
        array((2, tokens, LANES), jnp.int32),
        array((2, CHUNK, LANES), jnp.int32),
        array((channels, width), BF16),
    )
    ins, outs = [pltpu.SMEM] + [pltpu.VMEM] * 3, [pltpu.VMEM] * 3
    kernel, scratch = maps_kernel, []
    if rest:
        rows = tokens // lax.axis_size(NARROW)
        shapes += (array((rows, channels), F32), array((1,), jnp.int32))
        ins += [pltpu.SMEM, pltpu.HBM, pltpu.VMEM, pltpu.VMEM]
        outs += [pltpu.VMEM, pltpu.SMEM]
        kernel = functools.partial(window_kernel, width)
        scratch = [pltpu.VMEM((rows, channels), BF16), pltpu.SemaphoreType.DMA]
    return call(
        kernel,
        shapes,
        1 << 26,
        lax.axis_index(WIDE)[None],
        named,
        base,
        dec_weight,
        *rest,
        in_specs=specs(*ins),
        out_specs=specs(*outs),
        scratch_shapes=scratch,
    )


def decode(few, preact, maps, target, enc_bias, dec_weight):
    width, channels = dec_weight.shape
    tokens = maps.shape[1]
    latents, rec = call(
        functools.partial(decode_kernel, few),
        (array((tokens, width), BF16), array((tokens, channels), BF16)),
        2 * tokens * channels * width,
        preact,
        maps,
        enc_bias[None],
        dec_weight,
        in_specs=specs(pltpu.VMEM, pltpu.VMEM, pltpu.VMEM, pltpu.HBM),
        out_specs=specs(pltpu.VMEM, pl.ANY),
        scratch_shapes=[
            pltpu.VMEM(dec_weight.shape, BF16),
            pltpu.VMEM((tokens, channels), BF16),
            pltpu.SemaphoreType.DMA((4,)),
            pltpu.SemaphoreType.DMA((4,)),
        ],
    )
    sizes = sizes_of(NARROW)
    recs = swap_from_far(rec.reshape(-1, *target.shape), NARROW, sizes)
    mixed = call(
        functools.partial(mix_kernel, sizes),
        array(recs.shape, BF16),
        8 * recs.size,
        recs,
        target,
    )
    return latents, swap_from_far(mixed, NARROW, sizes).reshape(tokens, channels)


def latent_parts(few, back, turned_weight, slots):
    return call(
        functools.partial(grad_kernel, few),
        array((lax.axis_size(WIDE), 1 if few else 8, LANES), F32),
        2 * back.size * turned_weight.shape[1],
        back,
        turned_weight,
        slots,
    )


def outer(latents, back):
    shape = (latents.shape[1], back.shape[1])
    return call(
        outer_kernel,
        array(shape, BF16),
        2 * latents.size * back.shape[1],
        latents,
        back,
        out_specs=specs(pl.ANY)[0],
        scratch_shapes=[pltpu.VMEM(shape, BF16), pltpu.SemaphoreType.DMA((4,))],
    )


def own_gradient(few, parts, own, width):
    return call(functools.partial(own_kernel, few), array((CHUNK, width), F32), 1 << 20, parts, own)


def local(activations, enc_weight, enc_bias, dec_weight, dec_bias, active_ids):
    width = enc_weight.shape[1]
    group = lax.axis_index(NARROW)
    ids = active_ids.T
    partial, named, slots, base = encode(True, group[None], ids, activations, enc_weight)
    preact = summed_over_wide(partial)
    place_of = turned(group, sizes_of(NARROW))[None]
    maps, own, turned_weight, target, needed = find(
        named, base, dec_weight, place_of, activations, dec_bias[None], ids
    )
    wide = [lax.axis_size(WIDE)]
    latents, back = decode(True, preact, maps, target, enc_bias, dec_weight)
    parts = swap_from_far(latent_parts(True, back, turned_weight, slots), WIDE, wide)
    dec_grad = outer(latents, back)

    def few():
        return dec_grad, own_gradient(True, parts, own, width)

    def many():
        partial, named, slots, base = encode(False, group[None], ids, activations, enc_weight)
        preact = summed_over_wide(partial)
        maps, own, turned_weight = find(named, base, dec_weight)
        latents, back = decode(False, preact, maps, target, enc_bias, dec_weight)
        parts = swap_from_far(latent_parts(False, back, turned_weight, slots), WIDE, wide)
        return outer(latents, back), own_gradient(False, parts, own, width)

    return lax.cond(needed[0] <= LANES, few, many)


def solution(mesh):
    split = Mesh(mesh.devices.reshape(16, 2, 4, 4), ("wide_0", "wide_1", "narrow_0", "narrow_1"))
    return jax.shard_map(
        local,
        mesh=split,
        in_specs=(P(None, WIDE), P(WIDE, NARROW), P(NARROW), P(NARROW, WIDE), P(WIDE), P()),
        out_specs=(P(NARROW, WIDE), P(WIDE, NARROW)),
        check_vma=False,
    )
```

```python
import functools

import jax
import jax.numpy as jnp
from jax import lax
from jax.experimental import pallas as pl
from jax.experimental.pallas import tpu as pltpu
from jax.sharding import Mesh
from jax.sharding import PartitionSpec as P

NARROW = ("narrow_0", "narrow_1")
WIDE = ("wide_0", "wide_1")
LANES = 128
F32 = jnp.float32
BF16 = jnp.bfloat16
LIMIT = 16 * 1024 * 1024

CHUNK = 16
FEW = 16


def lookup(rows, lanes):
    return jnp.take_along_axis(rows, lanes, axis=1, mode="promise_in_bounds")


def pick_more(picked, rows, first, slots):
    low, high = slots & (LANES - 1), slots >> 7
    for c in range(rows.shape[1] // LANES):
        found = lookup(rows[:, c * LANES : (c + 1) * LANES], low)
        picked = jnp.where(high == first // LANES + c, found, picked)
    return picked


def pack(picked, few):
    picked = picked.reshape(-1, 2, 8, LANES)
    picked = picked[:, 0] + picked[:, 1]
    return jnp.sum(picked, axis=1, keepdims=True) if few else picked


def pick_slots(rows, slots, few):
    return pack(pick_more(jnp.zeros(slots.shape, F32), rows, 0, slots), few)


def unpack_rows(packed, few):
    if few:
        return jnp.broadcast_to(packed, (CHUNK, LANES))
    return jnp.concatenate([packed, packed], axis=0)


def place(values, maps, c, shift=None):
    lanes = (maps[c // 4] >> (8 * (c % 4))) & 255
    placed = lookup(values, (lanes - 1) & (LANES - 1))
    if shift is not None:
        placed = placed + shift
    return jnp.where(lanes > 0, placed, 0.0)


def up_to(counts):
    at = lax.broadcasted_iota(jnp.int32, counts.shape, 1) & (CHUNK - 1)
    for s in (1, 2, 4, 8):
        counts = counts + jnp.where(at >= s, pltpu.roll(counts, s, axis=1), 0)
    return counts


def fill_slots(few, group, width, ids, named, slots, base):
    count, tokens = ids.shape
    lane = lax.broadcasted_iota(jnp.int32, (1, LANES), 1)
    line = lax.broadcasted_iota(jnp.int32, (LANES, LANES), 0)
    within = ids[...] - group * width
    mine = (within >= 0) & (within < width)
    if few:
        entry = lax.broadcasted_iota(jnp.int32, (FEW, tokens), 0)
        earlier = lax.broadcasted_iota(jnp.int32, (count, count), 0) > lax.broadcasted_iota(jnp.int32, (count, count), 1)
        ones = jnp.where(mine, 1.0, 0.0)
        rank = jnp.dot(
            jnp.where(earlier, 1.0, 0.0).astype(BF16), ones.astype(BF16), preferred_element_type=F32
        )
        taken = (rank[count - 1 :] + ones[count - 1 :]).astype(jnp.int32)
        place_of = jnp.where(mine, rank.astype(jnp.int32), FEW)
        held = jnp.full((FEW, tokens), -1, jnp.int32)
        for k in range(count):
            held = jnp.where(entry == place_of[k : k + 1], within[k : k + 1], held)
    else:
        held = jnp.where(mine, within, -1)
    named[...] = held
    for i in range(tokens // LANES):
        cols = pl.ds(i * LANES, LANES)
        block = held[:, i * LANES : (i + 1) * LANES]
        if few:
            counts = jnp.broadcast_to(taken[:, i * LANES : (i + 1) * LANES], (8, LANES))
            first = up_to(counts) - counts
            spread = jnp.full((LANES, LANES), -1, jnp.int32)
            for k in range(FEW):
                at = jnp.where(block[k : k + 1] >= 0, first[:1] + k, -1)
                spread = jnp.where(line == at, block[k : k + 1], spread)
        else:
            first = jnp.broadcast_to(64 * ((lane >> 3) & 1), (8, LANES))
            spread = jnp.concatenate([block, block], axis=0)
            spread = jnp.where(line >> 6 == (lane >> 3) & 1, spread, -1)
        base[:, cols] = first
        slots[cols, :] = spread.T


def count_needed(width, ids, most):
    every = lax.broadcasted_iota(jnp.int32, (16, LANES), 0)
    needed = jnp.zeros((16, LANES), jnp.int32)
    for i in range(ids.shape[1] // LANES):
        owner = ids[:, pl.ds(i * LANES, LANES)] >> (width.bit_length() - 1)
        tally = jnp.zeros((16, LANES), jnp.int32)
        for k in range(ids.shape[0]):
            tally = tally + jnp.where(every == owner[k : k + 1], 1, 0)
        needed = jnp.maximum(needed, jnp.maximum(tally * (LANES // FEW), up_to(tally)))
    most[0] = jnp.max(needed)


def maps_kernel(owner, named, base, weight, out, own, turned_weight):
    count, tokens = named.shape
    line = lax.broadcasted_iota(jnp.int32, (LANES, LANES), 0)
    for i in range(tokens // LANES):
        cols = pl.ds(i * LANES, LANES)
        start = base[:, cols] + lax.broadcasted_iota(jnp.int32, (8, LANES), 0) + 1

        def body(n, maps):
            first = pl.multiple_of(8 * n, 8)
            eight = named[pl.ds(first, 8), cols]
            block = eight >> 7
            code = (start + first) << (8 * (block & 3))
            low = eight & (LANES - 1)
            codes = [
                jnp.where((block >= 0) & (block < 4), code, 0),
                jnp.where((block >= 4) & (block < 8), code, 0),
            ]
            for k in range(8):
                hit = line == low[k : k + 1]
                maps = [m | jnp.where(hit, f[k : k + 1], 0) for m, f in zip(maps, codes)]
            return tuple(maps)

        zero = jnp.zeros((LANES, LANES), jnp.int32)
        maps = lax.fori_loop(0, count // 8, body, (zero, zero))
        for m in range(2):
            out[m, cols, :] = maps[m].T
    own[...] = out[:, pl.ds(pl.multiple_of(owner[0] * CHUNK, CHUNK), CHUNK), :]
    for r in range(0, weight.shape[0], 256):
        turned_weight[:, pl.ds(r, 256)] = weight[pl.ds(r, 256), :].T


def window_kernel(width, owner, named, base, weight, ids, out, own, turned_weight, most):
    maps_kernel(owner, named, base, weight, out, own, turned_weight)
    count_needed(width, ids, most)


def encode_kernel(
    few,
    group,
    place_of,
    ids,
    act,
    weight,
    bias,
    packed,
    named,
    slots,
    base,
    target,
    act_here,
    weight_here,
    picked,
    arrived,
):
    width = weight.shape[1]
    block = width // 4
    pairs = [(act, act_here)]
    for n in range(4):
        cols = pl.ds(n * block, block)
        pairs.append((weight.at[:, cols], weight_here.at[:, cols]))
    copies = [pltpu.make_async_copy(*pair, arrived.at[n]) for n, pair in enumerate(pairs)]
    for copy in copies:
        copy.start()
    fill_slots(few, group[0], width, ids, named, slots, base)
    copies[0].wait()
    step = 8 * CHUNK
    for n in range(4):
        copies[n + 1].wait()
        for i in range(act.shape[0] // step):
            rows = pl.ds(i * step, step)
            part = jnp.dot(
                act_here[rows, :], weight_here[:, pl.ds(n * block, block)], preferred_element_type=F32
            )
            sofar = picked[rows, :] if n else jnp.zeros((step, LANES), F32)
            sofar = pick_more(sofar, part, n * block, slots[rows, :])
            if n < 3:
                picked[rows, :] = sofar
            else:
                done = pack(sofar, few)
                depth = 8 * done.shape[1]
                packed[pl.ds(i * depth, depth), :] = done.reshape(depth, LANES)
    mixed = target.shape[0]
    first = pl.multiple_of(place_of[0] * mixed, mixed)
    target[...] = bias[...] - act_here[pl.ds(first, mixed), :].astype(F32)


def decode_kernel(few, packed, maps, bias, weight, latents, rec, weight_here, arrived):
    step = 8 * CHUNK
    depth = 1 if few else 8
    steps = latents.shape[0] // step
    part = weight.shape[0] // 4
    coming = [
        pltpu.make_async_copy(weight.at[pl.ds(i * part, part)], weight_here.at[pl.ds(i * part, part)], arrived.at[i])
        for i in range(4)
    ]
    for copy in coming:
        copy.start()

    def fill(i):
        rows = pl.ds(i * step, step)
        chunks = [unpack_rows(packed[pl.ds((8 * i + q) * depth, depth), :], few) for q in range(8)]
        values = jnp.concatenate(chunks, axis=0)
        mine = [maps[0, rows, :], maps[1, rows, :]]
        blocks = [
            place(values, mine, c, bias[:, pl.ds(c * LANES, LANES)]) for c in range(latents.shape[1] // LANES)
        ]
        latents[rows, :] = jnp.concatenate(blocks, axis=1).astype(BF16)

    ahead = 2
    for i in range(ahead):
        fill(i)
    for copy in coming:
        copy.wait()
    for i in range(steps):
        rows = pl.ds(i * step, step)
        rec[rows, :] = jnp.dot(latents[rows, :], weight_here[...], preferred_element_type=F32).astype(rec.dtype)
        if i + ahead < steps:
            fill(i + ahead)


def mix_kernel(sizes, recs, target, out):
    groups = recs.shape[0]
    at_group = [turned(g, sizes) for g in range(groups)]
    for r in range(0, recs.shape[1], 16):
        for c in range(0, recs.shape[2], LANES):
            at = (pl.ds(r, 16), pl.ds(c, LANES))
            err = target[at]
            errs = []
            for g in range(groups):
                err = err + recs[(at_group[g], *at)].astype(F32)
                errs.append(err)
            suffix = jnp.zeros_like(err)
            for g in reversed(range(groups)):
                suffix = suffix + errs[g]
                out[(at_group[g], *at)] = (suffix * (1.0 / groups)).astype(out.dtype)


def grad_kernel(few, back, turned_weight, slots, out):
    step = 8 * CHUNK
    for i in range(back.shape[0] // step):
        rows = pl.ds(i * step, step)
        part = jnp.dot(back[rows, :], turned_weight[...], preferred_element_type=F32)
        first = (8 * i + out.shape[0] // 2) % out.shape[0]
        out[pl.ds(first, 8)] = pick_slots(part, slots[rows, :], few)


def outer_kernel(latents, back, out, here, sent):
    step = 256
    copies = []
    for i in range(out.shape[0] // step):
        rows = pl.ds(i * step, step)
        part = lax.dot_general(
            latents[:, i * step : (i + 1) * step],
            back[...],
            (((0,), (0,)), ((), ())),
            preferred_element_type=F32,
        )
        here[rows, :] = part.astype(out.dtype)
        copies.append(pltpu.make_async_copy(here.at[rows], out.at[rows], sent.at[i]))
        copies[-1].start()
    for copy in copies:
        copy.wait()


def own_kernel(few, pieces, maps, out):
    values = unpack_rows(jnp.sum(pieces[...], axis=0), few)
    mine = [maps[0], maps[1]]
    for c in range(out.shape[1] // LANES):
        out[:, pl.ds(c * LANES, LANES)] = place(values, mine, c)


def call(kernel, shapes, flops, *args, **params):
    moved = sum(a.size * a.dtype.itemsize for a in (*args, *jax.tree.leaves(shapes)))
    return pl.pallas_call(
        kernel,
        out_shape=shapes,
        compiler_params=pltpu.CompilerParams(vmem_limit_bytes=LIMIT),
        cost_estimate=pl.CostEstimate(flops=flops, bytes_accessed=moved, transcendentals=0),
        **params,
    )(*args)


def array(shape, dtype):
    return jax.ShapeDtypeStruct(shape, dtype)


def turned(place, sizes):
    out, step = 0, 1
    for size in reversed(sizes):
        out = out + (place // step % size + size // 2) % size * step
        step = step * size
    return out


def sizes_of(axes):
    return [lax.axis_size(a) for a in axes]


def swap_from_far(pieces, axes, sizes):
    order = [[turned(i, sizes) for i in range(pieces.shape[0])]]
    return lax.all_to_all(pieces, axes, 0, 0, axis_index_groups=order)


def summed_over_wide(partial):
    ring, core = WIDE
    rows = partial.shape[0] // 2
    both = lax.all_gather(partial, core)
    half = lax.dynamic_slice_in_dim(both, lax.axis_index(core) * rows, rows, 1)
    half = (half[0] + half[1]).astype(BF16)
    size = lax.axis_size(ring)
    pieces = swap_from_far(jnp.broadcast_to(half[None], (size, *half.shape)), ring, [size])
    return lax.all_gather(jnp.sum(pieces.astype(F32), axis=0), core, tiled=True)


def specs(*spaces):
    return [pl.BlockSpec(memory_space=m) for m in spaces]


def encode(few, ids, activations, enc_weight, dec_bias):
    group = lax.axis_index(NARROW)
    tokens, channels = activations.shape
    width = enc_weight.shape[1]
    depth = tokens // CHUNK * (1 if few else 8)
    return call(
        functools.partial(encode_kernel, few),
        (
            array((depth, LANES), F32),
            array((FEW if few else ids.shape[0], tokens), jnp.int32),
            array((tokens, LANES), jnp.int32),
            array((8, tokens), jnp.int32),
            array((tokens // lax.axis_size(NARROW), channels), F32),
        ),
        2 * tokens * channels * width,
        group[None],
        turned(group, sizes_of(NARROW))[None],
        ids,
        activations,
        enc_weight,
        dec_bias[None],
        in_specs=specs(pltpu.SMEM, pltpu.SMEM, pltpu.VMEM, pl.ANY, pl.ANY, pltpu.VMEM),
        scratch_shapes=[
            pltpu.VMEM(activations.shape, BF16),
            pltpu.VMEM(enc_weight.shape, BF16),
            pltpu.VMEM((tokens, LANES), F32),
            pltpu.SemaphoreType.DMA((5,)),
        ],
    )


def find(named, base, dec_weight, ids=None):
    tokens = named.shape[1]
    width, channels = dec_weight.shape
    shapes = (
        array((2, tokens, LANES), jnp.int32),
        array((2, CHUNK, LANES), jnp.int32),
        array((channels, width), BF16),
    )
    args, outs, kernel = [lax.axis_index(WIDE)[None], named, base, dec_weight], [pltpu.VMEM] * 3, maps_kernel
    if ids is not None:
        args.append(ids)
        shapes += (array((1,), jnp.int32),)
        outs.append(pltpu.SMEM)
        kernel = functools.partial(window_kernel, width)
    ins = [pltpu.SMEM] + [pltpu.VMEM] * (len(args) - 1)
    return call(kernel, shapes, 1 << 26, *args, in_specs=specs(*ins), out_specs=specs(*outs))


def decode(few, preact, maps, target, enc_bias, dec_weight):
    width, channels = dec_weight.shape
    tokens = maps.shape[1]
    latents, rec = call(
        functools.partial(decode_kernel, few),
        (array((tokens, width), BF16), array((tokens, channels), BF16)),
        2 * tokens * channels * width,
        preact,
        maps,
        enc_bias[None],
        dec_weight,
        in_specs=specs(pltpu.VMEM, pltpu.VMEM, pltpu.VMEM, pl.ANY),
        scratch_shapes=[pltpu.VMEM(dec_weight.shape, BF16), pltpu.SemaphoreType.DMA((4,))],
    )
    sizes = sizes_of(NARROW)
    recs = swap_from_far(rec.reshape(-1, *target.shape), NARROW, sizes)
    mixed = call(
        functools.partial(mix_kernel, sizes),
        array(recs.shape, BF16),
        8 * recs.size,
        recs,
        target,
    )
    return latents, swap_from_far(mixed, NARROW, sizes).reshape(tokens, channels)


def latent_parts(few, back, turned_weight, slots):
    return call(
        functools.partial(grad_kernel, few),
        array((lax.axis_size(WIDE), 1 if few else 8, LANES), F32),
        2 * back.size * turned_weight.shape[1],
        back,
        turned_weight,
        slots,
    )


def outer(latents, back):
    shape = (latents.shape[1], back.shape[1])
    return call(
        outer_kernel,
        array(shape, BF16),
        2 * latents.size * back.shape[1],
        latents,
        back,
        out_specs=specs(pl.ANY)[0],
        scratch_shapes=[pltpu.VMEM(shape, BF16), pltpu.SemaphoreType.DMA((4,))],
    )


def own_gradient(few, parts, own, width):
    return call(functools.partial(own_kernel, few), array((CHUNK, width), F32), 1 << 20, parts, own)


def local(activations, enc_weight, enc_bias, dec_weight, dec_bias, active_ids):
    width = enc_weight.shape[1]
    ids = active_ids.T
    partial, named, slots, base, target = encode(True, ids, activations, enc_weight, dec_bias)
    preact = summed_over_wide(partial)
    maps, own, turned_weight, needed = find(named, base, dec_weight, ids)
    wide = [lax.axis_size(WIDE)]
    latents, back = decode(True, preact, maps, target, enc_bias, dec_weight)
    parts = swap_from_far(latent_parts(True, back, turned_weight, slots), WIDE, wide)
    dec_grad = outer(latents, back)

    def few():
        return dec_grad, own_gradient(True, parts, own, width)

    def many():
        no_bias = jnp.zeros_like(dec_bias)
        partial, named, slots, base, _ = encode(False, ids, activations, enc_weight, no_bias)
        preact = summed_over_wide(partial)
        maps, own, turned_weight = find(named, base, dec_weight)
        latents, back = decode(False, preact, maps, target, enc_bias, dec_weight)
        parts = swap_from_far(latent_parts(False, back, turned_weight, slots), WIDE, wide)
        return outer(latents, back), own_gradient(False, parts, own, width)

    return lax.cond(needed[0] <= LANES, few, many)


def solution(mesh):
    split = Mesh(mesh.devices.reshape(16, 2, 4, 4), ("wide_0", "wide_1", "narrow_0", "narrow_1"))
    return jax.shard_map(
        local,
        mesh=split,
        in_specs=(P(None, WIDE), P(WIDE, NARROW), P(NARROW), P(NARROW, WIDE), P(WIDE), P()),
        out_specs=(P(NARROW, WIDE), P(WIDE, NARROW)),
        check_vma=False,
    )
```

```python
import functools

import jax
import jax.numpy as jnp
from jax import lax
from jax.experimental import pallas as pl
from jax.experimental.pallas import tpu as pltpu
from jax.sharding import Mesh
from jax.sharding import PartitionSpec as P

NARROW = ("narrow_0", "narrow_1")
WIDE = ("wide_0", "wide_1")
LANES = 128
F32 = jnp.float32
BF16 = jnp.bfloat16
LIMIT = 16 * 1024 * 1024

CHUNK = 16
FEW = 16


def lookup(rows, lanes):
    return jnp.take_along_axis(rows, lanes, axis=1, mode="promise_in_bounds")


def pick_more(picked, rows, first, slots):
    low, high = slots & (LANES - 1), slots >> 7
    for c in range(rows.shape[1] // LANES):
        found = lookup(rows[:, c * LANES : (c + 1) * LANES], low)
        picked = jnp.where(high == first // LANES + c, found, picked)
    return picked


def pack(picked, few):
    picked = picked.reshape(-1, 2, 8, LANES)
    picked = picked[:, 0] + picked[:, 1]
    return jnp.sum(picked, axis=1, keepdims=True) if few else picked


def pick_slots(rows, slots, few):
    return pack(pick_more(jnp.zeros(slots.shape, F32), rows, 0, slots), few)


def unpack_rows(packed, few):
    if few:
        return jnp.broadcast_to(packed, (CHUNK, LANES))
    return jnp.concatenate([packed, packed], axis=0)


def place(values, maps, c, shift=None):
    lanes = (maps[c // 4] >> (8 * (c % 4))) & 255
    placed = lookup(values, (lanes - 1) & (LANES - 1))
    if shift is not None:
        placed = placed + shift
    return jnp.where(lanes > 0, placed, 0.0)


def up_to(counts):
    at = lax.broadcasted_iota(jnp.int32, counts.shape, 1) & (CHUNK - 1)
    for s in (1, 2, 4, 8):
        counts = counts + jnp.where(at >= s, pltpu.roll(counts, s, axis=1), 0)
    return counts


def fill_slots(few, group, width, ids, named, slots, base):
    count, tokens = ids.shape
    lane = lax.broadcasted_iota(jnp.int32, (1, LANES), 1)
    line = lax.broadcasted_iota(jnp.int32, (LANES, LANES), 0)
    within = ids[...] - group * width
    mine = (within >= 0) & (within < width)
    if few:
        entry = lax.broadcasted_iota(jnp.int32, (FEW, tokens), 0)
        earlier = lax.broadcasted_iota(jnp.int32, (count, count), 0) > lax.broadcasted_iota(jnp.int32, (count, count), 1)
        ones = jnp.where(mine, 1.0, 0.0)
        rank = jnp.dot(
            jnp.where(earlier, 1.0, 0.0).astype(BF16), ones.astype(BF16), preferred_element_type=F32
        )
        taken = (rank[count - 1 :] + ones[count - 1 :]).astype(jnp.int32)
        place_of = jnp.where(mine, rank.astype(jnp.int32), FEW)
        held = jnp.full((FEW, tokens), -1, jnp.int32)
        for k in range(count):
            held = jnp.where(entry == place_of[k : k + 1], within[k : k + 1], held)
    else:
        held = jnp.where(mine, within, -1)
    named[...] = held
    for i in range(tokens // LANES):
        cols = pl.ds(i * LANES, LANES)
        block = held[:, i * LANES : (i + 1) * LANES]
        if few:
            counts = jnp.broadcast_to(taken[:, i * LANES : (i + 1) * LANES], (8, LANES))
            first = up_to(counts) - counts
            spread = jnp.full((LANES, LANES), -1, jnp.int32)
            for k in range(FEW):
                at = jnp.where(block[k : k + 1] >= 0, first[:1] + k, -1)
                spread = jnp.where(line == at, block[k : k + 1], spread)
        else:
            first = jnp.broadcast_to(64 * ((lane >> 3) & 1), (8, LANES))
            spread = jnp.concatenate([block, block], axis=0)
            spread = jnp.where(line >> 6 == (lane >> 3) & 1, spread, -1)
        base[:, cols] = first
        slots[cols, :] = spread.T


def count_needed(width, ids, most):
    every = lax.broadcasted_iota(jnp.int32, (16, LANES), 0)
    needed = jnp.zeros((16, LANES), jnp.int32)
    for i in range(ids.shape[1] // LANES):
        owner = ids[:, pl.ds(i * LANES, LANES)] >> (width.bit_length() - 1)
        tally = jnp.zeros((16, LANES), jnp.int32)
        for k in range(ids.shape[0]):
            tally = tally + jnp.where(every == owner[k : k + 1], 1, 0)
        needed = jnp.maximum(needed, jnp.maximum(tally * (LANES // FEW), up_to(tally)))
    most[0] = jnp.max(needed)


def maps_kernel(owner, named, base, weight, out, own, turned_weight, early):
    count, tokens = named.shape
    line = lax.broadcasted_iota(jnp.int32, (LANES, LANES), 0)
    for i in range(tokens // LANES):
        cols = pl.ds(i * LANES, LANES)
        start = base[:, cols] + lax.broadcasted_iota(jnp.int32, (8, LANES), 0) + 1

        def body(n, maps):
            first = pl.multiple_of(8 * n, 8)
            eight = named[pl.ds(first, 8), cols]
            block = eight >> 7
            code = (start + first) << (8 * (block & 3))
            low = eight & (LANES - 1)
            codes = [
                jnp.where((block >= 0) & (block < 4), code, 0),
                jnp.where((block >= 4) & (block < 8), code, 0),
            ]
            for k in range(8):
                hit = line == low[k : k + 1]
                maps = [m | jnp.where(hit, f[k : k + 1], 0) for m, f in zip(maps, codes)]
            return tuple(maps)

        zero = jnp.zeros((LANES, LANES), jnp.int32)
        maps = lax.fori_loop(0, count // 8, body, (zero, zero))
        for m in range(2):
            out[m, cols, :] = maps[m].T
    early[0] = jnp.where(owner[0] < 2, 1, 0)
    own[...] = out[:, pl.ds(pl.multiple_of(owner[0] * CHUNK, CHUNK), CHUNK), :]
    for r in range(0, weight.shape[0], 256):
        turned_weight[:, pl.ds(r, 256)] = weight[pl.ds(r, 256), :].T


def window_kernel(width, owner, named, base, weight, ids, out, own, turned_weight, early, most):
    maps_kernel(owner, named, base, weight, out, own, turned_weight, early)
    count_needed(width, ids, most)


def encode_kernel(
    few,
    group,
    place_of,
    ids,
    act,
    weight,
    bias,
    packed,
    named,
    slots,
    base,
    target,
    act_here,
    weight_here,
    picked,
    arrived,
):
    depth, width = weight.shape
    half, block = width // 2, depth // 4
    pairs = [(act, act_here)]
    for n in range(8):
        at = (pl.ds(n % 4 * block, block), pl.ds(n // 4 * half, half))
        pairs.append((weight.at[at], weight_here.at[at]))
    copies = [pltpu.make_async_copy(*pair, arrived.at[n]) for n, pair in enumerate(pairs)]
    for copy in copies:
        copy.start()
    fill_slots(few, group[0], width, ids, named, slots, base)
    copies[0].wait()
    step = 8 * CHUNK
    for n in range(2):
        for copy in copies[4 * n + 1 : 4 * n + 5]:
            copy.wait()
        for i in range(act.shape[0] // step):
            rows = pl.ds(i * step, step)
            part = jnp.dot(
                act_here[rows, :], weight_here[:, pl.ds(n * half, half)], preferred_element_type=F32
            )
            sofar = picked[rows, :] if n else jnp.zeros((step, LANES), F32)
            sofar = pick_more(sofar, part, n * half, slots[rows, :])
            if n:
                done = pack(sofar, few)
                lines = 8 * done.shape[1]
                packed[pl.ds(i * lines, lines), :] = done.reshape(lines, LANES)
            else:
                picked[rows, :] = sofar
    mixed = target.shape[0]
    first = pl.multiple_of(place_of[0] * mixed, mixed)
    target[...] = bias[...] - act_here[pl.ds(first, mixed), :].astype(F32)


def decode_kernel(few, packed, maps, bias, weight, latents, rec, weight_here, arrived):
    step = 8 * CHUNK
    depth = 1 if few else 8
    steps = latents.shape[0] // step
    part = weight.shape[0] // 4
    coming = [
        pltpu.make_async_copy(weight.at[pl.ds(i * part, part)], weight_here.at[pl.ds(i * part, part)], arrived.at[i])
        for i in range(4)
    ]
    for copy in coming:
        copy.start()

    def fill(i):
        rows = pl.ds(i * step, step)
        chunks = [unpack_rows(packed[pl.ds((8 * i + q) * depth, depth), :], few) for q in range(8)]
        values = jnp.concatenate(chunks, axis=0)
        mine = [maps[0, rows, :], maps[1, rows, :]]
        blocks = [
            place(values, mine, c, bias[:, pl.ds(c * LANES, LANES)]) for c in range(latents.shape[1] // LANES)
        ]
        latents[rows, :] = jnp.concatenate(blocks, axis=1).astype(BF16)

    ahead = 2
    for i in range(ahead):
        fill(i)
    for copy in coming:
        copy.wait()
    for i in range(steps):
        rows = pl.ds(i * step, step)
        rec[rows, :] = jnp.dot(latents[rows, :], weight_here[...], preferred_element_type=F32).astype(rec.dtype)
        if i + ahead < steps:
            fill(i + ahead)


def mix_kernel(sizes, recs, target, out):
    groups = recs.shape[0]
    at_group = [turned(g, sizes) for g in range(groups)]
    for r in range(0, recs.shape[1], 16):
        for c in range(0, recs.shape[2], LANES):
            at = (pl.ds(r, 16), pl.ds(c, LANES))
            err = target[at]
            errs = []
            for g in range(groups):
                err = err + recs[(at_group[g], *at)].astype(F32)
                errs.append(err)
            suffix = jnp.zeros_like(err)
            for g in reversed(range(groups)):
                suffix = suffix + errs[g]
                out[(at_group[g], *at)] = (suffix * (1.0 / groups)).astype(out.dtype)


def outer_into(latents, back, out, here, sent):
    step = 256
    copies = []
    for i in range(out.shape[0] // step):
        rows = pl.ds(i * step, step)
        part = lax.dot_general(
            latents[:, i * step : (i + 1) * step],
            back[...],
            (((0,), (0,)), ((), ())),
            preferred_element_type=F32,
        )
        here[rows, :] = part.astype(out.dtype)
        copies.append(pltpu.make_async_copy(here.at[rows], out.at[rows], sent.at[i]))
        copies[-1].start()
    for copy in copies:
        copy.wait()


def grad_kernel(few, early, back, turned_weight, slots, latents, grads, out, here, sent):
    step = 8 * CHUNK
    for i in range(back.shape[0] // step):
        rows = pl.ds(i * step, step)
        part = jnp.dot(back[rows, :], turned_weight[...], preferred_element_type=F32)
        first = (8 * i + grads.shape[0] // 2) % grads.shape[0]
        grads[pl.ds(first, 8)] = pick_slots(part, slots[rows, :], few)

    @pl.when(early[0] == 1)
    def _():
        outer_into(latents, back, out, here, sent)


def outer_kernel(early, latents, back, before, out, here, sent):
    @pl.when(early[0] == 0)
    def _():
        outer_into(latents, back, out, here, sent)


def own_kernel(few, pieces, maps, out):
    values = unpack_rows(jnp.sum(pieces[...], axis=0), few)
    mine = [maps[0], maps[1]]
    for c in range(out.shape[1] // LANES):
        out[:, pl.ds(c * LANES, LANES)] = place(values, mine, c)


def call(kernel, shapes, flops, *args, **params):
    moved = sum(a.size * a.dtype.itemsize for a in (*args, *jax.tree.leaves(shapes)))
    return pl.pallas_call(
        kernel,
        out_shape=shapes,
        compiler_params=pltpu.CompilerParams(vmem_limit_bytes=LIMIT),
        cost_estimate=pl.CostEstimate(flops=flops, bytes_accessed=moved, transcendentals=0),
        **params,
    )(*args)


def array(shape, dtype):
    return jax.ShapeDtypeStruct(shape, dtype)


def turned(place, sizes):
    out, step = 0, 1
    for size in reversed(sizes):
        out = out + (place // step % size + size // 2) % size * step
        step = step * size
    return out


def sizes_of(axes):
    return [lax.axis_size(a) for a in axes]


def swap_from_far(pieces, axes, sizes):
    order = [[turned(i, sizes) for i in range(pieces.shape[0])]]
    return lax.all_to_all(pieces, axes, 0, 0, axis_index_groups=order)


def summed_over_wide(partial):
    ring, core = WIDE
    rows = partial.shape[0] // 2
    both = lax.all_gather(partial, core)
    half = lax.dynamic_slice_in_dim(both, lax.axis_index(core) * rows, rows, 1)
    half = (half[0] + half[1]).astype(BF16)
    size = lax.axis_size(ring)
    pieces = swap_from_far(jnp.broadcast_to(half[None], (size, *half.shape)), ring, [size])
    return lax.all_gather(jnp.sum(pieces.astype(F32), axis=0), core, tiled=True)


def specs(*spaces):
    return [pl.BlockSpec(memory_space=m) for m in spaces]


def encode(few, ids, activations, enc_weight, dec_bias):
    group = lax.axis_index(NARROW)
    tokens, channels = activations.shape
    width = enc_weight.shape[1]
    depth = tokens // CHUNK * (1 if few else 8)
    return call(
        functools.partial(encode_kernel, few),
        (
            array((depth, LANES), F32),
            array((FEW if few else ids.shape[0], tokens), jnp.int32),
            array((tokens, LANES), jnp.int32),
            array((8, tokens), jnp.int32),
            array((tokens // lax.axis_size(NARROW), channels), F32),
        ),
        2 * tokens * channels * width,
        group[None],
        turned(group, sizes_of(NARROW))[None],
        ids,
        activations,
        enc_weight,
        dec_bias[None],
        in_specs=specs(pltpu.SMEM, pltpu.SMEM, pltpu.VMEM, pl.ANY, pl.ANY, pltpu.VMEM),
        scratch_shapes=[
            pltpu.VMEM(activations.shape, BF16),
            pltpu.VMEM(enc_weight.shape, BF16),
            pltpu.VMEM((tokens, LANES), F32),
            pltpu.SemaphoreType.DMA((9,)),
        ],
    )


def find(named, base, dec_weight, ids=None):
    tokens = named.shape[1]
    width, channels = dec_weight.shape
    shapes = (
        array((2, tokens, LANES), jnp.int32),
        array((2, CHUNK, LANES), jnp.int32),
        array((channels, width), BF16),
        array((1,), jnp.int32),
    )
    args, kernel = [lax.axis_index(WIDE)[None], named, base, dec_weight], maps_kernel
    outs = [pltpu.VMEM] * 3 + [pltpu.SMEM]
    if ids is not None:
        args.append(ids)
        shapes += (array((1,), jnp.int32),)
        outs.append(pltpu.SMEM)
        kernel = functools.partial(window_kernel, width)
    ins = [pltpu.SMEM] + [pltpu.VMEM] * (len(args) - 1)
    return call(kernel, shapes, 1 << 26, *args, in_specs=specs(*ins), out_specs=specs(*outs))


def decode(few, preact, maps, target, enc_bias, dec_weight):
    width, channels = dec_weight.shape
    tokens = maps.shape[1]
    latents, rec = call(
        functools.partial(decode_kernel, few),
        (array((tokens, width), BF16), array((tokens, channels), BF16)),
        2 * tokens * channels * width,
        preact,
        maps,
        enc_bias[None],
        dec_weight,
        in_specs=specs(pltpu.VMEM, pltpu.VMEM, pltpu.VMEM, pl.ANY),
        scratch_shapes=[pltpu.VMEM(dec_weight.shape, BF16), pltpu.SemaphoreType.DMA((4,))],
    )
    sizes = sizes_of(NARROW)
    recs = swap_from_far(rec.reshape(-1, *target.shape), NARROW, sizes)
    mixed = call(
        functools.partial(mix_kernel, sizes),
        array(recs.shape, BF16),
        8 * recs.size,
        recs,
        target,
    )
    return latents, swap_from_far(mixed, NARROW, sizes).reshape(tokens, channels)


def decoder_side(few, early, back, latents, turned_weight, slots):
    wide, width, channels = lax.axis_size(WIDE), latents.shape[1], back.shape[1]
    scratch = [pltpu.VMEM((width, channels), BF16), pltpu.SemaphoreType.DMA((4,))]
    grads, dec_grad = call(
        functools.partial(grad_kernel, few),
        (array((wide, 1 if few else 8, LANES), F32), array((width, channels), BF16)),
        2 * back.size * width,
        early,
        back,
        turned_weight,
        slots,
        latents,
        in_specs=specs(pltpu.SMEM, pltpu.VMEM, pltpu.VMEM, pltpu.VMEM, pltpu.VMEM),
        out_specs=specs(pltpu.VMEM, pl.ANY),
        scratch_shapes=scratch,
    )
    parts = swap_from_far(grads, WIDE, [wide])
    dec_grad = call(
        outer_kernel,
        array((width, channels), BF16),
        2 * back.size * width,
        early,
        latents,
        back,
        dec_grad,
        in_specs=specs(pltpu.SMEM, pltpu.VMEM, pltpu.VMEM, pl.ANY),
        out_specs=specs(pl.ANY)[0],
        scratch_shapes=scratch,
        input_output_aliases={3: 0},
    )
    return parts, dec_grad


def own_gradient(few, parts, own, width):
    return call(functools.partial(own_kernel, few), array((CHUNK, width), F32), 1 << 20, parts, own)


def local(activations, enc_weight, enc_bias, dec_weight, dec_bias, active_ids):
    width = enc_weight.shape[1]
    ids = active_ids.T
    partial, named, slots, base, target = encode(True, ids, activations, enc_weight, dec_bias)
    preact = summed_over_wide(partial)
    maps, own, turned_weight, early, needed = find(named, base, dec_weight, ids)
    latents, back = decode(True, preact, maps, target, enc_bias, dec_weight)
    parts, dec_grad = decoder_side(True, early, back, latents, turned_weight, slots)

    def few():
        return dec_grad, own_gradient(True, parts, own, width)

    def many():
        no_bias = jnp.zeros_like(dec_bias)
        partial, named, slots, base, _ = encode(False, ids, activations, enc_weight, no_bias)
        preact = summed_over_wide(partial)
        maps, own, turned_weight, early = find(named, base, dec_weight)
        latents, back = decode(False, preact, maps, target, enc_bias, dec_weight)
        parts, dec_grad = decoder_side(False, early, back, latents, turned_weight, slots)
        return dec_grad, own_gradient(False, parts, own, width)

    return lax.cond(needed[0] <= LANES, few, many)


def solution(mesh):
    split = Mesh(mesh.devices.reshape(16, 2, 4, 4), ("wide_0", "wide_1", "narrow_0", "narrow_1"))
    return jax.shard_map(
        local,
        mesh=split,
        in_specs=(P(None, WIDE), P(WIDE, NARROW), P(NARROW), P(NARROW, WIDE), P(WIDE), P()),
        out_specs=(P(NARROW, WIDE), P(WIDE, NARROW)),
        check_vma=False,
    )
```

```python
import functools

import jax
import jax.numpy as jnp
from jax import lax
from jax.experimental import pallas as pl
from jax.experimental.pallas import tpu as pltpu
from jax.sharding import Mesh
from jax.sharding import PartitionSpec as P

NARROW = ("narrow_0", "narrow_1")
WIDE = ("wide_0", "wide_1")
LANES = 128
F32 = jnp.float32
BF16 = jnp.bfloat16
LIMIT = 16 * 1024 * 1024

CHUNK = 16
FEW = 16


def lookup(rows, lanes):
    return jnp.take_along_axis(rows, lanes, axis=1, mode="promise_in_bounds")


def pick_more(picked, rows, first, slots):
    low, high = slots & (LANES - 1), slots >> 7
    for c in range(rows.shape[1] // LANES):
        found = lookup(rows[:, c * LANES : (c + 1) * LANES], low)
        picked = jnp.where(high == first // LANES + c, found, picked)
    return picked


def pack(picked, few):
    picked = picked.reshape(-1, 2, 8, LANES)
    picked = picked[:, 0] + picked[:, 1]
    return jnp.sum(picked, axis=1, keepdims=True) if few else picked


def pick_slots(rows, slots, few):
    return pack(pick_more(jnp.zeros(slots.shape, F32), rows, 0, slots), few)


def unpack_rows(packed, few):
    if few:
        return jnp.broadcast_to(packed, (CHUNK, LANES))
    return jnp.concatenate([packed, packed], axis=0)


def place(values, maps, c, shift=None):
    lanes = (maps[c // 4] >> (8 * (c % 4))) & 255
    placed = lookup(values, (lanes - 1) & (LANES - 1))
    if shift is not None:
        placed = placed + shift
    return jnp.where(lanes > 0, placed, 0.0)


def up_to(counts):
    at = lax.broadcasted_iota(jnp.int32, counts.shape, 1) & (CHUNK - 1)
    for s in (1, 2, 4, 8):
        counts = counts + jnp.where(at >= s, pltpu.roll(counts, s, axis=1), 0)
    return counts


def fill_slots(few, group, width, ids, named, slots, base):
    count, tokens = ids.shape
    lane = lax.broadcasted_iota(jnp.int32, (1, LANES), 1)
    line = lax.broadcasted_iota(jnp.int32, (LANES, LANES), 0)
    within = ids[...] - group * width
    mine = (within >= 0) & (within < width)
    if few:
        entry = lax.broadcasted_iota(jnp.int32, (FEW, tokens), 0)
        earlier = lax.broadcasted_iota(jnp.int32, (count, count), 0) > lax.broadcasted_iota(jnp.int32, (count, count), 1)
        ones = jnp.where(mine, 1.0, 0.0)
        rank = jnp.dot(
            jnp.where(earlier, 1.0, 0.0).astype(BF16), ones.astype(BF16), preferred_element_type=F32
        )
        taken = (rank[count - 1 :] + ones[count - 1 :]).astype(jnp.int32)
        place_of = jnp.where(mine, rank.astype(jnp.int32), FEW)
        held = jnp.full((FEW, tokens), -1, jnp.int32)
        for k in range(count):
            held = jnp.where(entry == place_of[k : k + 1], within[k : k + 1], held)
    else:
        held = jnp.where(mine, within, -1)
    named[...] = held
    for i in range(tokens // LANES):
        cols = pl.ds(i * LANES, LANES)
        block = held[:, i * LANES : (i + 1) * LANES]
        if few:
            counts = jnp.broadcast_to(taken[:, i * LANES : (i + 1) * LANES], (8, LANES))
            first = up_to(counts) - counts
            spread = jnp.full((LANES, LANES), -1, jnp.int32)
            for k in range(FEW):
                at = jnp.where(block[k : k + 1] >= 0, first[:1] + k, -1)
                spread = jnp.where(line == at, block[k : k + 1], spread)
        else:
            first = jnp.broadcast_to(64 * ((lane >> 3) & 1), (8, LANES))
            spread = jnp.concatenate([block, block], axis=0)
            spread = jnp.where(line >> 6 == (lane >> 3) & 1, spread, -1)
        base[:, cols] = first
        slots[cols, :] = spread.T


def count_needed(width, ids, most):
    every = lax.broadcasted_iota(jnp.int32, (16, LANES), 0)
    needed = jnp.zeros((16, LANES), jnp.int32)
    for i in range(ids.shape[1] // LANES):
        owner = ids[:, pl.ds(i * LANES, LANES)] >> (width.bit_length() - 1)
        tally = jnp.zeros((16, LANES), jnp.int32)
        for k in range(ids.shape[0]):
            tally = tally + jnp.where(every == owner[k : k + 1], 1, 0)
        needed = jnp.maximum(needed, jnp.maximum(tally * (LANES // FEW), up_to(tally)))
    most[0] = jnp.max(needed)


def maps_kernel(owner, named, base, weight, out, own, turned_weight):
    count, tokens = named.shape
    line = lax.broadcasted_iota(jnp.int32, (LANES, LANES), 0)
    for i in range(tokens // LANES):
        cols = pl.ds(i * LANES, LANES)
        start = base[:, cols] + lax.broadcasted_iota(jnp.int32, (8, LANES), 0) + 1

        def body(n, maps):
            first = pl.multiple_of(8 * n, 8)
            eight = named[pl.ds(first, 8), cols]
            block = eight >> 7
            code = (start + first) << (8 * (block & 3))
            low = eight & (LANES - 1)
            codes = [
                jnp.where((block >= 0) & (block < 4), code, 0),
                jnp.where((block >= 4) & (block < 8), code, 0),
            ]
            for k in range(8):
                hit = line == low[k : k + 1]
                maps = [m | jnp.where(hit, f[k : k + 1], 0) for m, f in zip(maps, codes)]
            return tuple(maps)

        zero = jnp.zeros((LANES, LANES), jnp.int32)
        maps = lax.fori_loop(0, count // 8, body, (zero, zero))
        for m in range(2):
            out[m, cols, :] = maps[m].T
    own[...] = out[:, pl.ds(pl.multiple_of(owner[0] * CHUNK, CHUNK), CHUNK), :]
    for r in range(0, weight.shape[0], 256):
        turned_weight[:, pl.ds(r, 256)] = weight[pl.ds(r, 256), :].T


def window_kernel(width, owner, named, base, weight, ids, out, own, turned_weight, most):
    maps_kernel(owner, named, base, weight, out, own, turned_weight)
    count_needed(width, ids, most)


def encode_kernel(
    few,
    group,
    place_of,
    ids,
    act,
    weight,
    bias,
    packed,
    named,
    slots,
    base,
    target,
    act_here,
    weight_here,
    picked,
    arrived,
):
    depth, width = weight.shape
    half, block = width // 2, depth // 4
    pairs = [(act, act_here)]
    for n in range(8):
        at = (pl.ds(n % 4 * block, block), pl.ds(n // 4 * half, half))
        pairs.append((weight.at[at], weight_here.at[at]))
    copies = [pltpu.make_async_copy(*pair, arrived.at[n]) for n, pair in enumerate(pairs)]
    for copy in copies:
        copy.start()
    fill_slots(few, group[0], width, ids, named, slots, base)
    copies[0].wait()
    step = 8 * CHUNK
    for n in range(2):
        for copy in copies[4 * n + 1 : 4 * n + 5]:
            copy.wait()
        for i in range(act.shape[0] // step):
            rows = pl.ds(i * step, step)
            part = jnp.dot(
                act_here[rows, :], weight_here[:, pl.ds(n * half, half)], preferred_element_type=F32
            )
            sofar = picked[rows, :] if n else jnp.zeros((step, LANES), F32)
            sofar = pick_more(sofar, part, n * half, slots[rows, :])
            if n:
                done = pack(sofar, few)
                lines = 8 * done.shape[1]
                packed[pl.ds(i * lines, lines), :] = done.reshape(lines, LANES)
            else:
                picked[rows, :] = sofar
    mixed = target.shape[0]
    first = pl.multiple_of(place_of[0] * mixed, mixed)
    target[...] = bias[...] - act_here[pl.ds(first, mixed), :].astype(F32)


def decode_kernel(few, packed, maps, bias, weight, latents, rec, weight_here, arrived):
    step = 8 * CHUNK
    depth = 1 if few else 8
    steps = latents.shape[0] // step
    part = weight.shape[0] // 4
    coming = [
        pltpu.make_async_copy(weight.at[pl.ds(i * part, part)], weight_here.at[pl.ds(i * part, part)], arrived.at[i])
        for i in range(4)
    ]
    for copy in coming:
        copy.start()

    def fill(i):
        rows = pl.ds(i * step, step)
        chunks = [unpack_rows(packed[pl.ds((8 * i + q) * depth, depth), :], few) for q in range(8)]
        values = jnp.concatenate(chunks, axis=0)
        mine = [maps[0, rows, :], maps[1, rows, :]]
        blocks = [
            place(values, mine, c, bias[:, pl.ds(c * LANES, LANES)]) for c in range(latents.shape[1] // LANES)
        ]
        latents[rows, :] = jnp.concatenate(blocks, axis=1).astype(BF16)

    ahead = 2
    for i in range(ahead):
        fill(i)
    for copy in coming:
        copy.wait()
    for i in range(steps):
        rows = pl.ds(i * step, step)
        rec[rows, :] = jnp.dot(latents[rows, :], weight_here[...], preferred_element_type=F32).astype(rec.dtype)
        if i + ahead < steps:
            fill(i + ahead)


def mix_kernel(sizes, recs, target, out):
    groups = recs.shape[0]
    at_group = [turned(g, sizes) for g in range(groups)]
    for r in range(0, recs.shape[1], 16):
        for c in range(0, recs.shape[2], LANES):
            at = (pl.ds(r, 16), pl.ds(c, LANES))
            err = target[at]
            errs = []
            for g in range(groups):
                err = err + recs[(at_group[g], *at)].astype(F32)
                errs.append(err)
            suffix = jnp.zeros_like(err)
            for g in reversed(range(groups)):
                suffix = suffix + errs[g]
                out[(at_group[g], *at)] = (suffix * (1.0 / groups)).astype(out.dtype)


def grad_kernel(few, back, turned_weight, slots, out):
    step = 8 * CHUNK
    for i in range(back.shape[0] // step):
        rows = pl.ds(i * step, step)
        part = jnp.dot(back[rows, :], turned_weight[...], preferred_element_type=F32)
        first = (8 * i + out.shape[0] // 2) % out.shape[0]
        out[pl.ds(first, 8)] = pick_slots(part, slots[rows, :], few)


def outer_kernel(latents, back, out, here, sent):
    step = 256
    copies = []
    for i in range(out.shape[0] // step):
        rows = pl.ds(i * step, step)
        part = lax.dot_general(
            latents[:, i * step : (i + 1) * step],
            back[...],
            (((0,), (0,)), ((), ())),
            preferred_element_type=F32,
        )
        here[rows, :] = part.astype(out.dtype)
        copies.append(pltpu.make_async_copy(here.at[rows], out.at[rows], sent.at[i]))
        copies[-1].start()
    for copy in copies:
        copy.wait()


def own_kernel(few, pieces, maps, out):
    values = unpack_rows(jnp.sum(pieces[...], axis=0), few)
    mine = [maps[0], maps[1]]
    for c in range(out.shape[1] // LANES):
        out[:, pl.ds(c * LANES, LANES)] = place(values, mine, c)


def call(kernel, shapes, flops, *args, **params):
    moved = sum(a.size * a.dtype.itemsize for a in (*args, *jax.tree.leaves(shapes)))
    return pl.pallas_call(
        kernel,
        out_shape=shapes,
        compiler_params=pltpu.CompilerParams(vmem_limit_bytes=LIMIT),
        cost_estimate=pl.CostEstimate(flops=flops, bytes_accessed=moved, transcendentals=0),
        **params,
    )(*args)


def array(shape, dtype):
    return jax.ShapeDtypeStruct(shape, dtype)


def turned(place, sizes):
    out, step = 0, 1
    for size in reversed(sizes):
        out = out + (place // step % size + size // 2) % size * step
        step = step * size
    return out


def sizes_of(axes):
    return [lax.axis_size(a) for a in axes]


def swap_from_far(pieces, axes, sizes):
    order = [[turned(i, sizes) for i in range(pieces.shape[0])]]
    return lax.all_to_all(pieces, axes, 0, 0, axis_index_groups=order)


def summed_over_wide(partial):
    ring, core = WIDE
    rows = partial.shape[0] // 2
    both = lax.all_gather(partial, core)
    half = lax.dynamic_slice_in_dim(both, lax.axis_index(core) * rows, rows, 1)
    half = (half[0] + half[1]).astype(BF16)
    size = lax.axis_size(ring)
    pieces = swap_from_far(jnp.broadcast_to(half[None], (size, *half.shape)), ring, [size])
    return lax.all_gather(jnp.sum(pieces.astype(F32), axis=0), core, tiled=True)


def specs(*spaces):
    return [pl.BlockSpec(memory_space=m) for m in spaces]


def encode(few, ids, activations, enc_weight, dec_bias):
    group = lax.axis_index(NARROW)
    tokens, channels = activations.shape
    width = enc_weight.shape[1]
    depth = tokens // CHUNK * (1 if few else 8)
    return call(
        functools.partial(encode_kernel, few),
        (
            array((depth, LANES), F32),
            array((FEW if few else ids.shape[0], tokens), jnp.int32),
            array((tokens, LANES), jnp.int32),
            array((8, tokens), jnp.int32),
            array((tokens // lax.axis_size(NARROW), channels), F32),
        ),
        2 * tokens * channels * width,
        group[None],
        turned(group, sizes_of(NARROW))[None],
        ids,
        activations,
        enc_weight,
        dec_bias[None],
        in_specs=specs(pltpu.SMEM, pltpu.SMEM, pltpu.VMEM, pl.ANY, pl.ANY, pltpu.VMEM),
        scratch_shapes=[
            pltpu.VMEM(activations.shape, BF16),
            pltpu.VMEM(enc_weight.shape, BF16),
            pltpu.VMEM((tokens, LANES), F32),
            pltpu.SemaphoreType.DMA((9,)),
        ],
    )


def find(named, base, dec_weight, ids=None):
    tokens = named.shape[1]
    width, channels = dec_weight.shape
    shapes = (
        array((2, tokens, LANES), jnp.int32),
        array((2, CHUNK, LANES), jnp.int32),
        array((channels, width), BF16),
    )
    args, outs, kernel = [lax.axis_index(WIDE)[None], named, base, dec_weight], [pltpu.VMEM] * 3, maps_kernel
    if ids is not None:
        args.append(ids)
        shapes += (array((1,), jnp.int32),)
        outs.append(pltpu.SMEM)
        kernel = functools.partial(window_kernel, width)
    ins = [pltpu.SMEM] + [pltpu.VMEM] * (len(args) - 1)
    return call(kernel, shapes, 1 << 26, *args, in_specs=specs(*ins), out_specs=specs(*outs))


def decode(few, preact, maps, target, enc_bias, dec_weight):
    width, channels = dec_weight.shape
    tokens = maps.shape[1]
    latents, rec = call(
        functools.partial(decode_kernel, few),
        (array((tokens, width), BF16), array((tokens, channels), BF16)),
        2 * tokens * channels * width,
        preact,
        maps,
        enc_bias[None],
        dec_weight,
        in_specs=specs(pltpu.VMEM, pltpu.VMEM, pltpu.VMEM, pl.ANY),
        scratch_shapes=[pltpu.VMEM(dec_weight.shape, BF16), pltpu.SemaphoreType.DMA((4,))],
    )
    sizes = sizes_of(NARROW)
    recs = swap_from_far(rec.reshape(-1, *target.shape), NARROW, sizes)
    mixed = call(
        functools.partial(mix_kernel, sizes),
        array(recs.shape, BF16),
        8 * recs.size,
        recs,
        target,
    )
    return latents, swap_from_far(mixed, NARROW, sizes).reshape(tokens, channels)


def latent_parts(few, back, turned_weight, slots):
    return call(
        functools.partial(grad_kernel, few),
        array((lax.axis_size(WIDE), 1 if few else 8, LANES), F32),
        2 * back.size * turned_weight.shape[1],
        back,
        turned_weight,
        slots,
    )


def outer(latents, back):
    shape = (latents.shape[1], back.shape[1])
    return call(
        outer_kernel,
        array(shape, BF16),
        2 * latents.size * back.shape[1],
        latents,
        back,
        out_specs=specs(pl.ANY)[0],
        scratch_shapes=[pltpu.VMEM(shape, BF16), pltpu.SemaphoreType.DMA((4,))],
    )


def own_gradient(few, parts, own, width):
    return call(functools.partial(own_kernel, few), array((CHUNK, width), F32), 1 << 20, parts, own)


def local(activations, enc_weight, enc_bias, dec_weight, dec_bias, active_ids):
    width = enc_weight.shape[1]
    ids = active_ids.T
    partial, named, slots, base, target = encode(True, ids, activations, enc_weight, dec_bias)
    preact = summed_over_wide(partial)
    maps, own, turned_weight, needed = find(named, base, dec_weight, ids)
    wide = [lax.axis_size(WIDE)]
    latents, back = decode(True, preact, maps, target, enc_bias, dec_weight)
    parts = swap_from_far(latent_parts(True, back, turned_weight, slots), WIDE, wide)
    dec_grad = outer(latents, back)

    def few():
        return dec_grad, own_gradient(True, parts, own, width)

    def many():
        no_bias = jnp.zeros_like(dec_bias)
        partial, named, slots, base, _ = encode(False, ids, activations, enc_weight, no_bias)
        preact = summed_over_wide(partial)
        maps, own, turned_weight = find(named, base, dec_weight)
        latents, back = decode(False, preact, maps, target, enc_bias, dec_weight)
        parts = swap_from_far(latent_parts(False, back, turned_weight, slots), WIDE, wide)
        return outer(latents, back), own_gradient(False, parts, own, width)

    return lax.cond(needed[0] <= LANES, few, many)


def solution(mesh):
    split = Mesh(mesh.devices.reshape(16, 2, 4, 4), ("wide_0", "wide_1", "narrow_0", "narrow_1"))
    return jax.shard_map(
        local,
        mesh=split,
        in_specs=(P(None, WIDE), P(WIDE, NARROW), P(NARROW), P(NARROW, WIDE), P(WIDE), P()),
        out_specs=(P(NARROW, WIDE), P(WIDE, NARROW)),
        check_vma=False,
    )
```

```python
import functools

import jax
import jax.numpy as jnp
from jax import lax
from jax.experimental import pallas as pl
from jax.experimental.pallas import tpu as pltpu
from jax.sharding import Mesh
from jax.sharding import PartitionSpec as P

NARROW = ("narrow_0", "narrow_1")
WIDE = ("wide_0", "wide_1")
LANES = 128
F32 = jnp.float32
BF16 = jnp.bfloat16
LIMIT = 16 * 1024 * 1024

CHUNK = 16
FEW = 16


def lookup(rows, lanes):
    return jnp.take_along_axis(rows, lanes, axis=1, mode="promise_in_bounds")


def pick_more(picked, rows, first, slots):
    low, high = slots & (LANES - 1), slots >> 7
    for c in range(rows.shape[1] // LANES):
        found = lookup(rows[:, c * LANES : (c + 1) * LANES], low)
        picked = jnp.where(high == first // LANES + c, found, picked)
    return picked


def pack(picked, few):
    picked = picked.reshape(-1, 2, 8, LANES)
    picked = picked[:, 0] + picked[:, 1]
    return jnp.sum(picked, axis=1, keepdims=True) if few else picked


def pick_slots(rows, slots, few):
    return pack(pick_more(jnp.zeros(slots.shape, F32), rows, 0, slots), few)


def unpack_rows(packed, few):
    if few:
        return jnp.broadcast_to(packed, (CHUNK, LANES))
    return jnp.concatenate([packed, packed], axis=0)


def place(values, maps, c, shift=None):
    lanes = (maps[c // 4] >> (8 * (c % 4))) & 255
    placed = lookup(values, (lanes - 1) & (LANES - 1))
    if shift is not None:
        placed = placed + shift
    return jnp.where(lanes > 0, placed, 0.0)


def up_to(counts):
    at = lax.broadcasted_iota(jnp.int32, counts.shape, 1) & (CHUNK - 1)
    for s in (1, 2, 4, 8):
        counts = counts + jnp.where(at >= s, pltpu.roll(counts, s, axis=1), 0)
    return counts


def fill_slots(few, group, width, ids, named, slots, base):
    count, tokens = ids.shape
    lane = lax.broadcasted_iota(jnp.int32, (1, LANES), 1)
    line = lax.broadcasted_iota(jnp.int32, (LANES, LANES), 0)
    within = ids[...] - group * width
    mine = (within >= 0) & (within < width)
    if few:
        entry = lax.broadcasted_iota(jnp.int32, (FEW, tokens), 0)
        earlier = lax.broadcasted_iota(jnp.int32, (count, count), 0) > lax.broadcasted_iota(jnp.int32, (count, count), 1)
        ones = jnp.where(mine, 1.0, 0.0)
        rank = jnp.dot(
            jnp.where(earlier, 1.0, 0.0).astype(BF16), ones.astype(BF16), preferred_element_type=F32
        )
        taken = (rank[count - 1 :] + ones[count - 1 :]).astype(jnp.int32)
        place_of = jnp.where(mine, rank.astype(jnp.int32), FEW)
        held = jnp.full((FEW, tokens), -1, jnp.int32)
        for k in range(count):
            held = jnp.where(entry == place_of[k : k + 1], within[k : k + 1], held)
    else:
        held = jnp.where(mine, within, -1)
    named[...] = held
    for i in range(tokens // LANES):
        cols = pl.ds(i * LANES, LANES)
        block = held[:, i * LANES : (i + 1) * LANES]
        if few:
            counts = jnp.broadcast_to(taken[:, i * LANES : (i + 1) * LANES], (8, LANES))
            first = up_to(counts) - counts
            spread = jnp.full((LANES, LANES), -1, jnp.int32)
            for k in range(FEW):
                at = jnp.where(block[k : k + 1] >= 0, first[:1] + k, -1)
                spread = jnp.where(line == at, block[k : k + 1], spread)
        else:
            first = jnp.broadcast_to(64 * ((lane >> 3) & 1), (8, LANES))
            spread = jnp.concatenate([block, block], axis=0)
            spread = jnp.where(line >> 6 == (lane >> 3) & 1, spread, -1)
        base[:, cols] = first
        slots[cols, :] = spread.T


def count_needed(width, ids, most):
    every = lax.broadcasted_iota(jnp.int32, (16, LANES), 0)
    needed = jnp.zeros((16, LANES), jnp.int32)
    for i in range(ids.shape[1] // LANES):
        owner = ids[:, pl.ds(i * LANES, LANES)] >> (width.bit_length() - 1)
        tally = jnp.zeros((16, LANES), jnp.int32)
        for k in range(ids.shape[0]):
            tally = tally + jnp.where(every == owner[k : k + 1], 1, 0)
        needed = jnp.maximum(needed, jnp.maximum(tally * (LANES // FEW), up_to(tally)))
    most[0] = jnp.max(needed)


def maps_kernel(owner, named, base, weight, out, own, turned_weight):
    count, tokens = named.shape
    line = lax.broadcasted_iota(jnp.int32, (LANES, LANES), 0)
    for i in range(tokens // LANES):
        cols = pl.ds(i * LANES, LANES)
        start = base[:, cols] + lax.broadcasted_iota(jnp.int32, (8, LANES), 0) + 1

        def body(n, maps):
            first = pl.multiple_of(8 * n, 8)
            eight = named[pl.ds(first, 8), cols]
            block = eight >> 7
            code = (start + first) << (8 * (block & 3))
            low = eight & (LANES - 1)
            codes = [
                jnp.where((block >= 0) & (block < 4), code, 0),
                jnp.where((block >= 4) & (block < 8), code, 0),
            ]
            for k in range(8):
                hit = line == low[k : k + 1]
                maps = [m | jnp.where(hit, f[k : k + 1], 0) for m, f in zip(maps, codes)]
            return tuple(maps)

        zero = jnp.zeros((LANES, LANES), jnp.int32)
        maps = lax.fori_loop(0, count // 8, body, (zero, zero))
        for m in range(2):
            out[m, cols, :] = maps[m].T
    own[...] = out[:, pl.ds(pl.multiple_of(owner[0] * CHUNK, CHUNK), CHUNK), :]
    for r in range(0, weight.shape[0], 256):
        turned_weight[:, pl.ds(r, 256)] = weight[pl.ds(r, 256), :].T


def window_kernel(width, owner, named, base, weight, ids, out, own, turned_weight, most):
    maps_kernel(owner, named, base, weight, out, own, turned_weight)
    count_needed(width, ids, most)


def encode_kernel(
    few,
    group,
    place_of,
    ids,
    act,
    weight,
    bias,
    packed,
    named,
    slots,
    base,
    target,
    act_here,
    weight_here,
    picked,
    arrived,
):
    depth, width = weight.shape
    half, block = width // 2, depth // 4
    pairs = [(act, act_here)]
    for n in range(8):
        at = (pl.ds(n % 4 * block, block), pl.ds(n // 4 * half, half))
        pairs.append((weight.at[at], weight_here.at[at]))
    copies = [pltpu.make_async_copy(*pair, arrived.at[n]) for n, pair in enumerate(pairs)]
    for copy in copies:
        copy.start()
    fill_slots(few, group[0], width, ids, named, slots, base)
    copies[0].wait()
    step = 8 * CHUNK
    for n in range(2):
        for copy in copies[4 * n + 1 : 4 * n + 5]:
            copy.wait()
        for i in range(act.shape[0] // step):
            rows = pl.ds(i * step, step)
            part = jnp.dot(
                act_here[rows, :], weight_here[:, pl.ds(n * half, half)], preferred_element_type=F32
            )
            sofar = picked[rows, :] if n else jnp.zeros((step, LANES), F32)
            sofar = pick_more(sofar, part, n * half, slots[rows, :])
            if n:
                done = pack(sofar, few)
                lines = 8 * done.shape[1]
                packed[pl.ds(i * lines, lines), :] = done.reshape(lines, LANES)
            else:
                picked[rows, :] = sofar
    mixed = target.shape[0]
    first = pl.multiple_of(place_of[0] * mixed, mixed)
    target[...] = bias[...] - act_here[pl.ds(first, mixed), :].astype(F32)


def decode_kernel(few, packed, maps, bias, weight, latents, rec, weight_here, arrived):
    step = 8 * CHUNK
    depth = 1 if few else 8
    steps = latents.shape[0] // step
    part = weight.shape[0] // 4
    coming = [
        pltpu.make_async_copy(weight.at[pl.ds(i * part, part)], weight_here.at[pl.ds(i * part, part)], arrived.at[i])
        for i in range(4)
    ]
    for copy in coming:
        copy.start()

    def fill(i):
        rows = pl.ds(i * step, step)
        chunks = [unpack_rows(packed[pl.ds((8 * i + q) * depth, depth), :], few) for q in range(8)]
        values = jnp.concatenate(chunks, axis=0)
        mine = [maps[0, rows, :], maps[1, rows, :]]
        blocks = [
            place(values, mine, c, bias[:, pl.ds(c * LANES, LANES)]) for c in range(latents.shape[1] // LANES)
        ]
        latents[rows, :] = jnp.concatenate(blocks, axis=1).astype(BF16)

    ahead = 2
    for i in range(ahead):
        fill(i)
    for copy in coming:
        copy.wait()
    for i in range(steps):
        rows = pl.ds(i * step, step)
        rec[rows, :] = jnp.dot(latents[rows, :], weight_here[...], preferred_element_type=F32).astype(rec.dtype)
        if i + ahead < steps:
            fill(i + ahead)


def mix_kernel(sizes, recs, target, out):
    groups = recs.shape[0]
    at_group = [turned(g, sizes) for g in range(groups)]
    for r in range(0, recs.shape[1], 16):
        for c in range(0, recs.shape[2], LANES):
            at = (pl.ds(r, 16), pl.ds(c, LANES))
            err = target[at]
            errs = []
            for g in range(groups):
                err = err + recs[(at_group[g], *at)].astype(F32)
                errs.append(err)
            suffix = jnp.zeros_like(err)
            for g in reversed(range(groups)):
                suffix = suffix + errs[g]
                out[(at_group[g], *at)] = (suffix * (1.0 / groups)).astype(out.dtype)


def grad_kernel(few, back, turned_weight, slots, out):
    step = 8 * CHUNK
    for i in range(back.shape[0] // step):
        rows = pl.ds(i * step, step)
        part = jnp.dot(back[rows, :], turned_weight[...], preferred_element_type=F32)
        first = (8 * i + out.shape[0] // 2) % out.shape[0]
        out[pl.ds(first, 8)] = pick_slots(part, slots[rows, :], few)


def outer_kernel(latents, back, out, here, sent):
    step = 256
    copies = []
    for i in range(out.shape[0] // step):
        rows = pl.ds(i * step, step)
        part = lax.dot_general(
            latents[:, i * step : (i + 1) * step],
            back[...],
            (((0,), (0,)), ((), ())),
            preferred_element_type=F32,
        )
        here[rows, :] = part.astype(out.dtype)
        copies.append(pltpu.make_async_copy(here.at[rows], out.at[rows], sent.at[i]))
        copies[-1].start()
    for copy in copies:
        copy.wait()


def own_kernel(few, pieces, maps, out):
    values = unpack_rows(jnp.sum(pieces[...], axis=0), few)
    mine = [maps[0], maps[1]]
    for c in range(out.shape[1] // LANES):
        out[:, pl.ds(c * LANES, LANES)] = place(values, mine, c)


def call(kernel, shapes, flops, *args, **params):
    moved = sum(a.size * a.dtype.itemsize for a in (*args, *jax.tree.leaves(shapes)))
    return pl.pallas_call(
        kernel,
        out_shape=shapes,
        compiler_params=pltpu.CompilerParams(vmem_limit_bytes=LIMIT),
        cost_estimate=pl.CostEstimate(flops=flops, bytes_accessed=moved, transcendentals=0),
        **params,
    )(*args)


def array(shape, dtype):
    return jax.ShapeDtypeStruct(shape, dtype)


def turned(place, sizes):
    out, step = 0, 1
    for size in reversed(sizes):
        out = out + (place // step % size + size // 2) % size * step
        step = step * size
    return out


def sizes_of(axes):
    return [lax.axis_size(a) for a in axes]


def swap_from_far(pieces, axes, sizes):
    order = [[turned(i, sizes) for i in range(pieces.shape[0])]]
    return lax.all_to_all(pieces, axes, 0, 0, axis_index_groups=order)


def summed_over_wide(partial):
    ring, core = WIDE
    rows = partial.shape[0] // 2
    both = lax.all_gather(partial, core)
    half = lax.dynamic_slice_in_dim(both, lax.axis_index(core) * rows, rows, 1)
    half = (half[0] + half[1]).astype(BF16)
    size = lax.axis_size(ring)
    order = [[(i + 3 * size // 8) % size for i in range(size)]]
    pieces = lax.all_to_all(
        jnp.broadcast_to(half[None], (size, *half.shape)), ring, 0, 0, axis_index_groups=order
    )
    return lax.all_gather(jnp.sum(pieces.astype(F32), axis=0), core, tiled=True)


def specs(*spaces):
    return [pl.BlockSpec(memory_space=m) for m in spaces]


def encode(few, ids, activations, enc_weight, dec_bias):
    group = lax.axis_index(NARROW)
    tokens, channels = activations.shape
    width = enc_weight.shape[1]
    depth = tokens // CHUNK * (1 if few else 8)
    return call(
        functools.partial(encode_kernel, few),
        (
            array((depth, LANES), F32),
            array((FEW if few else ids.shape[0], tokens), jnp.int32),
            array((tokens, LANES), jnp.int32),
            array((8, tokens), jnp.int32),
            array((tokens // lax.axis_size(NARROW), channels), F32),
        ),
        2 * tokens * channels * width,
        group[None],
        turned(group, sizes_of(NARROW))[None],
        ids,
        activations,
        enc_weight,
        dec_bias[None],
        in_specs=specs(pltpu.SMEM, pltpu.SMEM, pltpu.VMEM, pl.ANY, pl.ANY, pltpu.VMEM),
        scratch_shapes=[
            pltpu.VMEM(activations.shape, BF16),
            pltpu.VMEM(enc_weight.shape, BF16),
            pltpu.VMEM((tokens, LANES), F32),
            pltpu.SemaphoreType.DMA((9,)),
        ],
    )


def find(named, base, dec_weight, ids=None):
    tokens = named.shape[1]
    width, channels = dec_weight.shape
    shapes = (
        array((2, tokens, LANES), jnp.int32),
        array((2, CHUNK, LANES), jnp.int32),
        array((channels, width), BF16),
    )
    args, outs, kernel = [lax.axis_index(WIDE)[None], named, base, dec_weight], [pltpu.VMEM] * 3, maps_kernel
    if ids is not None:
        args.append(ids)
        shapes += (array((1,), jnp.int32),)
        outs.append(pltpu.SMEM)
        kernel = functools.partial(window_kernel, width)
    ins = [pltpu.SMEM] + [pltpu.VMEM] * (len(args) - 1)
    return call(kernel, shapes, 1 << 26, *args, in_specs=specs(*ins), out_specs=specs(*outs))


def decode(few, preact, maps, target, enc_bias, dec_weight):
    width, channels = dec_weight.shape
    tokens = maps.shape[1]
    latents, rec = call(
        functools.partial(decode_kernel, few),
        (array((tokens, width), BF16), array((tokens, channels), BF16)),
        2 * tokens * channels * width,
        preact,
        maps,
        enc_bias[None],
        dec_weight,
        in_specs=specs(pltpu.VMEM, pltpu.VMEM, pltpu.VMEM, pl.ANY),
        scratch_shapes=[pltpu.VMEM(dec_weight.shape, BF16), pltpu.SemaphoreType.DMA((4,))],
    )
    sizes = sizes_of(NARROW)
    recs = swap_from_far(rec.reshape(-1, *target.shape), NARROW, sizes)
    mixed = call(
        functools.partial(mix_kernel, sizes),
        array(recs.shape, BF16),
        8 * recs.size,
        recs,
        target,
    )
    return latents, swap_from_far(mixed, NARROW, sizes).reshape(tokens, channels)


def latent_parts(few, back, turned_weight, slots):
    return call(
        functools.partial(grad_kernel, few),
        array((lax.axis_size(WIDE), 1 if few else 8, LANES), F32),
        2 * back.size * turned_weight.shape[1],
        back,
        turned_weight,
        slots,
    )


def outer(latents, back):
    shape = (latents.shape[1], back.shape[1])
    return call(
        outer_kernel,
        array(shape, BF16),
        2 * latents.size * back.shape[1],
        latents,
        back,
        out_specs=specs(pl.ANY)[0],
        scratch_shapes=[pltpu.VMEM(shape, BF16), pltpu.SemaphoreType.DMA((4,))],
    )


def own_gradient(few, parts, own, width):
    return call(functools.partial(own_kernel, few), array((CHUNK, width), F32), 1 << 20, parts, own)


def local(activations, enc_weight, enc_bias, dec_weight, dec_bias, active_ids):
    width = enc_weight.shape[1]
    ids = active_ids.T
    partial, named, slots, base, target = encode(True, ids, activations, enc_weight, dec_bias)
    preact = summed_over_wide(partial)
    maps, own, turned_weight, needed = find(named, base, dec_weight, ids)
    wide = [lax.axis_size(WIDE)]
    latents, back = decode(True, preact, maps, target, enc_bias, dec_weight)
    parts = swap_from_far(latent_parts(True, back, turned_weight, slots), WIDE, wide)
    dec_grad = outer(latents, back)

    def few():
        return dec_grad, own_gradient(True, parts, own, width)

    def many():
        no_bias = jnp.zeros_like(dec_bias)
        partial, named, slots, base, _ = encode(False, ids, activations, enc_weight, no_bias)
        preact = summed_over_wide(partial)
        maps, own, turned_weight = find(named, base, dec_weight)
        latents, back = decode(False, preact, maps, target, enc_bias, dec_weight)
        parts = swap_from_far(latent_parts(False, back, turned_weight, slots), WIDE, wide)
        return outer(latents, back), own_gradient(False, parts, own, width)

    return lax.cond(needed[0] <= LANES, few, many)


def solution(mesh):
    split = Mesh(mesh.devices.reshape(16, 2, 4, 4), ("wide_0", "wide_1", "narrow_0", "narrow_1"))
    return jax.shard_map(
        local,
        mesh=split,
        in_specs=(P(None, WIDE), P(WIDE, NARROW), P(NARROW), P(NARROW, WIDE), P(WIDE), P()),
        out_specs=(P(NARROW, WIDE), P(WIDE, NARROW)),
        check_vma=False,
    )
```

```python
import functools

import jax
import jax.numpy as jnp
from jax import lax
from jax.experimental import pallas as pl
from jax.experimental.pallas import tpu as pltpu
from jax.sharding import Mesh
from jax.sharding import PartitionSpec as P

NARROW = ("narrow_0", "narrow_1")
WIDE = ("wide_0", "wide_1")
LANES = 128
F32 = jnp.float32
BF16 = jnp.bfloat16
LIMIT = 16 * 1024 * 1024

CHUNK = 16
FEW = 16


def lookup(rows, lanes):
    return jnp.take_along_axis(rows, lanes, axis=1, mode="promise_in_bounds")


def pick_more(picked, rows, first, slots):
    low, high = slots & (LANES - 1), slots >> 7
    for c in range(rows.shape[1] // LANES):
        found = lookup(rows[:, c * LANES : (c + 1) * LANES], low)
        picked = jnp.where(high == first // LANES + c, found, picked)
    return picked


def pack(picked, few):
    picked = picked.reshape(-1, 2, 8, LANES)
    picked = picked[:, 0] + picked[:, 1]
    return jnp.sum(picked, axis=1, keepdims=True) if few else picked


def pick_slots(rows, slots, few):
    return pack(pick_more(jnp.zeros(slots.shape, F32), rows, 0, slots), few)


def unpack_rows(packed, few):
    if few:
        return jnp.broadcast_to(packed, (CHUNK, LANES))
    return jnp.concatenate([packed, packed], axis=0)


def place(values, maps, c, shift=None):
    lanes = (maps[c // 4] >> (8 * (c % 4))) & 255
    placed = lookup(values, (lanes - 1) & (LANES - 1))
    if shift is not None:
        placed = placed + shift
    return jnp.where(lanes > 0, placed, 0.0)


def up_to(counts):
    at = lax.broadcasted_iota(jnp.int32, counts.shape, 1) & (CHUNK - 1)
    for s in (1, 2, 4, 8):
        counts = counts + jnp.where(at >= s, pltpu.roll(counts, s, axis=1), 0)
    return counts


def fill_slots(few, group, width, ids, named, slots, base):
    count, tokens = ids.shape
    lane = lax.broadcasted_iota(jnp.int32, (1, LANES), 1)
    line = lax.broadcasted_iota(jnp.int32, (LANES, LANES), 0)
    within = ids[...] - group * width
    mine = (within >= 0) & (within < width)
    if few:
        entry = lax.broadcasted_iota(jnp.int32, (FEW, tokens), 0)
        earlier = lax.broadcasted_iota(jnp.int32, (count, count), 0) > lax.broadcasted_iota(jnp.int32, (count, count), 1)
        ones = jnp.where(mine, 1.0, 0.0)
        rank = jnp.dot(
            jnp.where(earlier, 1.0, 0.0).astype(BF16), ones.astype(BF16), preferred_element_type=F32
        )
        taken = (rank[count - 1 :] + ones[count - 1 :]).astype(jnp.int32)
        place_of = jnp.where(mine, rank.astype(jnp.int32), FEW)
        held = jnp.full((FEW, tokens), -1, jnp.int32)
        for k in range(count):
            held = jnp.where(entry == place_of[k : k + 1], within[k : k + 1], held)
    else:
        held = jnp.where(mine, within, -1)
    named[...] = held
    for i in range(tokens // LANES):
        cols = pl.ds(i * LANES, LANES)
        block = held[:, i * LANES : (i + 1) * LANES]
        if few:
            counts = jnp.broadcast_to(taken[:, i * LANES : (i + 1) * LANES], (8, LANES))
            first = up_to(counts) - counts
            spread = jnp.full((LANES, LANES), -1, jnp.int32)
            for k in range(FEW):
                at = jnp.where(block[k : k + 1] >= 0, first[:1] + k, -1)
                spread = jnp.where(line == at, block[k : k + 1], spread)
        else:
            first = jnp.broadcast_to(64 * ((lane >> 3) & 1), (8, LANES))
            spread = jnp.concatenate([block, block], axis=0)
            spread = jnp.where(line >> 6 == (lane >> 3) & 1, spread, -1)
        base[:, cols] = first
        slots[cols, :] = spread.T


def count_needed(width, ids, most):
    every = lax.broadcasted_iota(jnp.int32, (16, LANES), 0)
    needed = jnp.zeros((16, LANES), jnp.int32)
    for i in range(ids.shape[1] // LANES):
        owner = ids[:, pl.ds(i * LANES, LANES)] >> (width.bit_length() - 1)
        tally = jnp.zeros((16, LANES), jnp.int32)
        for k in range(ids.shape[0]):
            tally = tally + jnp.where(every == owner[k : k + 1], 1, 0)
        needed = jnp.maximum(needed, jnp.maximum(tally * (LANES // FEW), up_to(tally)))
    most[0] = jnp.max(needed)


def maps_kernel(owner, named, base, weight, out, own, turned_weight, same_weight):
    count, tokens = named.shape
    line = lax.broadcasted_iota(jnp.int32, (LANES, LANES), 0)
    for i in range(tokens // LANES):
        cols = pl.ds(i * LANES, LANES)
        start = base[:, cols] + lax.broadcasted_iota(jnp.int32, (8, LANES), 0) + 1

        def body(n, maps):
            first = pl.multiple_of(8 * n, 8)
            eight = named[pl.ds(first, 8), cols]
            block = eight >> 7
            code = (start + first) << (8 * (block & 3))
            low = eight & (LANES - 1)
            codes = [
                jnp.where((block >= 0) & (block < 4), code, 0),
                jnp.where((block >= 4) & (block < 8), code, 0),
            ]
            for k in range(8):
                hit = line == low[k : k + 1]
                maps = [m | jnp.where(hit, f[k : k + 1], 0) for m, f in zip(maps, codes)]
            return tuple(maps)

        zero = jnp.zeros((LANES, LANES), jnp.int32)
        maps = lax.fori_loop(0, count // 8, body, (zero, zero))
        for m in range(2):
            out[m, cols, :] = maps[m].T
    same_weight[...] = weight[...]
    own[...] = out[:, pl.ds(pl.multiple_of(owner[0] * CHUNK, CHUNK), CHUNK), :]
    for r in range(0, weight.shape[0], 256):
        turned_weight[:, pl.ds(r, 256)] = weight[pl.ds(r, 256), :].T


def window_kernel(width, owner, named, base, weight, ids, out, own, turned_weight, same_weight, most):
    maps_kernel(owner, named, base, weight, out, own, turned_weight, same_weight)
    count_needed(width, ids, most)


def encode_kernel(
    few,
    group,
    place_of,
    ids,
    act,
    weight,
    bias,
    packed,
    named,
    slots,
    base,
    target,
    act_here,
    weight_here,
    picked,
    arrived,
):
    depth, width = weight.shape
    half, block = width // 2, depth // 4
    pairs = [(act, act_here)]
    for n in range(8):
        at = (pl.ds(n % 4 * block, block), pl.ds(n // 4 * half, half))
        pairs.append((weight.at[at], weight_here.at[at]))
    copies = [pltpu.make_async_copy(*pair, arrived.at[n]) for n, pair in enumerate(pairs)]
    for copy in copies:
        copy.start()
    fill_slots(few, group[0], width, ids, named, slots, base)
    copies[0].wait()
    step = 8 * CHUNK
    for n in range(2):
        for copy in copies[4 * n + 1 : 4 * n + 5]:
            copy.wait()
        for i in range(act.shape[0] // step):
            rows = pl.ds(i * step, step)
            part = jnp.dot(
                act_here[rows, :], weight_here[:, pl.ds(n * half, half)], preferred_element_type=F32
            )
            sofar = picked[rows, :] if n else jnp.zeros((step, LANES), F32)
            sofar = pick_more(sofar, part, n * half, slots[rows, :])
            if n:
                done = pack(sofar, few)
                lines = 8 * done.shape[1]
                packed[pl.ds(i * lines, lines), :] = done.reshape(lines, LANES)
            else:
                picked[rows, :] = sofar
    mixed = target.shape[0]
    first = pl.multiple_of(place_of[0] * mixed, mixed)
    target[...] = bias[...] - act_here[pl.ds(first, mixed), :].astype(F32)


def decode_kernel(few, packed, maps, bias, weight, latents, rec):
    step = 8 * CHUNK
    depth = 1 if few else 8
    steps = latents.shape[0] // step
    def fill(i):
        rows = pl.ds(i * step, step)
        chunks = [unpack_rows(packed[pl.ds((8 * i + q) * depth, depth), :], few) for q in range(8)]
        values = jnp.concatenate(chunks, axis=0)
        mine = [maps[0, rows, :], maps[1, rows, :]]
        blocks = [
            place(values, mine, c, bias[:, pl.ds(c * LANES, LANES)]) for c in range(latents.shape[1] // LANES)
        ]
        latents[rows, :] = jnp.concatenate(blocks, axis=1).astype(BF16)

    for i in range(steps):
        rows = pl.ds(i * step, step)
        fill(i)
        rec[rows, :] = jnp.dot(latents[rows, :], weight[...], preferred_element_type=F32).astype(rec.dtype)


def mix_kernel(sizes, recs, target, out):
    groups = recs.shape[0]
    at_group = [turned(g, sizes) for g in range(groups)]
    for r in range(0, recs.shape[1], 16):
        for c in range(0, recs.shape[2], LANES):
            at = (pl.ds(r, 16), pl.ds(c, LANES))
            err = target[at]
            errs = []
            for g in range(groups):
                err = err + recs[(at_group[g], *at)].astype(F32)
                errs.append(err)
            suffix = jnp.zeros_like(err)
            for g in reversed(range(groups)):
                suffix = suffix + errs[g]
                out[(at_group[g], *at)] = (suffix * (1.0 / groups)).astype(out.dtype)


def grad_kernel(few, back, turned_weight, slots, out):
    step = 8 * CHUNK
    for i in range(back.shape[0] // step):
        rows = pl.ds(i * step, step)
        part = jnp.dot(back[rows, :], turned_weight[...], preferred_element_type=F32)
        first = (8 * i + out.shape[0] // 2) % out.shape[0]
        out[pl.ds(first, 8)] = pick_slots(part, slots[rows, :], few)


def outer_kernel(latents, back, out, here, sent):
    step = 256
    copies = []
    for i in range(out.shape[0] // step):
        rows = pl.ds(i * step, step)
        part = lax.dot_general(
            latents[:, i * step : (i + 1) * step],
            back[...],
            (((0,), (0,)), ((), ())),
            preferred_element_type=F32,
        )
        here[rows, :] = part.astype(out.dtype)
        copies.append(pltpu.make_async_copy(here.at[rows], out.at[rows], sent.at[i]))
        copies[-1].start()
    for copy in copies:
        copy.wait()


def own_kernel(few, pieces, maps, out):
    values = unpack_rows(jnp.sum(pieces[...], axis=0), few)
    mine = [maps[0], maps[1]]
    for c in range(out.shape[1] // LANES):
        out[:, pl.ds(c * LANES, LANES)] = place(values, mine, c)


def call(kernel, shapes, flops, *args, **params):
    moved = sum(a.size * a.dtype.itemsize for a in (*args, *jax.tree.leaves(shapes)))
    return pl.pallas_call(
        kernel,
        out_shape=shapes,
        compiler_params=pltpu.CompilerParams(vmem_limit_bytes=LIMIT),
        cost_estimate=pl.CostEstimate(flops=flops, bytes_accessed=moved, transcendentals=0),
        **params,
    )(*args)


def array(shape, dtype):
    return jax.ShapeDtypeStruct(shape, dtype)


def turned(place, sizes):
    out, step = 0, 1
    for size in reversed(sizes):
        out = out + (place // step % size + size // 2) % size * step
        step = step * size
    return out


def sizes_of(axes):
    return [lax.axis_size(a) for a in axes]


def swap_from_far(pieces, axes, sizes):
    order = [[turned(i, sizes) for i in range(pieces.shape[0])]]
    return lax.all_to_all(pieces, axes, 0, 0, axis_index_groups=order)


def summed_over_wide(partial):
    ring, core = WIDE
    rows = partial.shape[0] // 2
    both = lax.all_gather(partial, core)
    half = lax.dynamic_slice_in_dim(both, lax.axis_index(core) * rows, rows, 1)
    half = (half[0] + half[1]).astype(BF16)
    size = lax.axis_size(ring)
    pieces = swap_from_far(jnp.broadcast_to(half[None], (size, *half.shape)), ring, [size])
    return lax.all_gather(jnp.sum(pieces.astype(F32), axis=0), core, tiled=True)


def specs(*spaces):
    return [pl.BlockSpec(memory_space=m) for m in spaces]


def encode(few, ids, activations, enc_weight, dec_bias):
    group = lax.axis_index(NARROW)
    tokens, channels = activations.shape
    width = enc_weight.shape[1]
    depth = tokens // CHUNK * (1 if few else 8)
    return call(
        functools.partial(encode_kernel, few),
        (
            array((depth, LANES), F32),
            array((FEW if few else ids.shape[0], tokens), jnp.int32),
            array((tokens, LANES), jnp.int32),
            array((8, tokens), jnp.int32),
            array((tokens // lax.axis_size(NARROW), channels), F32),
        ),
        2 * tokens * channels * width,
        group[None],
        turned(group, sizes_of(NARROW))[None],
        ids,
        activations,
        enc_weight,
        dec_bias[None],
        in_specs=specs(pltpu.SMEM, pltpu.SMEM, pltpu.VMEM, pl.ANY, pl.ANY, pltpu.VMEM),
        scratch_shapes=[
            pltpu.VMEM(activations.shape, BF16),
            pltpu.VMEM(enc_weight.shape, BF16),
            pltpu.VMEM((tokens, LANES), F32),
            pltpu.SemaphoreType.DMA((9,)),
        ],
    )


def find(named, base, dec_weight, ids=None):
    tokens = named.shape[1]
    width, channels = dec_weight.shape
    shapes = (
        array((2, tokens, LANES), jnp.int32),
        array((2, CHUNK, LANES), jnp.int32),
        array((channels, width), BF16),
        array((width, channels), BF16),
    )
    args, outs, kernel = [lax.axis_index(WIDE)[None], named, base, dec_weight], [pltpu.VMEM] * 4, maps_kernel
    if ids is not None:
        args.append(ids)
        shapes += (array((1,), jnp.int32),)
        outs.append(pltpu.SMEM)
        kernel = functools.partial(window_kernel, width)
    ins = [pltpu.SMEM] + [pltpu.VMEM] * (len(args) - 1)
    return call(kernel, shapes, 1 << 26, *args, in_specs=specs(*ins), out_specs=specs(*outs))


def decode(few, preact, maps, target, enc_bias, dec_weight):
    width, channels = dec_weight.shape
    tokens = maps.shape[1]
    latents, rec = call(
        functools.partial(decode_kernel, few),
        (array((tokens, width), BF16), array((tokens, channels), BF16)),
        2 * tokens * channels * width,
        preact,
        maps,
        enc_bias[None],
        dec_weight,
    )
    sizes = sizes_of(NARROW)
    recs = swap_from_far(rec.reshape(-1, *target.shape), NARROW, sizes)
    mixed = call(
        functools.partial(mix_kernel, sizes),
        array(recs.shape, BF16),
        8 * recs.size,
        recs,
        target,
    )
    return latents, swap_from_far(mixed, NARROW, sizes).reshape(tokens, channels)


def latent_parts(few, back, turned_weight, slots):
    return call(
        functools.partial(grad_kernel, few),
        array((lax.axis_size(WIDE), 1 if few else 8, LANES), F32),
        2 * back.size * turned_weight.shape[1],
        back,
        turned_weight,
        slots,
    )


def outer(latents, back):
    shape = (latents.shape[1], back.shape[1])
    return call(
        outer_kernel,
        array(shape, BF16),
        2 * latents.size * back.shape[1],
        latents,
        back,
        out_specs=specs(pl.ANY)[0],
        scratch_shapes=[pltpu.VMEM(shape, BF16), pltpu.SemaphoreType.DMA((4,))],
    )


def own_gradient(few, parts, own, width):
    return call(functools.partial(own_kernel, few), array((CHUNK, width), F32), 1 << 20, parts, own)


def local(activations, enc_weight, enc_bias, dec_weight, dec_bias, active_ids):
    width = enc_weight.shape[1]
    ids = active_ids.T
    partial, named, slots, base, target = encode(True, ids, activations, enc_weight, dec_bias)
    preact = summed_over_wide(partial)
    maps, own, turned_weight, same_weight, needed = find(named, base, dec_weight, ids)
    wide = [lax.axis_size(WIDE)]
    latents, back = decode(True, preact, maps, target, enc_bias, same_weight)
    parts = swap_from_far(latent_parts(True, back, turned_weight, slots), WIDE, wide)
    dec_grad = outer(latents, back)

    def few():
        return dec_grad, own_gradient(True, parts, own, width)

    def many():
        no_bias = jnp.zeros_like(dec_bias)
        partial, named, slots, base, _ = encode(False, ids, activations, enc_weight, no_bias)
        preact = summed_over_wide(partial)
        maps, own, turned_weight, same_weight = find(named, base, dec_weight)
        latents, back = decode(False, preact, maps, target, enc_bias, same_weight)
        parts = swap_from_far(latent_parts(False, back, turned_weight, slots), WIDE, wide)
        return outer(latents, back), own_gradient(False, parts, own, width)

    return lax.cond(needed[0] <= LANES, few, many)


def solution(mesh):
    split = Mesh(mesh.devices.reshape(16, 2, 4, 4), ("wide_0", "wide_1", "narrow_0", "narrow_1"))
    return jax.shard_map(
        local,
        mesh=split,
        in_specs=(P(None, WIDE), P(WIDE, NARROW), P(NARROW), P(NARROW, WIDE), P(WIDE), P()),
        out_specs=(P(NARROW, WIDE), P(WIDE, NARROW)),
        check_vma=False,
    )
```
